32 devices in a mesh: tm: 4 (over z), chan: 8 (over y, x, core).
Axes of the slice: x: 2, y: 2, z: 4, core: 2. Of those that a mesh axis runs over, the one named last changes fastest.
Arguments:
- signal: float32 [256, 8192], P('chan', 'tm'), may hold values from -6 to 6
- band: float32 [2, 16, 256], replicated, may hold values from -4 to 4
- response: float32 [2, 4, 16, 2048], P(None, 'tm', None, 'chan'), may hold values from -6 to 6
- offsets: int32 [4, 2048], P('tm', 'chan'), may hold values from 0 to 255, as said below
Outputs:
- smoothed: float32 [256, 8192], P('chan', 'tm')
The draws below stay inside these ranges and needn't reach their ends.
Inputs may be any that keep to these rules, and one draw needn't show every extreme that they name: Row c of bin k's gain holds the columns c + offsets + j, wrapping around the 256 channels; every offset lies within 8 of 0 modulo 256, and entry [p, q] is the same for all p and for all q in one run of 64 consecutive q.
All inputs are finite; a program needn't handle non-finite values.
Results may differ from the reference program's by a relative error of at most 0.0003.
Values sent between devices are 32-bit elements; how exact they have to be, the bound alone decides.
A program may use at most 64 MiB of HBM per device.

```python
import jax
import jax.numpy as jnp
from jax import lax

CHANNELS = 256
BAND = 16
T_DEV = 2048
PHASES = 4
SECTIONS = 2
SAMPLES = 8192


def draw_offsets(key, part):
    run_count = 32
    drift = jax.random.randint(key, (run_count,), -(BAND // 2), BAND // 2 + 1)
    run_ids = jnp.arange(run_count, dtype=jnp.int32)
    drift = jnp.where(run_ids == 0, BAND // 2, drift)
    drift = jnp.where(run_ids == 1, -(BAND // 2), drift)
    drift = jnp.where(run_ids == 2, -1, drift)
    drift = jnp.where(run_ids == 3, 0, drift)
    value = drift % CHANNELS
    row_vals = jnp.repeat(value, T_DEV // run_count)
    return jnp.broadcast_to(row_vals[None, :], (PHASES, T_DEV)).astype(jnp.int32)


def block_levels(key, dims, cuts, least, largest):
    def one(axis_at, shards_of):
        heights = jax.random.uniform(jax.random.fold_in(jax.random.fold_in(key, 6), axis_at), (shards_of,), jnp.float32, least / len(cuts), largest / len(cuts))
        return jnp.repeat(jnp.exp(heights), dims[axis_at] // shards_of).reshape((-1,) + (1,) * (len(dims) - axis_at - 1))

    factor_of = one(*cuts[0])
    for cut in cuts[1:]:
        factor_of = factor_of * one(*cut)
    return factor_of


def bell_draw(stream_key, extent, width, limit, split=(), held_as=jnp.bfloat16):
    gain = block_levels(stream_key, extent, split, -0.22, 0.18) if split else 1.0
    values = jax.random.normal(stream_key, extent, jnp.float32) * width * gain
    return jnp.minimum(jnp.maximum(values, -limit), limit).astype(held_as)


def setup_inputs(seed: int = 0) -> dict:
    splits = jax.random.split(jax.random.key(seed), 5)
    return {
        "signal": bell_draw(splits[0], (CHANNELS, SAMPLES), 1.0, 6.0, ((0, 8), (1, 4)), jnp.float32),
        "band": bell_draw(splits[1], (2, BAND, CHANNELS), 0.3, 4.0, (), jnp.float32),
        "response": bell_draw(splits[2], (2, PHASES, BAND, T_DEV), 0.7, 6.0, ((1, 4), (3, 8)), jnp.float32),
        "offsets": draw_offsets(jax.random.fold_in(splits[4], 71), 0),
    }


def reverse_index(value, bit_count):
    result = 0
    for bit_index in range(bit_count):
        result = result + ((value >> bit_index) & 1) * (1 << (bit_count - 1 - bit_index))
    return result


def reference(signal, band, response, offsets):
    total_len = SAMPLES
    reorder = jnp.array([reverse_index(p, SECTIONS) for p in range(PHASES)], dtype=jnp.int32)
    resp_nat = response[:, reorder]
    resp_nat = jnp.transpose(resp_nat, (0, 2, 3, 1)).reshape(2, BAND, total_len)
    offset_nat = jnp.transpose(offsets[reorder], (1, 0)).reshape(total_len)
    spectrum = jnp.fft.fft(signal, axis=1)
    coefficient = band[0] + 1j * band[1]
    block_count = PHASES
    spec_blocks = jnp.transpose(spectrum.reshape(CHANNELS, block_count, T_DEV), (1, 0, 2))
    resp_blocks = jnp.transpose((resp_nat[0] + 1j * resp_nat[1]).reshape(BAND, block_count, T_DEV), (1, 0, 2))
    offset_blocks = offset_nat.reshape(block_count, T_DEV)

    def mix_block(packed):
        spec_part, resp_part, offset_row = packed
        gather_idx = (jnp.arange(CHANNELS, dtype=jnp.int32)[:, None] + offset_row[None, :]) % CHANNELS
        moved = jnp.take_along_axis(spec_part, gather_idx, axis=0)
        extended = jnp.concatenate([moved, moved[:BAND - 1]], axis=0)
        accumulated = jnp.zeros_like(spec_part)
        for lag_step in range(BAND):
            accumulated = accumulated + coefficient[lag_step][:, None] * resp_part[lag_step][None, :] * extended[lag_step:lag_step + CHANNELS]
        return accumulated

    mixed = lax.map(mix_block, (spec_blocks, resp_blocks, offset_blocks))
    mixed = jnp.transpose(mixed, (1, 0, 2)).reshape(CHANNELS, total_len)
    return jnp.real(jnp.fft.ifft(mixed, axis=1)).astype(jnp.float32)
```

```python
import math

import jax
import jax.numpy as jnp
import numpy as np
from jax import lax
from jax.experimental import pallas as pl
from jax.experimental.pallas import tpu as pltpu
from jax.sharding import PartitionSpec as P

PRECISE = lax.Precision.HIGHEST


def from_partner(block, axis, stride):
    count = lax.axis_size(axis)
    route = []
    for low in range(count):
        high = low | 1 << stride
        if high != low and high < count:
            route += [(low, high), (high, low)]
    return lax.ppermute(block, axis, route)


def twiddle(numer, length):
    angle = -2.0 * math.pi / length * numer.astype(jnp.float32)
    return (jnp.cos(angle), jnp.sin(angle))


def dft_table(length):
    steps = lax.iota(jnp.int32, length)
    return twiddle(steps[:, None] * steps[None, :] % length, length)


def reverse_bits(value, bit_count):
    result = value * 0
    for bit_index in range(bit_count):
        result = result + value // (1 << bit_index) % 2 * (1 << bit_count - 1 - bit_index)
    return result


def complex_einsum(form, left_real, left_imag, right_real, right_imag):
    out_real = jnp.einsum(form, left_real, right_real, precision=PRECISE) - jnp.einsum(
        form, left_imag, right_imag, precision=PRECISE
    )
    out_imag = jnp.einsum(form, left_real, right_imag, precision=PRECISE) + jnp.einsum(
        form, left_imag, right_real, precision=PRECISE
    )
    return (out_real, out_imag)


def forward_local(real_part, imag_part, phase_bin, total_len, inner_len):
    channel_count, length = real_part.shape
    outer_len = length // inner_len
    sample_pos = lax.iota(jnp.int32, length)
    cosine, sine_part = twiddle(sample_pos * phase_bin % total_len, total_len)
    real_part, imag_part = (
        real_part * cosine - imag_part * sine_part,
        real_part * sine_part + imag_part * cosine,
    )
    real_part = real_part.reshape(channel_count, inner_len, outer_len)
    imag_part = imag_part.reshape(channel_count, inner_len, outer_len)
    table_real, table_imag = dft_table(inner_len)
    real_part, imag_part = complex_einsum(
        "cab,ak->cbk", real_part, imag_part, table_real, table_imag
    )
    outer_ids = lax.iota(jnp.int32, outer_len)[:, None]
    inner_ids = lax.iota(jnp.int32, inner_len)[None, :]
    cosine, sine_part = twiddle(outer_ids * inner_ids, length)
    real_part, imag_part = (
        real_part * cosine - imag_part * sine_part,
        real_part * sine_part + imag_part * cosine,
    )
    table_real, table_imag = dft_table(outer_len)
    return complex_einsum("cbk,bm->mck", real_part, imag_part, table_real, table_imag)


def inverse_local(spec_real, spec_imag, phase_bin, total_len):
    outer_len, channel_count, inner_len = spec_real.shape
    length = outer_len * inner_len
    table_real, table_imag = dft_table(outer_len)
    real_part, imag_part = complex_einsum(
        "mck,mb->cbk", spec_real, spec_imag, table_real, -table_imag
    )
    outer_ids = lax.iota(jnp.int32, outer_len)[:, None]
    inner_ids = lax.iota(jnp.int32, inner_len)[None, :]
    cosine, sine_part = twiddle(outer_ids * inner_ids, length)
    sine_part = -sine_part
    real_part, imag_part = (
        real_part * cosine - imag_part * sine_part,
        real_part * sine_part + imag_part * cosine,
    )
    table_real, table_imag = dft_table(inner_len)
    real_part, imag_part = complex_einsum(
        "cbk,ka->cab", real_part, imag_part, table_real, -table_imag
    )
    real_part = real_part.reshape(channel_count, length)
    imag_part = imag_part.reshape(channel_count, length)
    sample_pos = lax.iota(jnp.int32, length)
    cosine, sine_part = twiddle(sample_pos * phase_bin % total_len, total_len)
    sine_part = -sine_part
    return (real_part * cosine - imag_part * sine_part, real_part * sine_part + imag_part * cosine)


def mix_bins(spread, band, response, offsets):
    fine_len, channel_all, inner_len = (spread.shape[1], spread.shape[2], spread.shape[3])
    band_width = band.shape[1]
    half_width = band_width // 2
    shift_cols = offsets.reshape(1, fine_len, 1, inner_len)
    centered = (shift_cols + half_width) % channel_all - half_width
    moved = jnp.zeros_like(spread)
    for shift_amount in range(-half_width, half_width + 1):
        rolled = jnp.roll(spread, -shift_amount, axis=2)
        moved = jnp.where(centered == shift_amount, rolled, moved)
    moved_real = moved[0]
    moved_imag = moved[1]
    wide_real = jnp.concatenate([moved_real, moved_real[:, : band_width - 1]], axis=1)
    wide_imag = jnp.concatenate([moved_imag, moved_imag[:, : band_width - 1]], axis=1)
    responses = response.reshape(2, band_width, fine_len, 1, inner_len)
    acc_real = jnp.zeros_like(moved_real)
    acc_imag = jnp.zeros_like(moved_imag)
    for lag_index in range(band_width):
        value_real = wide_real[:, lag_index : lag_index + channel_all]
        value_imag = wide_imag[:, lag_index : lag_index + channel_all]
        gain_real = band[0, lag_index][None, :, None]
        gain_imag = band[1, lag_index][None, :, None]
        coef_real = gain_real * responses[0, lag_index] - gain_imag * responses[1, lag_index]
        coef_imag = gain_real * responses[1, lag_index] + gain_imag * responses[0, lag_index]
        acc_real = acc_real + coef_real * value_real - coef_imag * value_imag
        acc_imag = acc_imag + coef_real * value_imag + coef_imag * value_real
    return (acc_real, acc_imag)


def per_device(signal, band, response, offsets):
    blocks = lax.axis_size("tm")
    levels = blocks.bit_length() - 1
    device_pos = lax.axis_index("tm")
    phase_bin = reverse_bits(device_pos, levels)
    channel_count, length = signal.shape
    total_len = length * blocks
    inner_len = math.gcd(128, length // lax.axis_size("chan"))
    real_part = signal
    imag_part = jnp.zeros_like(signal)
    for bit_index in range(levels - 1, -1, -1):
        half_span = 1 << bit_index
        partner = from_partner(jnp.stack([real_part, imag_part]), "tm", bit_index)
        upper_half = device_pos // half_span % 2 == 1
        cosine, sine_part = twiddle(device_pos % half_span, 2 * half_span)
        diff_real = partner[0] - real_part
        diff_imag = partner[1] - imag_part
        new_real = jnp.where(
            upper_half, diff_real * cosine - diff_imag * sine_part, real_part + partner[0]
        )
        new_imag = jnp.where(
            upper_half, diff_real * sine_part + diff_imag * cosine, imag_part + partner[1]
        )
        real_part, imag_part = (new_real, new_imag)
    spec_real, spec_imag = forward_local(real_part, imag_part, phase_bin, total_len, inner_len)
    spread = lax.all_to_all(
        jnp.stack([spec_real, spec_imag]), "chan", split_axis=1, concat_axis=2, tiled=True
    )
    mixed_real, mixed_imag = mix_bins(spread, band, response, offsets)
    returned = lax.all_to_all(
        jnp.stack([mixed_real, mixed_imag]), "chan", split_axis=2, concat_axis=1, tiled=True
    )
    real_part, imag_part = inverse_local(returned[0], returned[1], phase_bin, total_len)
    for bit_index in range(levels):
        half_span = 1 << bit_index
        partner = from_partner(jnp.stack([real_part, imag_part]), "tm", bit_index)
        upper_half = device_pos // half_span % 2 == 1
        cosine, sine_part = twiddle(device_pos % half_span, 2 * half_span)
        sine_part = -sine_part
        base_real = jnp.where(upper_half, partner[0], real_part)
        base_imag = jnp.where(upper_half, partner[1], imag_part)
        scaled_real = jnp.where(upper_half, real_part, partner[0])
        scaled_imag = jnp.where(upper_half, imag_part, partner[1])
        prod_real = scaled_real * cosine - scaled_imag * sine_part
        prod_imag = scaled_real * sine_part + scaled_imag * cosine
        real_part = jnp.where(upper_half, base_real - prod_real, base_real + prod_real)
        imag_part = jnp.where(upper_half, base_imag - prod_imag, base_imag + prod_imag)
    smoothed = real_part / total_len
    return smoothed


TM, CHAN, ROWS, LANES, OUTER, BANDW, HALF = 4, 8, 8, 128, 64, 16, 8
DEVICES = TM * CHAN
TOTAL = OUTER * LANES


def split_hi_lo(value):
    hi = value.astype(jnp.bfloat16)
    return hi, (value - hi.astype(jnp.float32)).astype(jnp.bfloat16)


def dot3(left, right, dims):
    (lh, ll), (rh, rl) = left, right

    def one(a, b):
        return lax.dot_general(a, b, (dims, ((), ())), preferred_element_type=jnp.float32)

    return one(lh, rh) + (one(lh, rl) + one(ll, rh))


def outer_table():
    n1 = np.arange(OUTER)
    table = np.zeros((OUTER, OUTER))
    for pair in range(DEVICES):
        angle = 2 * np.pi * (n1 * pair % OUTER) / OUTER
        table[2 * pair] = np.cos(angle)
        table[2 * pair + 1] = -np.sin(angle) if pair else (-1.0) ** n1
    return table


def rev(t):
    return (t % 2) * 2 + t // 2


def fused(signal, resp, band, base, turn, table, out,
          xin, ybuf, sbuf, rbuf, rt, xp, mv, mm, wh, wl, dbuf, yback, zbuf, rsend, rrecv, send, recv):
    t, g = lax.axis_index("tm"), lax.axis_index("chan")
    d = CHAN // 2 * g + rev(t)
    e = TM * g + t

    def remote(src, dst, k, target):
        return pltpu.make_async_remote_copy(
            src_ref=src, dst_ref=dst, send_sem=send.at[k], recv_sem=recv.at[k],
            device_id=target, device_id_type=pl.DeviceIdType.MESH)

    def local(src, dst, sem):
        return pltpu.make_async_copy(src, dst, sem)

    for hop in range(1, TM):
        to = (t + hop) % TM
        remote(signal.at[pl.ds(ROWS * to, ROWS)], xin.at[:, pl.ds(16 * t, 16)], 0, (to, g)).start()
    local(signal.at[pl.ds(ROWS * t, ROWS)], xin.at[:, pl.ds(16 * t, 16)], recv.at[0]).start()

    def send_resp(part, s, block, target):
        return pltpu.make_async_remote_copy(
            src_ref=resp.at[s], dst_ref=rbuf.at[part, pl.ds(16 * block, 16)], send_sem=rsend.at[part],
            recv_sem=rrecv.at[part], device_id=target, device_id_type=pl.DeviceIdType.MESH)

    t_b = jnp.where(t < 2, t, 5 - t)
    s_own = jnp.where(t == 0, (8 - g) % 8, 7 - g) + 8
    local(resp.at[g], rbuf.at[0, pl.ds(16 * g, 16)], rrecv.at[0]).start()
    for hop in range(1, CHAN):
        to = (g + hop) % CHAN
        send_resp(0, to, g, (t, to)).start()
        send_resp(1, jnp.where(t == 0, (8 - to) % 8, 7 - to) + 8, g, (t_b, to)).start()

    @pl.when(t < 2)
    def _():
        local(resp.at[s_own], rbuf.at[1, pl.ds(16 * g, 16)], rrecv.at[1]).start()

    @pl.when(t >= 2)
    def _():
        pltpu.make_async_remote_copy(
            src_ref=resp.at[s_own], dst_ref=rbuf.at[1, pl.ds(16 * g, 16)], send_sem=rsend.at[2],
            recv_sem=rrecv.at[1], device_id=(5 - t, g), device_id_type=pl.DeviceIdType.MESH).start()

    first = d == 0
    for part in range(2):
        tc, ts = turn[:, 2 * part : 2 * part + 1], turn[:, 2 * part + 1 : 2 * part + 2]
        bc, bs = base[0], base[1]
        tr = tc * bc - ts * bs
        ti = tc * bs + ts * bc
        zero = jnp.zeros_like(tr)
        if part == 0:
            blocks = ((tr, ti), (jnp.where(first, zero, -ti), jnp.where(first, zero, tr)))
        else:
            blocks = ((jnp.where(first, zero, tr), jnp.where(first, zero, ti)),
                      (jnp.where(first, tr, ti), jnp.where(first, ti, -tr)))
        for row in range(2):
            for col in range(2):
                hi, lo = split_hi_lo(blocks[row][col])
                where = (slice(LANES * row, LANES * (row + 1)),
                         slice(LANES * (2 * part + col), LANES * (2 * part + col + 1)))
                wh[where] = hi
                wl[where] = lo

    local(xin, xin, recv.at[0]).wait()
    ycols = ybuf.reshape(DEVICES * 2 * ROWS, LANES)
    for c in range(ROWS):
        ycols[pl.ds(c, OUTER, stride=ROWS), :] = dot3((table[0], table[1]), split_hi_lo(xin[c]), ((1,), (0,)))

    def send_pair(hop, carry):
        to = (d + hop) % DEVICES
        remote(ybuf.at[to], sbuf.at[e], 1, (rev(to % 4), to // 4)).start()
        return carry

    lax.fori_loop(1, DEVICES, send_pair, 0)
    local(ybuf.at[d], sbuf.at[e], recv.at[1]).start()

    for part in range(2):
        local(rbuf.at[part], rbuf.at[part], rrecv.at[part]).wait()
        rt[part] = rbuf[part].T

    local(sbuf, sbuf, recv.at[1]).wait()
    rows = jnp.concatenate([sbuf[:, 0].reshape(256, LANES), sbuf[:, 1].reshape(256, LANES)], axis=1)
    spec = dot3(split_hi_lo(rows), (wh[...], wl[...]), ((1,), (0,)))
    for part in range(2):
        for ri in range(2):
            at = LANES * (2 * part + ri)
            piece = spec[:, at : at + LANES]
            xp[part, ri, 8:264] = piece
            xp[part, ri, 0:8] = piece[248:256]
            xp[part, ri, 264:288] = piece[0:24]

    def shift(i, carry):
        at = 8 * i
        for part in range(2):
            off = jnp.broadcast_to(rt[part, 32:33, :], (8, LANES))
            got = [jnp.zeros((8, LANES), jnp.float32)] * 2
            for o in range(-HALF, HALF + 1):
                hit = off == float(o)
                for ri in range(2):
                    got[ri] = jnp.where(hit, xp[part, ri, pl.ds(at + 8 + o, 8), :], got[ri])
            for ri in range(2):
                mv[part, ri, pl.ds(pl.multiple_of(at, 8), 8), :] = got[ri]
        return carry

    lax.fori_loop(0, 34, shift, 0)

    def chunk(step, carry):
        top = 64 * ((step + g // 2) % 4)

        def mix(i, inner):
            at = pl.multiple_of(top + 8 * i, 8)
            gains = band[pl.ds(at, 8), :]
            acc = [jnp.zeros((8, LANES), jnp.float32)] * 4
            for j in range(BANDW):
                br = jnp.broadcast_to(gains[:, j : j + 1], (8, LANES))
                bi = jnp.broadcast_to(gains[:, BANDW + j : BANDW + j + 1], (8, LANES))
                for part in range(2):
                    rr, ri = rt[part, j : j + 1, :], rt[part, BANDW + j : BANDW + j + 1, :]
                    cr = br * rr - bi * ri
                    ci = br * ri + bi * rr
                    xr = mv[part, 0, pl.ds(at + j, 8), :]
                    xi = mv[part, 1, pl.ds(at + j, 8), :]
                    acc[2 * part] = acc[2 * part] + (cr * xr - ci * xi)
                    acc[2 * part + 1] = acc[2 * part + 1] + (cr * xi + ci * xr)
            for q in range(4):
                mm[pl.ds(pl.multiple_of(8 * i, 8), 8), LANES * q : LANES * (q + 1)] = acc[q]
            return inner

        lax.fori_loop(0, 8, mix, 0)
        back = dot3(split_hi_lo(mm[...]), (wh[...], wl[...]), ((1,), (1,)))
        e0 = top // 8
        for ri in range(2):
            dbuf[pl.ds(e0, 8), ri] = back[:, LANES * ri : LANES * (ri + 1)].reshape(8, 8, LANES)

        def send_back(u, inner):
            to = e0 + u

            @pl.when(to != e)
            def _():
                remote(dbuf.at[to], yback.at[d], 2, (to % TM, to // TM)).start()

            @pl.when(to == e)
            def _():
                local(dbuf.at[to], yback.at[d], recv.at[2]).start()

            return inner

        lax.fori_loop(0, 8, send_back, 0)
        return carry

    lax.fori_loop(0, 4, chunk, 0)

    local(yback, yback, recv.at[2]).wait()
    bcols = yback.reshape(DEVICES * 2 * ROWS, LANES)
    for c in range(ROWS):
        zbuf[c] = dot3((table[2], table[3]), split_hi_lo(bcols[pl.ds(c, OUTER, stride=ROWS), :]), ((1,), (0,)))
    for hop in range(1, TM):
        to = (t + hop) % TM
        remote(zbuf.at[:, pl.ds(16 * to, 16)], out.at[pl.ds(ROWS * t, ROWS)], 3, (to, g)).start()
    local(zbuf.at[:, pl.ds(16 * t, 16)], out.at[pl.ds(ROWS * t, ROWS)], recv.at[3]).start()
    local(out, out, recv.at[3]).wait()

    for k in (0, 3):
        local(signal.at[pl.ds(0, 24)], signal.at[pl.ds(0, 24)], send.at[k]).wait()
    for k in (1, 2):
        local(ybuf.at[pl.ds(0, 31)], ybuf.at[pl.ds(0, 31)], send.at[k]).wait()
    for part in range(2):
        local(resp.at[pl.ds(0, 7)], resp.at[pl.ds(0, 7)], rsend.at[part]).wait()

    @pl.when(t >= 2)
    def _():
        local(resp.at[0], resp.at[0], rsend.at[2]).wait()


def per_device_fused(signal, band, response, offsets):
    t, g = lax.axis_index("tm"), lax.axis_index("chan")
    d = CHAN // 2 * g + rev(t)
    resp = response.reshape(2 * BANDW, 16, 16).transpose(2, 1, 0)
    centered = ((offsets + HALF) % 256 - HALF).astype(jnp.float32).reshape(1, 16, 16).transpose(2, 1, 0)
    resp = jnp.pad(jnp.concatenate([resp, centered], axis=2), ((0, 0), (0, 0), (0, LANES - 2 * BANDW - 1)))
    gains = band.reshape(2 * BANDW, 256).T

    n2 = np.arange(LANES)
    angle = -2 * np.pi * (n2[:, None] * n2[None, :] % LANES) / LANES
    base = jnp.asarray(np.stack([np.cos(angle), np.sin(angle)]).astype(np.float32))
    pairs = np.arange(DEVICES)[:, None]
    other = np.where(pairs == 0, DEVICES, OUTER - pairs)
    turns = [-2 * np.pi * (n2[None, :] * k1 % TOTAL) / TOTAL for k1 in (pairs, other)]
    turn = np.stack([np.cos(turns[0]), np.sin(turns[0]), np.cos(turns[1]), np.sin(turns[1])], axis=-1)
    turn = lax.dynamic_index_in_dim(jnp.asarray(turn.astype(np.float32)), d, 0, keepdims=False)
    forward = outer_table()
    tables = []
    for matrix in (forward, forward.T / TOTAL):
        matrix = matrix.astype(np.float32)
        hi = matrix.astype(jnp.bfloat16)
        tables += [hi, (matrix - hi.astype(np.float32)).astype(jnp.bfloat16)]
    table = jnp.asarray(np.stack(tables))

    f32 = jnp.float32
    vmem = pl.BlockSpec(memory_space=pltpu.VMEM)
    out = pl.pallas_call(
        fused,
        out_shape=jax.ShapeDtypeStruct((32, 16, LANES), f32),
        in_specs=[vmem] * 6,
        out_specs=vmem,
        scratch_shapes=[
            pltpu.VMEM((ROWS, OUTER, LANES), f32),
            pltpu.VMEM((DEVICES, 2, ROWS, LANES), f32),
            pltpu.VMEM((DEVICES, 2, ROWS, LANES), f32),
            pltpu.VMEM((2, LANES, LANES), f32),
            pltpu.VMEM((2, LANES, LANES), f32),
            pltpu.VMEM((2, 2, 288, LANES), f32),
            pltpu.VMEM((2, 2, 272, LANES), f32),
            pltpu.VMEM((64, 4 * LANES), f32),
            pltpu.VMEM((2 * LANES, 4 * LANES), jnp.bfloat16),
            pltpu.VMEM((2 * LANES, 4 * LANES), jnp.bfloat16),
            pltpu.VMEM((DEVICES, 2, ROWS, LANES), f32),
            pltpu.VMEM((DEVICES, 2, ROWS, LANES), f32),
            pltpu.VMEM((ROWS, OUTER, LANES), f32),
            pltpu.SemaphoreType.DMA((3,)),
            pltpu.SemaphoreType.DMA((2,)),
            pltpu.SemaphoreType.DMA((4,)),
            pltpu.SemaphoreType.DMA((4,)),
        ],
        compiler_params=pltpu.CompilerParams(has_side_effects=True, vmem_limit_bytes=32 << 20),
    )(signal.reshape(32, 16, LANES), resp, gains, base, turn, table)
    return out.reshape(32, 16 * LANES)


def solution(mesh):
    sizes = dict(mesh.shape)
    tuned = sizes["tm"] == TM and sizes["chan"] == CHAN
    in_specs = (P("chan", "tm"), P(), P(None, "tm", None, "chan"), P("tm", "chan"))
    out_specs = P("chan", "tm")
    return jax.shard_map(
        per_device_fused if tuned else per_device, mesh=mesh, in_specs=in_specs, out_specs=out_specs, check_vma=False
    )
```

```python
import math

import jax
import jax.numpy as jnp
import numpy as np
from jax import lax
from jax.experimental import pallas as pl
from jax.experimental.pallas import tpu as pltpu
from jax.sharding import PartitionSpec as P

PRECISE = lax.Precision.HIGHEST


def from_partner(block, axis, stride):
    count = lax.axis_size(axis)
    route = []
    for low in range(count):
        high = low | 1 << stride
        if high != low and high < count:
            route += [(low, high), (high, low)]
    return lax.ppermute(block, axis, route)


def twiddle(numer, length):
    angle = -2.0 * math.pi / length * numer.astype(jnp.float32)
    return (jnp.cos(angle), jnp.sin(angle))


def dft_table(length):
    steps = lax.iota(jnp.int32, length)
    return twiddle(steps[:, None] * steps[None, :] % length, length)


def reverse_bits(value, bit_count):
    result = value * 0
    for bit_index in range(bit_count):
        result = result + value // (1 << bit_index) % 2 * (1 << bit_count - 1 - bit_index)
    return result


def complex_einsum(form, left_real, left_imag, right_real, right_imag):
    out_real = jnp.einsum(form, left_real, right_real, precision=PRECISE) - jnp.einsum(
        form, left_imag, right_imag, precision=PRECISE
    )
    out_imag = jnp.einsum(form, left_real, right_imag, precision=PRECISE) + jnp.einsum(
        form, left_imag, right_real, precision=PRECISE
    )
    return (out_real, out_imag)


def forward_local(real_part, imag_part, phase_bin, total_len, inner_len):
    channel_count, length = real_part.shape
    outer_len = length // inner_len
    sample_pos = lax.iota(jnp.int32, length)
    cosine, sine_part = twiddle(sample_pos * phase_bin % total_len, total_len)
    real_part, imag_part = (
        real_part * cosine - imag_part * sine_part,
        real_part * sine_part + imag_part * cosine,
    )
    real_part = real_part.reshape(channel_count, inner_len, outer_len)
    imag_part = imag_part.reshape(channel_count, inner_len, outer_len)
    table_real, table_imag = dft_table(inner_len)
    real_part, imag_part = complex_einsum(
        "cab,ak->cbk", real_part, imag_part, table_real, table_imag
    )
    outer_ids = lax.iota(jnp.int32, outer_len)[:, None]
    inner_ids = lax.iota(jnp.int32, inner_len)[None, :]
    cosine, sine_part = twiddle(outer_ids * inner_ids, length)
    real_part, imag_part = (
        real_part * cosine - imag_part * sine_part,
        real_part * sine_part + imag_part * cosine,
    )
    table_real, table_imag = dft_table(outer_len)
    return complex_einsum("cbk,bm->mck", real_part, imag_part, table_real, table_imag)


def inverse_local(spec_real, spec_imag, phase_bin, total_len):
    outer_len, channel_count, inner_len = spec_real.shape
    length = outer_len * inner_len
    table_real, table_imag = dft_table(outer_len)
    real_part, imag_part = complex_einsum(
        "mck,mb->cbk", spec_real, spec_imag, table_real, -table_imag
    )
    outer_ids = lax.iota(jnp.int32, outer_len)[:, None]
    inner_ids = lax.iota(jnp.int32, inner_len)[None, :]
    cosine, sine_part = twiddle(outer_ids * inner_ids, length)
    sine_part = -sine_part
    real_part, imag_part = (
        real_part * cosine - imag_part * sine_part,
        real_part * sine_part + imag_part * cosine,
    )
    table_real, table_imag = dft_table(inner_len)
    real_part, imag_part = complex_einsum(
        "cbk,ka->cab", real_part, imag_part, table_real, -table_imag
    )
    real_part = real_part.reshape(channel_count, length)
    imag_part = imag_part.reshape(channel_count, length)
    sample_pos = lax.iota(jnp.int32, length)
    cosine, sine_part = twiddle(sample_pos * phase_bin % total_len, total_len)
    sine_part = -sine_part
    return (real_part * cosine - imag_part * sine_part, real_part * sine_part + imag_part * cosine)


def mix_bins(spread, band, response, offsets):
    fine_len, channel_all, inner_len = (spread.shape[1], spread.shape[2], spread.shape[3])
    band_width = band.shape[1]
    half_width = band_width // 2
    shift_cols = offsets.reshape(1, fine_len, 1, inner_len)
    centered = (shift_cols + half_width) % channel_all - half_width
    moved = jnp.zeros_like(spread)
    for shift_amount in range(-half_width, half_width + 1):
        rolled = jnp.roll(spread, -shift_amount, axis=2)
        moved = jnp.where(centered == shift_amount, rolled, moved)
    moved_real = moved[0]
    moved_imag = moved[1]
    wide_real = jnp.concatenate([moved_real, moved_real[:, : band_width - 1]], axis=1)
    wide_imag = jnp.concatenate([moved_imag, moved_imag[:, : band_width - 1]], axis=1)
    responses = response.reshape(2, band_width, fine_len, 1, inner_len)
    acc_real = jnp.zeros_like(moved_real)
    acc_imag = jnp.zeros_like(moved_imag)
    for lag_index in range(band_width):
        value_real = wide_real[:, lag_index : lag_index + channel_all]
        value_imag = wide_imag[:, lag_index : lag_index + channel_all]
        gain_real = band[0, lag_index][None, :, None]
        gain_imag = band[1, lag_index][None, :, None]
        coef_real = gain_real * responses[0, lag_index] - gain_imag * responses[1, lag_index]
        coef_imag = gain_real * responses[1, lag_index] + gain_imag * responses[0, lag_index]
        acc_real = acc_real + coef_real * value_real - coef_imag * value_imag
        acc_imag = acc_imag + coef_real * value_imag + coef_imag * value_real
    return (acc_real, acc_imag)


def per_device(signal, band, response, offsets):
    blocks = lax.axis_size("tm")
    levels = blocks.bit_length() - 1
    device_pos = lax.axis_index("tm")
    phase_bin = reverse_bits(device_pos, levels)
    channel_count, length = signal.shape
    total_len = length * blocks
    inner_len = math.gcd(128, length // lax.axis_size("chan"))
    real_part = signal
    imag_part = jnp.zeros_like(signal)
    for bit_index in range(levels - 1, -1, -1):
        half_span = 1 << bit_index
        partner = from_partner(jnp.stack([real_part, imag_part]), "tm", bit_index)
        upper_half = device_pos // half_span % 2 == 1
        cosine, sine_part = twiddle(device_pos % half_span, 2 * half_span)
        diff_real = partner[0] - real_part
        diff_imag = partner[1] - imag_part
        new_real = jnp.where(
            upper_half, diff_real * cosine - diff_imag * sine_part, real_part + partner[0]
        )
        new_imag = jnp.where(
            upper_half, diff_real * sine_part + diff_imag * cosine, imag_part + partner[1]
        )
        real_part, imag_part = (new_real, new_imag)
    spec_real, spec_imag = forward_local(real_part, imag_part, phase_bin, total_len, inner_len)
    spread = lax.all_to_all(
        jnp.stack([spec_real, spec_imag]), "chan", split_axis=1, concat_axis=2, tiled=True
    )
    mixed_real, mixed_imag = mix_bins(spread, band, response, offsets)
    returned = lax.all_to_all(
        jnp.stack([mixed_real, mixed_imag]), "chan", split_axis=2, concat_axis=1, tiled=True
    )
    real_part, imag_part = inverse_local(returned[0], returned[1], phase_bin, total_len)
    for bit_index in range(levels):
        half_span = 1 << bit_index
        partner = from_partner(jnp.stack([real_part, imag_part]), "tm", bit_index)
        upper_half = device_pos // half_span % 2 == 1
        cosine, sine_part = twiddle(device_pos % half_span, 2 * half_span)
        sine_part = -sine_part
        base_real = jnp.where(upper_half, partner[0], real_part)
        base_imag = jnp.where(upper_half, partner[1], imag_part)
        scaled_real = jnp.where(upper_half, real_part, partner[0])
        scaled_imag = jnp.where(upper_half, imag_part, partner[1])
        prod_real = scaled_real * cosine - scaled_imag * sine_part
        prod_imag = scaled_real * sine_part + scaled_imag * cosine
        real_part = jnp.where(upper_half, base_real - prod_real, base_real + prod_real)
        imag_part = jnp.where(upper_half, base_imag - prod_imag, base_imag + prod_imag)
    smoothed = real_part / total_len
    return smoothed


TM, CHAN, ROWS, LANES, OUTER, BANDW, HALF = 4, 8, 8, 128, 64, 16, 8
DEVICES = TM * CHAN
TOTAL = OUTER * LANES


def split_hi_lo(value):
    hi = value.astype(jnp.bfloat16)
    return hi, (value - hi.astype(jnp.float32)).astype(jnp.bfloat16)


def dot3(left, right, dims):
    (lh, ll), (rh, rl) = left, right

    def one(a, b):
        return lax.dot_general(a, b, (dims, ((), ())), preferred_element_type=jnp.float32)

    return one(lh, rh) + (one(lh, rl) + one(ll, rh))


def outer_table():
    n1 = np.arange(OUTER)
    table = np.zeros((OUTER, OUTER))
    for pair in range(DEVICES):
        angle = 2 * np.pi * (n1 * pair % OUTER) / OUTER
        table[2 * pair] = np.cos(angle)
        table[2 * pair + 1] = -np.sin(angle) if pair else (-1.0) ** n1
    return table


def rev(t):
    return (t % 2) * 2 + t // 2


def outer_product(table, value):
    hi, lo = split_hi_lo(value)
    return jnp.dot(table.astype(jnp.bfloat16), jnp.concatenate([hi, lo, hi], axis=0), preferred_element_type=jnp.float32)


def fused(signal, response, offsets, band_in, base_in, turn_in, table_in, out,
          base, turn, table, resp, tall, band, xs, xin, ybuf, sbuf, rbuf, rt, xp, mv, mm, wh, wl, vh, vl,
          dbuf, yback, zbuf, rsend, rrecv, send, recv, own):
    t, g = lax.axis_index("tm"), lax.axis_index("chan")
    d = CHAN // 2 * g + rev(t)
    e = TM * g + t

    def remote(src, dst, k, target):
        return pltpu.make_async_remote_copy(
            src_ref=src, dst_ref=dst, send_sem=send.at[k], recv_sem=recv.at[k],
            device_id=target, device_id_type=pl.DeviceIdType.MESH)

    def local(src, dst, sem):
        return pltpu.make_async_copy(src, dst, sem)

    for hop in (2, 1, 3):
        to = (t + hop) % TM
        remote(signal.at[pl.ds(ROWS * to, ROWS)], xin.at[t], 0, (to, g)).start()
    local(signal.at[pl.ds(ROWS * t, ROWS)], xin.at[t], recv.at[0]).start()
    constants = [local(base_in, base, own.at[0]), local(turn_in.at[d], turn, own.at[1]),
                 local(table_in, table, own.at[2])]
    for copy in constants:
        copy.start()

    centered = ((offsets[...] + HALF) % 256 - HALF).astype(jnp.float32)
    filler = jnp.zeros((LANES - 2 * BANDW - 8, 256), jnp.float32)
    tall[...] = jnp.concatenate([response[...], jnp.broadcast_to(centered, (8, 256)), filler], axis=0).T
    for s in range(16):
        resp[s] = tall[pl.ds(s, 16, stride=16), :]

    def send_resp(part, s, block, target):
        return pltpu.make_async_remote_copy(
            src_ref=resp.at[s], dst_ref=rbuf.at[part, pl.ds(16 * block, 16)], send_sem=rsend.at[part],
            recv_sem=rrecv.at[part], device_id=target, device_id_type=pl.DeviceIdType.MESH)

    t_b = jnp.where(t < 2, t, 5 - t)
    s_own = jnp.where(t == 0, (8 - g) % 8, 7 - g) + 8
    local(resp.at[g], rbuf.at[0, pl.ds(16 * g, 16)], rrecv.at[0]).start()
    for hop in range(1, CHAN):
        to = (g + hop) % CHAN
        send_resp(0, to, g, (t, to)).start()
        send_resp(1, jnp.where(t == 0, (8 - to) % 8, 7 - to) + 8, g, (t_b, to)).start()

    @pl.when(t < 2)
    def _():
        local(resp.at[s_own], rbuf.at[1, pl.ds(16 * g, 16)], rrecv.at[1]).start()

    @pl.when(t >= 2)
    def _():
        pltpu.make_async_remote_copy(
            src_ref=resp.at[s_own], dst_ref=rbuf.at[1, pl.ds(16 * g, 16)], send_sem=rsend.at[2],
            recv_sem=rrecv.at[1], device_id=(5 - t, g), device_id_type=pl.DeviceIdType.MESH).start()

    band[...] = jnp.concatenate([band_in[...], jnp.zeros((LANES - 2 * BANDW, 256), jnp.float32)], axis=0).T

    for copy in constants:
        copy.wait()
    first = d == 0
    for part in range(2):
        tc, ts = turn[2 * part : 2 * part + 1, :], turn[2 * part + 1 : 2 * part + 2, :]
        bc, bs = base[0], base[1]
        tr = tc * bc - ts * bs
        ti = tc * bs + ts * bc
        zero = jnp.zeros_like(tr)
        if part == 0:
            blocks = ((tr, ti), (jnp.where(first, zero, -ti), jnp.where(first, zero, tr)))
        else:
            blocks = ((jnp.where(first, zero, tr), jnp.where(first, zero, ti)),
                      (jnp.where(first, tr, ti), jnp.where(first, ti, -tr)))
        for row in range(2):
            for col in range(2):
                inner = slice(LANES * row, LANES * (row + 1))
                outer = slice(LANES * (2 * part + col), LANES * (2 * part + col + 1))
                vh[outer, inner], vl[outer, inner] = split_hi_lo(blocks[row][col])
                wh[inner, outer], wl[inner, outer] = split_hi_lo(blocks[row][col].T)

    local(xin, xin, recv.at[0]).wait()
    for b in range(TM):
        for i in range(16):
            xs[pl.ds(ROWS * (16 * b + i), ROWS), :] = xin[b, :, LANES * i : LANES * (i + 1)]
    ycols = ybuf.reshape(DEVICES * 2 * ROWS, LANES)
    taken = jnp.concatenate([xs[pl.ds(c, OUTER, stride=ROWS), :] for c in range(ROWS)], axis=1)
    result = outer_product(table[0], taken)
    for c in range(ROWS):
        ycols[pl.ds(c, OUTER, stride=ROWS), :] = result[:, LANES * c : LANES * (c + 1)]

    def send_pair(hop, carry):
        to = (d + hop) % DEVICES
        remote(ybuf.at[to], sbuf.at[e], 1, (rev(to % 4), to // 4)).start()
        return carry

    lax.fori_loop(1, DEVICES, send_pair, 0)
    local(ybuf.at[d], sbuf.at[e], recv.at[1]).start()

    for part in range(2):
        local(rbuf.at[part], rbuf.at[part], rrecv.at[part]).wait()
        rt[part] = rbuf[part].T

    local(sbuf, sbuf, recv.at[1]).wait()
    rows = jnp.concatenate([sbuf[:, 0].reshape(256, LANES), sbuf[:, 1].reshape(256, LANES)], axis=1)
    spec = dot3(split_hi_lo(rows), (wh[...], wl[...]), ((1,), (0,)))
    for part in range(2):
        for ri in range(2):
            at = LANES * (2 * part + ri)
            piece = spec[:, at : at + LANES]
            xp[part, ri, 8:264] = piece
            xp[part, ri, 0:8] = piece[248:256]
            xp[part, ri, 264:288] = piece[0:24]

    def shift(i, carry):
        at = 8 * i
        for part in range(2):
            off = jnp.broadcast_to(rt[part, 32:33, :], (8, LANES))
            got = [jnp.zeros((8, LANES), jnp.float32)] * 2
            for o in range(-HALF, HALF + 1):
                hit = off == float(o)
                for ri in range(2):
                    got[ri] = jnp.where(hit, xp[part, ri, pl.ds(at + 8 + o, 8), :], got[ri])
            for ri in range(2):
                mv[part, ri, pl.ds(pl.multiple_of(at, 8), 8), :] = got[ri]
        return carry

    lax.fori_loop(0, 34, shift, 0, unroll=2)

    def chunk(step, carry):
        top = 64 * ((step + g // 2) % 4)

        def mix(i, inner):
            at = pl.multiple_of(top + 8 * i, 8)
            gains = band[pl.ds(at, 8), :]
            acc = [jnp.zeros((8, LANES), jnp.float32)] * 4
            for j in range(BANDW):
                br = jnp.broadcast_to(gains[:, j : j + 1], (8, LANES))
                bi = jnp.broadcast_to(gains[:, BANDW + j : BANDW + j + 1], (8, LANES))
                for part in range(2):
                    rr, ri = rt[part, j : j + 1, :], rt[part, BANDW + j : BANDW + j + 1, :]
                    cr = br * rr - bi * ri
                    ci = br * ri + bi * rr
                    xr = mv[part, 0, pl.ds(at + j, 8), :]
                    xi = mv[part, 1, pl.ds(at + j, 8), :]
                    acc[2 * part] = acc[2 * part] + (cr * xr - ci * xi)
                    acc[2 * part + 1] = acc[2 * part + 1] + (cr * xi + ci * xr)
            for q in range(4):
                mm[pl.ds(pl.multiple_of(8 * i, 8), 8), LANES * q : LANES * (q + 1)] = acc[q]
            return inner

        lax.fori_loop(0, 8, mix, 0)
        back = dot3(split_hi_lo(mm[...]), (vh[...], vl[...]), ((1,), (0,)))
        e0 = top // 8
        for ri in range(2):
            dbuf[pl.ds(e0, 8), ri] = back[:, LANES * ri : LANES * (ri + 1)].reshape(8, 8, LANES)

        def send_back(u, inner):
            to = e0 + u

            @pl.when(to != e)
            def _():
                remote(dbuf.at[to], yback.at[d], 2, (to % TM, to // TM)).start()

            @pl.when(to == e)
            def _():
                local(dbuf.at[to], yback.at[d], recv.at[2]).start()

            return inner

        lax.fori_loop(0, 8, send_back, 0)
        return carry

    lax.fori_loop(0, 4, chunk, 0)

    local(yback, yback, recv.at[2]).wait()
    bcols = yback.reshape(DEVICES * 2 * ROWS, LANES)
    taken = jnp.concatenate([bcols[pl.ds(c, OUTER, stride=ROWS), :] for c in range(ROWS)], axis=1)
    result = outer_product(table[1], taken)
    for c in range(ROWS):
        xs[pl.ds(c, OUTER, stride=ROWS), :] = result[:, LANES * c : LANES * (c + 1)]
    for b in range(TM):
        for i in range(16):
            zbuf[b, :, LANES * i : LANES * (i + 1)] = xs[pl.ds(ROWS * (16 * b + i), ROWS), :]
    for hop in (2, 1, 3):
        to = (t + hop) % TM
        remote(zbuf.at[to], out.at[pl.ds(ROWS * t, ROWS)], 3, (to, g)).start()
    local(zbuf.at[t], out.at[pl.ds(ROWS * t, ROWS)], recv.at[3]).start()
    local(out, out, recv.at[3]).wait()

    for k in (0, 3):
        local(signal.at[pl.ds(0, 24)], signal.at[pl.ds(0, 24)], send.at[k]).wait()
    for k in (1, 2):
        local(ybuf.at[pl.ds(0, 31)], ybuf.at[pl.ds(0, 31)], send.at[k]).wait()
    for part in range(2):
        local(resp.at[pl.ds(0, 7)], resp.at[pl.ds(0, 7)], rsend.at[part]).wait()

    @pl.when(t >= 2)
    def _():
        local(resp.at[0], resp.at[0], rsend.at[2]).wait()


def per_device_fused(signal, band, response, offsets):
    n2 = np.arange(LANES)
    angle = -2 * np.pi * (n2[:, None] * n2[None, :] % LANES) / LANES
    base = jnp.asarray(np.stack([np.cos(angle), np.sin(angle)]).astype(np.float32))
    pairs = np.arange(DEVICES)[:, None]
    other = np.where(pairs == 0, DEVICES, OUTER - pairs)
    turns = [-2 * np.pi * (n2[None, :] * k1 % TOTAL) / TOTAL for k1 in (pairs, other)]
    rows = [np.cos(turns[0]), np.sin(turns[0]), np.cos(turns[1]), np.sin(turns[1])]
    turn = jnp.asarray(np.stack(rows * 2, axis=1).astype(np.float32))
    forward = outer_table()
    tables = []
    for matrix in (forward, forward.T / TOTAL):
        matrix = matrix.astype(np.float32)
        hi = matrix.astype(jnp.bfloat16)
        lo = (matrix - hi.astype(np.float32)).astype(jnp.bfloat16)
        tables.append(np.concatenate([hi, hi, lo], axis=1).astype(np.float32))
    table = jnp.asarray(np.stack(tables))

    f32 = jnp.float32
    hbm = pl.BlockSpec(memory_space=pl.ANY)
    vmem = pl.BlockSpec(memory_space=pltpu.VMEM)
    out = pl.pallas_call(
        fused,
        out_shape=jax.ShapeDtypeStruct((32, 16 * LANES), f32),
        in_specs=[hbm, vmem, vmem, vmem, hbm, hbm, hbm],
        out_specs=hbm,
        scratch_shapes=[
            pltpu.VMEM((2, LANES, LANES), f32),
            pltpu.VMEM((8, LANES), f32),
            pltpu.VMEM((2, OUTER, 3 * OUTER), f32),
            pltpu.VMEM((16, 16, LANES), f32),
            pltpu.VMEM((2 * LANES, LANES), f32),
            pltpu.VMEM((2 * LANES, LANES), f32),
            pltpu.VMEM((OUTER * ROWS, LANES), f32),
            pltpu.VMEM((TM, ROWS, 16 * LANES), f32),
            pltpu.VMEM((DEVICES, 2, ROWS, LANES), f32),
            pltpu.VMEM((DEVICES, 2, ROWS, LANES), f32),
            pltpu.VMEM((2, LANES, LANES), f32),
            pltpu.VMEM((2, LANES, LANES), f32),
            pltpu.VMEM((2, 2, 288, LANES), f32),
            pltpu.VMEM((2, 2, 272, LANES), f32),
            pltpu.VMEM((64, 4 * LANES), f32),
            pltpu.VMEM((2 * LANES, 4 * LANES), jnp.bfloat16),
            pltpu.VMEM((2 * LANES, 4 * LANES), jnp.bfloat16),
            pltpu.VMEM((4 * LANES, 2 * LANES), jnp.bfloat16),
            pltpu.VMEM((4 * LANES, 2 * LANES), jnp.bfloat16),
            pltpu.VMEM((DEVICES, 2, ROWS, LANES), f32),
            pltpu.VMEM((DEVICES, 2, ROWS, LANES), f32),
            pltpu.VMEM((TM, ROWS, 16 * LANES), f32),
            pltpu.SemaphoreType.DMA((3,)),
            pltpu.SemaphoreType.DMA((2,)),
            pltpu.SemaphoreType.DMA((4,)),
            pltpu.SemaphoreType.DMA((4,)),
            pltpu.SemaphoreType.DMA((3,)),
        ],
        compiler_params=pltpu.CompilerParams(has_side_effects=True, vmem_limit_bytes=32 << 20),
    )(signal, response.reshape(2 * BANDW, 256), offsets, band.reshape(2 * BANDW, 256), base, turn, table)
    return out


def solution(mesh):
    sizes = dict(mesh.shape)
    tuned = sizes["tm"] == TM and sizes["chan"] == CHAN
    in_specs = (P("chan", "tm"), P(), P(None, "tm", None, "chan"), P("tm", "chan"))
    out_specs = P("chan", "tm")
    return jax.shard_map(
        per_device_fused if tuned else per_device, mesh=mesh, in_specs=in_specs, out_specs=out_specs, check_vma=False
    )
```

```python
import math

import jax
import jax.numpy as jnp
import numpy as np
from jax import lax
from jax.experimental import pallas as pl
from jax.experimental.pallas import tpu as pltpu
from jax.sharding import PartitionSpec as P

PRECISE = lax.Precision.HIGHEST


def from_partner(block, axis, stride):
    count = lax.axis_size(axis)
    route = []
    for low in range(count):
        high = low | 1 << stride
        if high != low and high < count:
            route += [(low, high), (high, low)]
    return lax.ppermute(block, axis, route)


def twiddle(numer, length):
    angle = -2.0 * math.pi / length * numer.astype(jnp.float32)
    return (jnp.cos(angle), jnp.sin(angle))


def dft_table(length):
    steps = lax.iota(jnp.int32, length)
    return twiddle(steps[:, None] * steps[None, :] % length, length)


def reverse_bits(value, bit_count):
    result = value * 0
    for bit_index in range(bit_count):
        result = result + value // (1 << bit_index) % 2 * (1 << bit_count - 1 - bit_index)
    return result


def complex_einsum(form, left_real, left_imag, right_real, right_imag):
    out_real = jnp.einsum(form, left_real, right_real, precision=PRECISE) - jnp.einsum(
        form, left_imag, right_imag, precision=PRECISE
    )
    out_imag = jnp.einsum(form, left_real, right_imag, precision=PRECISE) + jnp.einsum(
        form, left_imag, right_real, precision=PRECISE
    )
    return (out_real, out_imag)


def forward_local(real_part, imag_part, phase_bin, total_len, inner_len):
    channel_count, length = real_part.shape
    outer_len = length // inner_len
    sample_pos = lax.iota(jnp.int32, length)
    cosine, sine_part = twiddle(sample_pos * phase_bin % total_len, total_len)
    real_part, imag_part = (
        real_part * cosine - imag_part * sine_part,
        real_part * sine_part + imag_part * cosine,
    )
    real_part = real_part.reshape(channel_count, inner_len, outer_len)
    imag_part = imag_part.reshape(channel_count, inner_len, outer_len)
    table_real, table_imag = dft_table(inner_len)
    real_part, imag_part = complex_einsum(
        "cab,ak->cbk", real_part, imag_part, table_real, table_imag
    )
    outer_ids = lax.iota(jnp.int32, outer_len)[:, None]
    inner_ids = lax.iota(jnp.int32, inner_len)[None, :]
    cosine, sine_part = twiddle(outer_ids * inner_ids, length)
    real_part, imag_part = (
        real_part * cosine - imag_part * sine_part,
        real_part * sine_part + imag_part * cosine,
    )
    table_real, table_imag = dft_table(outer_len)
    return complex_einsum("cbk,bm->mck", real_part, imag_part, table_real, table_imag)


def inverse_local(spec_real, spec_imag, phase_bin, total_len):
    outer_len, channel_count, inner_len = spec_real.shape
    length = outer_len * inner_len
    table_real, table_imag = dft_table(outer_len)
    real_part, imag_part = complex_einsum(
        "mck,mb->cbk", spec_real, spec_imag, table_real, -table_imag
    )
    outer_ids = lax.iota(jnp.int32, outer_len)[:, None]
    inner_ids = lax.iota(jnp.int32, inner_len)[None, :]
    cosine, sine_part = twiddle(outer_ids * inner_ids, length)
    sine_part = -sine_part
    real_part, imag_part = (
        real_part * cosine - imag_part * sine_part,
        real_part * sine_part + imag_part * cosine,
    )
    table_real, table_imag = dft_table(inner_len)
    real_part, imag_part = complex_einsum(
        "cbk,ka->cab", real_part, imag_part, table_real, -table_imag
    )
    real_part = real_part.reshape(channel_count, length)
    imag_part = imag_part.reshape(channel_count, length)
    sample_pos = lax.iota(jnp.int32, length)
    cosine, sine_part = twiddle(sample_pos * phase_bin % total_len, total_len)
    sine_part = -sine_part
    return (real_part * cosine - imag_part * sine_part, real_part * sine_part + imag_part * cosine)


def mix_bins(spread, band, response, offsets):
    fine_len, channel_all, inner_len = (spread.shape[1], spread.shape[2], spread.shape[3])
    band_width = band.shape[1]
    half_width = band_width // 2
    shift_cols = offsets.reshape(1, fine_len, 1, inner_len)
    centered = (shift_cols + half_width) % channel_all - half_width
    moved = jnp.zeros_like(spread)
    for shift_amount in range(-half_width, half_width + 1):
        rolled = jnp.roll(spread, -shift_amount, axis=2)
        moved = jnp.where(centered == shift_amount, rolled, moved)
    moved_real = moved[0]
    moved_imag = moved[1]
    wide_real = jnp.concatenate([moved_real, moved_real[:, : band_width - 1]], axis=1)
    wide_imag = jnp.concatenate([moved_imag, moved_imag[:, : band_width - 1]], axis=1)
    responses = response.reshape(2, band_width, fine_len, 1, inner_len)
    acc_real = jnp.zeros_like(moved_real)
    acc_imag = jnp.zeros_like(moved_imag)
    for lag_index in range(band_width):
        value_real = wide_real[:, lag_index : lag_index + channel_all]
        value_imag = wide_imag[:, lag_index : lag_index + channel_all]
        gain_real = band[0, lag_index][None, :, None]
        gain_imag = band[1, lag_index][None, :, None]
        coef_real = gain_real * responses[0, lag_index] - gain_imag * responses[1, lag_index]
        coef_imag = gain_real * responses[1, lag_index] + gain_imag * responses[0, lag_index]
        acc_real = acc_real + coef_real * value_real - coef_imag * value_imag
        acc_imag = acc_imag + coef_real * value_imag + coef_imag * value_real
    return (acc_real, acc_imag)


def per_device(signal, band, response, offsets):
    blocks = lax.axis_size("tm")
    levels = blocks.bit_length() - 1
    device_pos = lax.axis_index("tm")
    phase_bin = reverse_bits(device_pos, levels)
    channel_count, length = signal.shape
    total_len = length * blocks
    inner_len = math.gcd(128, length // lax.axis_size("chan"))
    real_part = signal
    imag_part = jnp.zeros_like(signal)
    for bit_index in range(levels - 1, -1, -1):
        half_span = 1 << bit_index
        partner = from_partner(jnp.stack([real_part, imag_part]), "tm", bit_index)
        upper_half = device_pos // half_span % 2 == 1
        cosine, sine_part = twiddle(device_pos % half_span, 2 * half_span)
        diff_real = partner[0] - real_part
        diff_imag = partner[1] - imag_part
        new_real = jnp.where(
            upper_half, diff_real * cosine - diff_imag * sine_part, real_part + partner[0]
        )
        new_imag = jnp.where(
            upper_half, diff_real * sine_part + diff_imag * cosine, imag_part + partner[1]
        )
        real_part, imag_part = (new_real, new_imag)
    spec_real, spec_imag = forward_local(real_part, imag_part, phase_bin, total_len, inner_len)
    spread = lax.all_to_all(
        jnp.stack([spec_real, spec_imag]), "chan", split_axis=1, concat_axis=2, tiled=True
    )
    mixed_real, mixed_imag = mix_bins(spread, band, response, offsets)
    returned = lax.all_to_all(
        jnp.stack([mixed_real, mixed_imag]), "chan", split_axis=2, concat_axis=1, tiled=True
    )
    real_part, imag_part = inverse_local(returned[0], returned[1], phase_bin, total_len)
    for bit_index in range(levels):
        half_span = 1 << bit_index
        partner = from_partner(jnp.stack([real_part, imag_part]), "tm", bit_index)
        upper_half = device_pos // half_span % 2 == 1
        cosine, sine_part = twiddle(device_pos % half_span, 2 * half_span)
        sine_part = -sine_part
        base_real = jnp.where(upper_half, partner[0], real_part)
        base_imag = jnp.where(upper_half, partner[1], imag_part)
        scaled_real = jnp.where(upper_half, real_part, partner[0])
        scaled_imag = jnp.where(upper_half, imag_part, partner[1])
        prod_real = scaled_real * cosine - scaled_imag * sine_part
        prod_imag = scaled_real * sine_part + scaled_imag * cosine
        real_part = jnp.where(upper_half, base_real - prod_real, base_real + prod_real)
        imag_part = jnp.where(upper_half, base_imag - prod_imag, base_imag + prod_imag)
    smoothed = real_part / total_len
    return smoothed


TM, CHAN, ROWS, LANES, OUTER, BANDW, HALF = 4, 8, 8, 128, 64, 16, 8
DEVICES = TM * CHAN
TOTAL = OUTER * LANES


def split_hi_lo(value):
    hi = value.astype(jnp.bfloat16)
    return hi, (value - hi.astype(jnp.float32)).astype(jnp.bfloat16)


def dot3(left, right, dims):
    (lh, ll), (rh, rl) = left, right

    def one(a, b):
        return lax.dot_general(a, b, (dims, ((), ())), preferred_element_type=jnp.float32)

    return one(lh, rh) + (one(lh, rl) + one(ll, rh))


def outer_table():
    n1 = np.arange(OUTER)
    table = np.zeros((OUTER, OUTER))
    for pair in range(DEVICES):
        angle = 2 * np.pi * (n1 * pair % OUTER) / OUTER
        table[2 * pair] = np.cos(angle)
        table[2 * pair + 1] = -np.sin(angle) if pair else (-1.0) ** n1
    return table


def rev(t):
    return (t % 2) * 2 + t // 2


def outer_product(table, value):
    hi, lo = split_hi_lo(value)
    return jnp.dot(table.astype(jnp.bfloat16), jnp.concatenate([hi, lo, hi], axis=0), preferred_element_type=jnp.float32)


def fused(signal, response_in, offsets_in, band_in, base_in, turn_in, table_in, out,
          response, offsets, band_rows, base, turn, table, resp, tall, band, xs, xin, ybuf, sbuf, rbuf, rt, xp, mv, mm, wh, wl, vh, vl,
          dbuf, yback, zbuf, rsend, rrecv, send, recv, own):
    t, g = lax.axis_index("tm"), lax.axis_index("chan")
    d = CHAN // 2 * g + rev(t)
    e = TM * g + t

    def remote(src, dst, k, target):
        return pltpu.make_async_remote_copy(
            src_ref=src, dst_ref=dst, send_sem=send.at[k], recv_sem=recv.at[k],
            device_id=target, device_id_type=pl.DeviceIdType.MESH)

    def local(src, dst, sem):
        return pltpu.make_async_copy(src, dst, sem)

    barrier = pltpu.get_barrier_semaphore()
    for hop in range(1, TM):
        pl.semaphore_signal(barrier, inc=1, device_id=((t + hop) % TM, g), device_id_type=pl.DeviceIdType.MESH)
    for hop in range(1, CHAN):
        pl.semaphore_signal(barrier, inc=1, device_id=(t, (g + hop) % CHAN), device_id_type=pl.DeviceIdType.MESH)
    copies = [local(src, dst, own.at[i]) for i, (src, dst) in enumerate((
        (response_in, response), (offsets_in, offsets), (band_in, band_rows), (base_in, base),
        (turn_in.at[d], turn), (table_in, table)))]
    for copy in copies:
        copy.start()
    pl.semaphore_wait(barrier, TM + CHAN - 2)

    for hop in (2, 1, 3):
        to = (t + hop) % TM
        remote(signal.at[pl.ds(ROWS * to, ROWS)], xin.at[t], 0, (to, g)).start()
    local(signal.at[pl.ds(ROWS * t, ROWS)], xin.at[t], recv.at[0]).start()

    copies[0].wait()
    copies[1].wait()
    centered = ((offsets[...] + HALF) % 256 - HALF).astype(jnp.float32)
    filler = jnp.zeros((LANES - 2 * BANDW - 8, 256), jnp.float32)
    tall[...] = jnp.concatenate([response[...], jnp.broadcast_to(centered, (8, 256)), filler], axis=0).T
    for s in range(16):
        resp[s] = tall[pl.ds(s, 16, stride=16), :]

    def send_resp(part, s, block, target):
        return pltpu.make_async_remote_copy(
            src_ref=resp.at[s], dst_ref=rbuf.at[part, pl.ds(16 * block, 16)], send_sem=rsend.at[part],
            recv_sem=rrecv.at[part], device_id=target, device_id_type=pl.DeviceIdType.MESH)

    t_b = jnp.where(t < 2, t, 5 - t)
    s_own = jnp.where(t == 0, (8 - g) % 8, 7 - g) + 8
    local(resp.at[g], rbuf.at[0, pl.ds(16 * g, 16)], rrecv.at[0]).start()
    for hop in range(1, CHAN):
        to = (g + hop) % CHAN
        send_resp(0, to, g, (t, to)).start()

    def send_b():
        for hop in range(1, CHAN):
            to = (g + hop) % CHAN
            send_resp(1, jnp.where(t == 0, (8 - to) % 8, 7 - to) + 8, g, (t_b, to)).start()

    @pl.when(t < 2)
    def _():
        send_b()
        local(resp.at[s_own], rbuf.at[1, pl.ds(16 * g, 16)], rrecv.at[1]).start()

    copies[2].wait()
    band[...] = jnp.concatenate([band_rows[...], jnp.zeros((LANES - 2 * BANDW, 256), jnp.float32)], axis=0).T

    for copy in copies[3:]:
        copy.wait()
    first = d == 0
    for part in range(2):
        tc, ts = turn[2 * part : 2 * part + 1, :], turn[2 * part + 1 : 2 * part + 2, :]
        bc, bs = base[0], base[1]
        tr = tc * bc - ts * bs
        ti = tc * bs + ts * bc
        zero = jnp.zeros_like(tr)
        if part == 0:
            blocks = ((tr, ti), (jnp.where(first, zero, -ti), jnp.where(first, zero, tr)))
        else:
            blocks = ((jnp.where(first, zero, tr), jnp.where(first, zero, ti)),
                      (jnp.where(first, tr, ti), jnp.where(first, ti, -tr)))
        for row in range(2):
            for col in range(2):
                inner = slice(LANES * row, LANES * (row + 1))
                outer = slice(LANES * (2 * part + col), LANES * (2 * part + col + 1))
                vh[outer, inner], vl[outer, inner] = split_hi_lo(blocks[row][col])
                wh[inner, outer], wl[inner, outer] = split_hi_lo(blocks[row][col].T)

    local(xin, xin, recv.at[0]).wait()

    @pl.when(t >= 2)
    def _():
        send_b()
        pltpu.make_async_remote_copy(
            src_ref=resp.at[s_own], dst_ref=rbuf.at[1, pl.ds(16 * g, 16)], send_sem=rsend.at[2],
            recv_sem=rrecv.at[1], device_id=(5 - t, g), device_id_type=pl.DeviceIdType.MESH).start()

    for b in range(TM):
        for i in range(16):
            xs[pl.ds(ROWS * (16 * b + i), ROWS), :] = xin[b, :, LANES * i : LANES * (i + 1)]
    ycols = ybuf.reshape(DEVICES * 2 * ROWS, LANES)
    taken = jnp.concatenate([xs[pl.ds(c, OUTER, stride=ROWS), :] for c in range(ROWS)], axis=1)
    result = outer_product(table[0], taken)
    for c in range(ROWS):
        ycols[pl.ds(c, OUTER, stride=ROWS), :] = result[:, LANES * c : LANES * (c + 1)]

    def send_pair(hop, carry):
        to = (d + hop) % DEVICES
        remote(ybuf.at[to], sbuf.at[e], 1, (rev(to % 4), to // 4)).start()
        return carry

    lax.fori_loop(1, DEVICES, send_pair, 0)
    local(ybuf.at[d], sbuf.at[e], recv.at[1]).start()

    for part in range(2):
        local(rbuf.at[part], rbuf.at[part], rrecv.at[part]).wait()
        rt[part] = rbuf[part].T

    local(sbuf, sbuf, recv.at[1]).wait()
    rows = jnp.concatenate([sbuf[:, 0].reshape(256, LANES), sbuf[:, 1].reshape(256, LANES)], axis=1)
    spec = dot3(split_hi_lo(rows), (wh[...], wl[...]), ((1,), (0,)))
    for part in range(2):
        for ri in range(2):
            at = LANES * (2 * part + ri)
            piece = spec[:, at : at + LANES]
            xp[part, ri, 8:264] = piece
            xp[part, ri, 0:8] = piece[248:256]
            xp[part, ri, 264:288] = piece[0:24]

    def shift(i, carry):
        at = 8 * i
        for part in range(2):
            off = jnp.broadcast_to(rt[part, 32:33, :], (8, LANES))
            got = [jnp.zeros((8, LANES), jnp.float32)] * 2
            for o in range(-HALF, HALF + 1):
                hit = off == float(o)
                for ri in range(2):
                    got[ri] = jnp.where(hit, xp[part, ri, pl.ds(at + 8 + o, 8), :], got[ri])
            for ri in range(2):
                mv[part, ri, pl.ds(pl.multiple_of(at, 8), 8), :] = got[ri]
        return carry

    lax.fori_loop(0, 34, shift, 0, unroll=2)

    def chunk(step, carry):
        top = 64 * ((step + g // 2) % 4)

        def mix(i, inner):
            at = pl.multiple_of(top + 8 * i, 8)
            gains = band[pl.ds(at, 8), :]
            acc = [jnp.zeros((8, LANES), jnp.float32)] * 4
            for j in range(BANDW):
                br = jnp.broadcast_to(gains[:, j : j + 1], (8, LANES))
                bi = jnp.broadcast_to(gains[:, BANDW + j : BANDW + j + 1], (8, LANES))
                for part in range(2):
                    rr, ri = rt[part, j : j + 1, :], rt[part, BANDW + j : BANDW + j + 1, :]
                    cr = br * rr - bi * ri
                    ci = br * ri + bi * rr
                    xr = mv[part, 0, pl.ds(at + j, 8), :]
                    xi = mv[part, 1, pl.ds(at + j, 8), :]
                    acc[2 * part] = acc[2 * part] + (cr * xr - ci * xi)
                    acc[2 * part + 1] = acc[2 * part + 1] + (cr * xi + ci * xr)
            for q in range(4):
                mm[pl.ds(pl.multiple_of(8 * i, 8), 8), LANES * q : LANES * (q + 1)] = acc[q]
            return inner

        lax.fori_loop(0, 8, mix, 0)
        back = dot3(split_hi_lo(mm[...]), (vh[...], vl[...]), ((1,), (0,)))
        e0 = top // 8
        for ri in range(2):
            dbuf[pl.ds(e0, 8), ri] = back[:, LANES * ri : LANES * (ri + 1)].reshape(8, 8, LANES)

        def send_back(u, inner):
            to = e0 + u

            @pl.when(to != e)
            def _():
                remote(dbuf.at[to], yback.at[d], 2, (to % TM, to // TM)).start()

            @pl.when(to == e)
            def _():
                local(dbuf.at[to], yback.at[d], recv.at[2]).start()

            return inner

        lax.fori_loop(0, 8, send_back, 0)
        return carry

    lax.fori_loop(0, 4, chunk, 0)

    local(yback, yback, recv.at[2]).wait()
    bcols = yback.reshape(DEVICES * 2 * ROWS, LANES)
    taken = jnp.concatenate([bcols[pl.ds(c, OUTER, stride=ROWS), :] for c in range(ROWS)], axis=1)
    result = outer_product(table[1], taken)
    for c in range(ROWS):
        xs[pl.ds(c, OUTER, stride=ROWS), :] = result[:, LANES * c : LANES * (c + 1)]
    for b in range(TM):
        for i in range(16):
            zbuf[b, :, LANES * i : LANES * (i + 1)] = xs[pl.ds(ROWS * (16 * b + i), ROWS), :]
    for hop in (2, 1, 3):
        to = (t + hop) % TM
        remote(zbuf.at[to], out.at[pl.ds(ROWS * t, ROWS)], 3, (to, g)).start()
    local(zbuf.at[t], out.at[pl.ds(ROWS * t, ROWS)], recv.at[3]).start()
    local(out, out, recv.at[3]).wait()

    for k in (0, 3):
        local(signal.at[pl.ds(0, 24)], signal.at[pl.ds(0, 24)], send.at[k]).wait()
    for k in (1, 2):
        local(ybuf.at[pl.ds(0, 31)], ybuf.at[pl.ds(0, 31)], send.at[k]).wait()
    for part in range(2):
        local(resp.at[pl.ds(0, 7)], resp.at[pl.ds(0, 7)], rsend.at[part]).wait()

    @pl.when(t >= 2)
    def _():
        local(resp.at[0], resp.at[0], rsend.at[2]).wait()


def per_device_fused(signal, band, response, offsets):
    n2 = np.arange(LANES)
    angle = -2 * np.pi * (n2[:, None] * n2[None, :] % LANES) / LANES
    base = jnp.asarray(np.stack([np.cos(angle), np.sin(angle)]).astype(np.float32))
    pairs = np.arange(DEVICES)[:, None]
    other = np.where(pairs == 0, DEVICES, OUTER - pairs)
    turns = [-2 * np.pi * (n2[None, :] * k1 % TOTAL) / TOTAL for k1 in (pairs, other)]
    rows = [np.cos(turns[0]), np.sin(turns[0]), np.cos(turns[1]), np.sin(turns[1])]
    turn = jnp.asarray(np.stack(rows * 2, axis=1).astype(np.float32))
    forward = outer_table()
    tables = []
    for matrix in (forward, forward.T / TOTAL):
        matrix = matrix.astype(np.float32)
        hi = matrix.astype(jnp.bfloat16)
        lo = (matrix - hi.astype(np.float32)).astype(jnp.bfloat16)
        tables.append(np.concatenate([hi, hi, lo], axis=1).astype(np.float32))
    table = jnp.asarray(np.stack(tables))

    f32 = jnp.float32
    hbm = pl.BlockSpec(memory_space=pl.ANY)
    out = pl.pallas_call(
        fused,
        out_shape=jax.ShapeDtypeStruct((32, 16 * LANES), f32),
        in_specs=[hbm] * 7,
        out_specs=hbm,
        scratch_shapes=[
            pltpu.VMEM((2 * BANDW, 256), f32),
            pltpu.VMEM((1, 256), jnp.int32),
            pltpu.VMEM((2 * BANDW, 256), f32),
            pltpu.VMEM((2, LANES, LANES), f32),
            pltpu.VMEM((8, LANES), f32),
            pltpu.VMEM((2, OUTER, 3 * OUTER), f32),
            pltpu.VMEM((16, 16, LANES), f32),
            pltpu.VMEM((2 * LANES, LANES), f32),
            pltpu.VMEM((2 * LANES, LANES), f32),
            pltpu.VMEM((OUTER * ROWS, LANES), f32),
            pltpu.VMEM((TM, ROWS, 16 * LANES), f32),
            pltpu.VMEM((DEVICES, 2, ROWS, LANES), f32),
            pltpu.VMEM((DEVICES, 2, ROWS, LANES), f32),
            pltpu.VMEM((2, LANES, LANES), f32),
            pltpu.VMEM((2, LANES, LANES), f32),
            pltpu.VMEM((2, 2, 288, LANES), f32),
            pltpu.VMEM((2, 2, 272, LANES), f32),
            pltpu.VMEM((64, 4 * LANES), f32),
            pltpu.VMEM((2 * LANES, 4 * LANES), jnp.bfloat16),
            pltpu.VMEM((2 * LANES, 4 * LANES), jnp.bfloat16),
            pltpu.VMEM((4 * LANES, 2 * LANES), jnp.bfloat16),
            pltpu.VMEM((4 * LANES, 2 * LANES), jnp.bfloat16),
            pltpu.VMEM((DEVICES, 2, ROWS, LANES), f32),
            pltpu.VMEM((DEVICES, 2, ROWS, LANES), f32),
            pltpu.VMEM((TM, ROWS, 16 * LANES), f32),
            pltpu.SemaphoreType.DMA((3,)),
            pltpu.SemaphoreType.DMA((2,)),
            pltpu.SemaphoreType.DMA((4,)),
            pltpu.SemaphoreType.DMA((4,)),
            pltpu.SemaphoreType.DMA((6,)),
        ],
        compiler_params=pltpu.CompilerParams(collective_id=0, has_side_effects=True, vmem_limit_bytes=64 << 20),
    )(signal, response.reshape(2 * BANDW, 256), offsets, band.reshape(2 * BANDW, 256), base, turn, table)
    return out


def solution(mesh):
    sizes = dict(mesh.shape)
    tuned = sizes["tm"] == TM and sizes["chan"] == CHAN
    in_specs = (P("chan", "tm"), P(), P(None, "tm", None, "chan"), P("tm", "chan"))
    out_specs = P("chan", "tm")
    return jax.shard_map(
        per_device_fused if tuned else per_device, mesh=mesh, in_specs=in_specs, out_specs=out_specs, check_vma=False
    )
```

```python
import math

import jax
import jax.numpy as jnp
import numpy as np
from jax import lax
from jax.experimental import pallas as pl
from jax.experimental.pallas import tpu as pltpu
from jax.sharding import PartitionSpec as P

PRECISE = lax.Precision.HIGHEST


def from_partner(block, axis, stride):
    count = lax.axis_size(axis)
    route = []
    for low in range(count):
        high = low | 1 << stride
        if high != low and high < count:
            route += [(low, high), (high, low)]
    return lax.ppermute(block, axis, route)


def twiddle(numer, length):
    angle = -2.0 * math.pi / length * numer.astype(jnp.float32)
    return (jnp.cos(angle), jnp.sin(angle))


def dft_table(length):
    steps = lax.iota(jnp.int32, length)
    return twiddle(steps[:, None] * steps[None, :] % length, length)


def reverse_bits(value, bit_count):
    result = value * 0
    for bit_index in range(bit_count):
        result = result + value // (1 << bit_index) % 2 * (1 << bit_count - 1 - bit_index)
    return result


def complex_einsum(form, left_real, left_imag, right_real, right_imag):
    out_real = jnp.einsum(form, left_real, right_real, precision=PRECISE) - jnp.einsum(
        form, left_imag, right_imag, precision=PRECISE
    )
    out_imag = jnp.einsum(form, left_real, right_imag, precision=PRECISE) + jnp.einsum(
        form, left_imag, right_real, precision=PRECISE
    )
    return (out_real, out_imag)


def forward_local(real_part, imag_part, phase_bin, total_len, inner_len):
    channel_count, length = real_part.shape
    outer_len = length // inner_len
    sample_pos = lax.iota(jnp.int32, length)
    cosine, sine_part = twiddle(sample_pos * phase_bin % total_len, total_len)
    real_part, imag_part = (
        real_part * cosine - imag_part * sine_part,
        real_part * sine_part + imag_part * cosine,
    )
    real_part = real_part.reshape(channel_count, inner_len, outer_len)
    imag_part = imag_part.reshape(channel_count, inner_len, outer_len)
    table_real, table_imag = dft_table(inner_len)
    real_part, imag_part = complex_einsum(
        "cab,ak->cbk", real_part, imag_part, table_real, table_imag
    )
    outer_ids = lax.iota(jnp.int32, outer_len)[:, None]
    inner_ids = lax.iota(jnp.int32, inner_len)[None, :]
    cosine, sine_part = twiddle(outer_ids * inner_ids, length)
    real_part, imag_part = (
        real_part * cosine - imag_part * sine_part,
        real_part * sine_part + imag_part * cosine,
    )
    table_real, table_imag = dft_table(outer_len)
    return complex_einsum("cbk,bm->mck", real_part, imag_part, table_real, table_imag)


def inverse_local(spec_real, spec_imag, phase_bin, total_len):
    outer_len, channel_count, inner_len = spec_real.shape
    length = outer_len * inner_len
    table_real, table_imag = dft_table(outer_len)
    real_part, imag_part = complex_einsum(
        "mck,mb->cbk", spec_real, spec_imag, table_real, -table_imag
    )
    outer_ids = lax.iota(jnp.int32, outer_len)[:, None]
    inner_ids = lax.iota(jnp.int32, inner_len)[None, :]
    cosine, sine_part = twiddle(outer_ids * inner_ids, length)
    sine_part = -sine_part
    real_part, imag_part = (
        real_part * cosine - imag_part * sine_part,
        real_part * sine_part + imag_part * cosine,
    )
    table_real, table_imag = dft_table(inner_len)
    real_part, imag_part = complex_einsum(
        "cbk,ka->cab", real_part, imag_part, table_real, -table_imag
    )
    real_part = real_part.reshape(channel_count, length)
    imag_part = imag_part.reshape(channel_count, length)
    sample_pos = lax.iota(jnp.int32, length)
    cosine, sine_part = twiddle(sample_pos * phase_bin % total_len, total_len)
    sine_part = -sine_part
    return (real_part * cosine - imag_part * sine_part, real_part * sine_part + imag_part * cosine)


def mix_bins(spread, band, response, offsets):
    fine_len, channel_all, inner_len = (spread.shape[1], spread.shape[2], spread.shape[3])
    band_width = band.shape[1]
    half_width = band_width // 2
    shift_cols = offsets.reshape(1, fine_len, 1, inner_len)
    centered = (shift_cols + half_width) % channel_all - half_width
    moved = jnp.zeros_like(spread)
    for shift_amount in range(-half_width, half_width + 1):
        rolled = jnp.roll(spread, -shift_amount, axis=2)
        moved = jnp.where(centered == shift_amount, rolled, moved)
    moved_real = moved[0]
    moved_imag = moved[1]
    wide_real = jnp.concatenate([moved_real, moved_real[:, : band_width - 1]], axis=1)
    wide_imag = jnp.concatenate([moved_imag, moved_imag[:, : band_width - 1]], axis=1)
    responses = response.reshape(2, band_width, fine_len, 1, inner_len)
    acc_real = jnp.zeros_like(moved_real)
    acc_imag = jnp.zeros_like(moved_imag)
    for lag_index in range(band_width):
        value_real = wide_real[:, lag_index : lag_index + channel_all]
        value_imag = wide_imag[:, lag_index : lag_index + channel_all]
        gain_real = band[0, lag_index][None, :, None]
        gain_imag = band[1, lag_index][None, :, None]
        coef_real = gain_real * responses[0, lag_index] - gain_imag * responses[1, lag_index]
        coef_imag = gain_real * responses[1, lag_index] + gain_imag * responses[0, lag_index]
        acc_real = acc_real + coef_real * value_real - coef_imag * value_imag
        acc_imag = acc_imag + coef_real * value_imag + coef_imag * value_real
    return (acc_real, acc_imag)


def per_device(signal, band, response, offsets):
    blocks = lax.axis_size("tm")
    levels = blocks.bit_length() - 1
    device_pos = lax.axis_index("tm")
    phase_bin = reverse_bits(device_pos, levels)
    channel_count, length = signal.shape
    total_len = length * blocks
    inner_len = math.gcd(128, length // lax.axis_size("chan"))
    real_part = signal
    imag_part = jnp.zeros_like(signal)
    for bit_index in range(levels - 1, -1, -1):
        half_span = 1 << bit_index
        partner = from_partner(jnp.stack([real_part, imag_part]), "tm", bit_index)
        upper_half = device_pos // half_span % 2 == 1
        cosine, sine_part = twiddle(device_pos % half_span, 2 * half_span)
        diff_real = partner[0] - real_part
        diff_imag = partner[1] - imag_part
        new_real = jnp.where(
            upper_half, diff_real * cosine - diff_imag * sine_part, real_part + partner[0]
        )
        new_imag = jnp.where(
            upper_half, diff_real * sine_part + diff_imag * cosine, imag_part + partner[1]
        )
        real_part, imag_part = (new_real, new_imag)
    spec_real, spec_imag = forward_local(real_part, imag_part, phase_bin, total_len, inner_len)
    spread = lax.all_to_all(
        jnp.stack([spec_real, spec_imag]), "chan", split_axis=1, concat_axis=2, tiled=True
    )
    mixed_real, mixed_imag = mix_bins(spread, band, response, offsets)
    returned = lax.all_to_all(
        jnp.stack([mixed_real, mixed_imag]), "chan", split_axis=2, concat_axis=1, tiled=True
    )
    real_part, imag_part = inverse_local(returned[0], returned[1], phase_bin, total_len)
    for bit_index in range(levels):
        half_span = 1 << bit_index
        partner = from_partner(jnp.stack([real_part, imag_part]), "tm", bit_index)
        upper_half = device_pos // half_span % 2 == 1
        cosine, sine_part = twiddle(device_pos % half_span, 2 * half_span)
        sine_part = -sine_part
        base_real = jnp.where(upper_half, partner[0], real_part)
        base_imag = jnp.where(upper_half, partner[1], imag_part)
        scaled_real = jnp.where(upper_half, real_part, partner[0])
        scaled_imag = jnp.where(upper_half, imag_part, partner[1])
        prod_real = scaled_real * cosine - scaled_imag * sine_part
        prod_imag = scaled_real * sine_part + scaled_imag * cosine
        real_part = jnp.where(upper_half, base_real - prod_real, base_real + prod_real)
        imag_part = jnp.where(upper_half, base_imag - prod_imag, base_imag + prod_imag)
    smoothed = real_part / total_len
    return smoothed


TM, CHAN, ROWS, LANES, OUTER, BANDW, HALF = 4, 8, 8, 128, 64, 16, 8
DEVICES = TM * CHAN
TOTAL = OUTER * LANES


def split_hi_lo(value):
    hi = value.astype(jnp.bfloat16)
    return hi, (value - hi.astype(jnp.float32)).astype(jnp.bfloat16)


def product(value, table_hi, table_lo):
    hi, lo = split_hi_lo(value)
    rows = value.shape[0]
    both = jnp.dot(jnp.concatenate([hi, lo], axis=0), table_hi[...], preferred_element_type=jnp.float32)
    return both[:rows] + (both[rows:] + jnp.dot(hi, table_lo[...], preferred_element_type=jnp.float32))


def outer_table():
    n1 = np.arange(OUTER)
    table = np.zeros((OUTER, OUTER))
    for pair in range(DEVICES):
        angle = 2 * np.pi * (n1 * pair % OUTER) / OUTER
        table[2 * pair] = np.cos(angle)
        table[2 * pair + 1] = -np.sin(angle) if pair else (-1.0) ** n1
    return table


def rev(t):
    return (t % 2) * 2 + t // 2


def outer_product(table, value):
    hi, lo = split_hi_lo(value)
    return jnp.dot(table.astype(jnp.bfloat16), jnp.concatenate([hi, lo, hi], axis=0), preferred_element_type=jnp.float32)


def fused(signal, response_in, offsets_in, band_in, base_in, turn_in, table_in, out,
          response, offsets, band_rows, base, turn, table, resp, tall, band, xs, xin, ybuf, sbuf, rbuf, rt, xp, mv, mm, wh, wl, vh, vl,
          dbuf, yback, zbuf, rsend, rrecv, send, recv, own, arrive):
    t, g = lax.axis_index("tm"), lax.axis_index("chan")
    d = CHAN // 2 * g + rev(t)
    e = TM * g + t

    def remote(src, dst, k, target):
        return pltpu.make_async_remote_copy(
            src_ref=src, dst_ref=dst, send_sem=send.at[k], recv_sem=recv.at[k],
            device_id=target, device_id_type=pl.DeviceIdType.MESH)

    def local(src, dst, sem):
        return pltpu.make_async_copy(src, dst, sem)

    barrier = pltpu.get_barrier_semaphore()
    for hop in range(1, TM):
        pl.semaphore_signal(barrier, inc=1, device_id=((t + hop) % TM, g), device_id_type=pl.DeviceIdType.MESH)
    for hop in range(1, CHAN):
        pl.semaphore_signal(barrier, inc=1, device_id=(t, (g + hop) % CHAN), device_id_type=pl.DeviceIdType.MESH)
    copies = [local(src, dst, own.at[i]) for i, (src, dst) in enumerate((
        (response_in, response), (offsets_in, offsets), (band_in, band_rows), (base_in, base),
        (turn_in.at[d], turn), (table_in, table)))]
    for copy in copies:
        copy.start()
    pl.semaphore_wait(barrier, TM + CHAN - 2)

    for hop in (2, 1, 3):
        to = (t + hop) % TM
        remote(signal.at[pl.ds(ROWS * to, ROWS)], xin.at[t], 0, (to, g)).start()
    local(signal.at[pl.ds(ROWS * t, ROWS)], xin.at[t], recv.at[0]).start()

    copies[0].wait()
    copies[1].wait()
    centered = ((offsets[...] + HALF) % 256 - HALF).astype(jnp.float32)
    filler = jnp.zeros((LANES - 2 * BANDW - 8, 256), jnp.float32)
    tall[...] = jnp.concatenate([response[...], jnp.broadcast_to(centered, (8, 256)), filler], axis=0).T
    for s in range(16):
        resp[s] = tall[pl.ds(s, 16, stride=16), :]

    def send_resp(part, s, block, target):
        return pltpu.make_async_remote_copy(
            src_ref=resp.at[s], dst_ref=rbuf.at[part, pl.ds(16 * block, 16)], send_sem=rsend.at[part],
            recv_sem=rrecv.at[part], device_id=target, device_id_type=pl.DeviceIdType.MESH)

    t_b = jnp.where(t < 2, t, 5 - t)
    s_own = jnp.where(t == 0, (8 - g) % 8, 7 - g) + 8
    local(resp.at[g], rbuf.at[0, pl.ds(16 * g, 16)], rrecv.at[0]).start()
    for hop in range(1, CHAN):
        to = (g + hop) % CHAN
        send_resp(0, to, g, (t, to)).start()

    def send_b():
        for hop in range(1, CHAN):
            to = (g + hop) % CHAN
            send_resp(1, jnp.where(t == 0, (8 - to) % 8, 7 - to) + 8, g, (t_b, to)).start()

    @pl.when(t < 2)
    def _():
        send_b()
        local(resp.at[s_own], rbuf.at[1, pl.ds(16 * g, 16)], rrecv.at[1]).start()

    copies[2].wait()
    band[...] = jnp.concatenate([band_rows[...], jnp.zeros((LANES - 2 * BANDW, 256), jnp.float32)], axis=0).T

    for copy in copies[3:]:
        copy.wait()
    first = d == 0
    for part in range(2):
        tc, ts = turn[2 * part : 2 * part + 1, :], turn[2 * part + 1 : 2 * part + 2, :]
        bc, bs = base[0], base[1]
        tr = tc * bc - ts * bs
        ti = tc * bs + ts * bc
        zero = jnp.zeros_like(tr)
        if part == 0:
            blocks = ((tr, ti), (jnp.where(first, zero, -ti), jnp.where(first, zero, tr)))
        else:
            blocks = ((jnp.where(first, zero, tr), jnp.where(first, zero, ti)),
                      (jnp.where(first, tr, ti), jnp.where(first, ti, -tr)))
        for row in range(2):
            for col in range(2):
                inner = slice(LANES * row, LANES * (row + 1))
                outer = slice(LANES * (2 * part + col), LANES * (2 * part + col + 1))
                vh[outer, inner], vl[outer, inner] = split_hi_lo(blocks[row][col])
                wh[inner, outer], wl[inner, outer] = split_hi_lo(blocks[row][col].T)

    local(xin, xin, recv.at[0]).wait()

    @pl.when(t >= 2)
    def _():
        send_b()
        pltpu.make_async_remote_copy(
            src_ref=resp.at[s_own], dst_ref=rbuf.at[1, pl.ds(16 * g, 16)], send_sem=rsend.at[2],
            recv_sem=rrecv.at[1], device_id=(5 - t, g), device_id_type=pl.DeviceIdType.MESH).start()

    for b in range(TM):
        for i in range(16):
            xs[pl.ds(ROWS * (16 * b + i), ROWS), :] = xin[b, :, LANES * i : LANES * (i + 1)]
    ycols = ybuf.reshape(DEVICES * 2 * ROWS, LANES)
    taken = jnp.concatenate([xs[pl.ds(c, OUTER, stride=ROWS), :] for c in range(ROWS)], axis=1)
    result = outer_product(table[0], taken)
    for c in range(ROWS):
        ycols[pl.ds(c, OUTER, stride=ROWS), :] = result[:, LANES * c : LANES * (c + 1)]

    line = g // 2

    def send_pair(hop, carry):
        to = 8 * ((line + 4 - hop // 8) % 4) + (d + hop) % 8
        pltpu.make_async_remote_copy(
            src_ref=ybuf.at[to], dst_ref=sbuf.at[e], send_sem=send.at[1], recv_sem=arrive.at[line],
            device_id=(rev(to % 4), to // 4), device_id_type=pl.DeviceIdType.MESH).start()
        return carry

    local(ybuf.at[d], sbuf.at[e], arrive.at[line]).start()
    lax.fori_loop(1, DEVICES, send_pair, 0)

    for part in range(2):
        local(rbuf.at[part], rbuf.at[part], rrecv.at[part]).wait()
        rt[part] = rbuf[part].T

    def ingest(i):
        q = (line + i) % 4
        eight = sbuf.at[pl.ds(8 * q, 8)]
        local(eight, eight, arrive.at[q]).wait()
        rows = jnp.concatenate([eight[:, 0].reshape(64, LANES), eight[:, 1].reshape(64, LANES)], axis=1)
        spec = product(rows, wh, wl)
        for part in range(2):
            for ri in range(2):
                at = LANES * (2 * part + ri)
                xp[part, ri, pl.ds(pl.multiple_of(64 * i, 64), 64), :] = spec[:, at : at + LANES]

    def shift(i, carry):
        at = 8 * i
        for part in range(2):
            off = jnp.broadcast_to(rt[part, 32:33, :], (8, LANES))
            got = [jnp.zeros((8, LANES), jnp.float32)] * 2
            for o in range(-HALF, HALF + 1):
                hit = off == float(o)
                for ri in range(2):
                    got[ri] = jnp.where(hit, xp[part, ri, pl.ds(at + o, 8), :], got[ri])
            for ri in range(2):
                mv[part, ri, pl.ds(pl.multiple_of(at, 8), 8), :] = got[ri]
        return carry

    ingest(0)
    for part in range(2):
        for ri in range(2):
            xp[part, ri, 256:288] = xp[part, ri, 0:32]
    lax.fori_loop(1, 3, shift, 0, unroll=2)

    def chunk(step, carry):
        @pl.when(step < 3)
        def _():
            ingest(step + 1)

        lax.fori_loop(0, 8, lambda i, inner: shift(8 * step + 3 + i, inner), 0, unroll=2)

        def mix(i, inner):
            at = 64 * step + 8 + 8 * i
            gains = band[pl.ds(pl.multiple_of((64 * line + at) % 256, 8), 8), :]
            acc = [jnp.zeros((8, LANES), jnp.float32)] * 4
            for j in range(BANDW):
                br = jnp.broadcast_to(gains[:, j : j + 1], (8, LANES))
                bi = jnp.broadcast_to(gains[:, BANDW + j : BANDW + j + 1], (8, LANES))
                for part in range(2):
                    rr, ri = rt[part, j : j + 1, :], rt[part, BANDW + j : BANDW + j + 1, :]
                    cr = br * rr - bi * ri
                    ci = br * ri + bi * rr
                    xr = mv[part, 0, pl.ds(at + j, 8), :]
                    xi = mv[part, 1, pl.ds(at + j, 8), :]
                    acc[2 * part] = acc[2 * part] + (cr * xr - ci * xi)
                    acc[2 * part + 1] = acc[2 * part + 1] + (cr * xi + ci * xr)
            for q in range(4):
                mm[pl.ds(pl.multiple_of(8 * i, 8), 8), LANES * q : LANES * (q + 1)] = acc[q]
            return inner

        lax.fori_loop(0, 8, mix, 0, unroll=2)
        back = product(mm[...], vh, vl)
        for ri in range(2):
            dbuf[pl.ds(8 * step, 8), ri] = back[:, LANES * ri : LANES * (ri + 1)].reshape(8, 8, LANES)

        def send_back(u, inner):
            source = dbuf.at[8 * step + u]
            to = (8 * line + 8 * step + 1 + u) % DEVICES

            @pl.when(to != e)
            def _():
                remote(source, yback.at[d], 2, (to % TM, to // TM)).start()

            @pl.when(to == e)
            def _():
                local(source, yback.at[d], recv.at[2]).start()

            return inner

        lax.fori_loop(0, 8, send_back, 0)
        return carry

    lax.fori_loop(0, 4, chunk, 0)

    local(yback, yback, recv.at[2]).wait()
    bcols = yback.reshape(DEVICES * 2 * ROWS, LANES)
    taken = jnp.concatenate([bcols[pl.ds(c, OUTER, stride=ROWS), :] for c in range(ROWS)], axis=1)
    result = outer_product(table[1], taken)
    for c in range(ROWS):
        xs[pl.ds(c, OUTER, stride=ROWS), :] = result[:, LANES * c : LANES * (c + 1)]
    for b in range(TM):
        for i in range(16):
            zbuf[b, :, LANES * i : LANES * (i + 1)] = xs[pl.ds(ROWS * (16 * b + i), ROWS), :]
    for hop in (2, 1, 3):
        to = (t + hop) % TM
        remote(zbuf.at[to], out.at[pl.ds(ROWS * t, ROWS)], 3, (to, g)).start()
    local(zbuf.at[t], out.at[pl.ds(ROWS * t, ROWS)], recv.at[3]).start()
    local(out, out, recv.at[3]).wait()

    for k in (0, 3):
        local(signal.at[pl.ds(0, 24)], signal.at[pl.ds(0, 24)], send.at[k]).wait()
    for k in (1, 2):
        local(ybuf.at[pl.ds(0, 31)], ybuf.at[pl.ds(0, 31)], send.at[k]).wait()
    for part in range(2):
        local(resp.at[pl.ds(0, 7)], resp.at[pl.ds(0, 7)], rsend.at[part]).wait()

    @pl.when(t >= 2)
    def _():
        local(resp.at[0], resp.at[0], rsend.at[2]).wait()


def per_device_fused(signal, band, response, offsets):
    n2 = np.arange(LANES)
    angle = -2 * np.pi * (n2[:, None] * n2[None, :] % LANES) / LANES
    base = jnp.asarray(np.stack([np.cos(angle), np.sin(angle)]).astype(np.float32))
    pairs = np.arange(DEVICES)[:, None]
    other = np.where(pairs == 0, DEVICES, OUTER - pairs)
    turns = [-2 * np.pi * (n2[None, :] * k1 % TOTAL) / TOTAL for k1 in (pairs, other)]
    rows = [np.cos(turns[0]), np.sin(turns[0]), np.cos(turns[1]), np.sin(turns[1])]
    turn = jnp.asarray(np.stack(rows * 2, axis=1).astype(np.float32))
    forward = outer_table()
    tables = []
    for matrix in (forward, forward.T / TOTAL):
        matrix = matrix.astype(np.float32)
        hi = matrix.astype(jnp.bfloat16)
        lo = (matrix - hi.astype(np.float32)).astype(jnp.bfloat16)
        tables.append(np.concatenate([hi, hi, lo], axis=1).astype(np.float32))
    table = jnp.asarray(np.stack(tables))

    f32 = jnp.float32
    hbm = pl.BlockSpec(memory_space=pl.ANY)
    out = pl.pallas_call(
        fused,
        out_shape=jax.ShapeDtypeStruct((32, 16 * LANES), f32),
        in_specs=[hbm] * 7,
        out_specs=hbm,
        scratch_shapes=[
            pltpu.VMEM((2 * BANDW, 256), f32),
            pltpu.VMEM((1, 256), jnp.int32),
            pltpu.VMEM((2 * BANDW, 256), f32),
            pltpu.VMEM((2, LANES, LANES), f32),
            pltpu.VMEM((8, LANES), f32),
            pltpu.VMEM((2, OUTER, 3 * OUTER), f32),
            pltpu.VMEM((16, 16, LANES), f32),
            pltpu.VMEM((2 * LANES, LANES), f32),
            pltpu.VMEM((2 * LANES, LANES), f32),
            pltpu.VMEM((OUTER * ROWS, LANES), f32),
            pltpu.VMEM((TM, ROWS, 16 * LANES), f32),
            pltpu.VMEM((DEVICES, 2, ROWS, LANES), f32),
            pltpu.VMEM((DEVICES, 2, ROWS, LANES), f32),
            pltpu.VMEM((2, LANES, LANES), f32),
            pltpu.VMEM((2, LANES, LANES), f32),
            pltpu.VMEM((2, 2, 288, LANES), f32),
            pltpu.VMEM((2, 2, 280, LANES), f32),
            pltpu.VMEM((64, 4 * LANES), f32),
            pltpu.VMEM((2 * LANES, 4 * LANES), jnp.bfloat16),
            pltpu.VMEM((2 * LANES, 4 * LANES), jnp.bfloat16),
            pltpu.VMEM((4 * LANES, 2 * LANES), jnp.bfloat16),
            pltpu.VMEM((4 * LANES, 2 * LANES), jnp.bfloat16),
            pltpu.VMEM((DEVICES, 2, ROWS, LANES), f32),
            pltpu.VMEM((DEVICES, 2, ROWS, LANES), f32),
            pltpu.VMEM((TM, ROWS, 16 * LANES), f32),
            pltpu.SemaphoreType.DMA((3,)),
            pltpu.SemaphoreType.DMA((2,)),
            pltpu.SemaphoreType.DMA((4,)),
            pltpu.SemaphoreType.DMA((4,)),
            pltpu.SemaphoreType.DMA((6,)),
            pltpu.SemaphoreType.DMA((4,)),
        ],
        compiler_params=pltpu.CompilerParams(collective_id=0, has_side_effects=True, vmem_limit_bytes=64 << 20),
    )(signal, response.reshape(2 * BANDW, 256), offsets, band.reshape(2 * BANDW, 256), base, turn, table)
    return out


def solution(mesh):
    sizes = dict(mesh.shape)
    tuned = sizes["tm"] == TM and sizes["chan"] == CHAN
    in_specs = (P("chan", "tm"), P(), P(None, "tm", None, "chan"), P("tm", "chan"))
    out_specs = P("chan", "tm")
    return jax.shard_map(
        per_device_fused if tuned else per_device, mesh=mesh, in_specs=in_specs, out_specs=out_specs, check_vma=False
    )
```

```python
import math

import jax
import jax.numpy as jnp
import numpy as np
from jax import lax
from jax.experimental import pallas as pl
from jax.experimental.pallas import tpu as pltpu
from jax.sharding import PartitionSpec as P

PRECISE = lax.Precision.HIGHEST


def from_partner(block, axis, stride):
    count = lax.axis_size(axis)
    route = []
    for low in range(count):
        high = low | 1 << stride
        if high != low and high < count:
            route += [(low, high), (high, low)]
    return lax.ppermute(block, axis, route)


def twiddle(numer, length):
    angle = -2.0 * math.pi / length * numer.astype(jnp.float32)
    return (jnp.cos(angle), jnp.sin(angle))


def dft_table(length):
    steps = lax.iota(jnp.int32, length)
    return twiddle(steps[:, None] * steps[None, :] % length, length)


def reverse_bits(value, bit_count):
    result = value * 0
    for bit_index in range(bit_count):
        result = result + value // (1 << bit_index) % 2 * (1 << bit_count - 1 - bit_index)
    return result


def complex_einsum(form, left_real, left_imag, right_real, right_imag):
    out_real = jnp.einsum(form, left_real, right_real, precision=PRECISE) - jnp.einsum(
        form, left_imag, right_imag, precision=PRECISE
    )
    out_imag = jnp.einsum(form, left_real, right_imag, precision=PRECISE) + jnp.einsum(
        form, left_imag, right_real, precision=PRECISE
    )
    return (out_real, out_imag)


def forward_local(real_part, imag_part, phase_bin, total_len, inner_len):
    channel_count, length = real_part.shape
    outer_len = length // inner_len
    sample_pos = lax.iota(jnp.int32, length)
    cosine, sine_part = twiddle(sample_pos * phase_bin % total_len, total_len)
    real_part, imag_part = (
        real_part * cosine - imag_part * sine_part,
        real_part * sine_part + imag_part * cosine,
    )
    real_part = real_part.reshape(channel_count, inner_len, outer_len)
    imag_part = imag_part.reshape(channel_count, inner_len, outer_len)
    table_real, table_imag = dft_table(inner_len)
    real_part, imag_part = complex_einsum(
        "cab,ak->cbk", real_part, imag_part, table_real, table_imag
    )
    outer_ids = lax.iota(jnp.int32, outer_len)[:, None]
    inner_ids = lax.iota(jnp.int32, inner_len)[None, :]
    cosine, sine_part = twiddle(outer_ids * inner_ids, length)
    real_part, imag_part = (
        real_part * cosine - imag_part * sine_part,
        real_part * sine_part + imag_part * cosine,
    )
    table_real, table_imag = dft_table(outer_len)
    return complex_einsum("cbk,bm->mck", real_part, imag_part, table_real, table_imag)


def inverse_local(spec_real, spec_imag, phase_bin, total_len):
    outer_len, channel_count, inner_len = spec_real.shape
    length = outer_len * inner_len
    table_real, table_imag = dft_table(outer_len)
    real_part, imag_part = complex_einsum(
        "mck,mb->cbk", spec_real, spec_imag, table_real, -table_imag
    )
    outer_ids = lax.iota(jnp.int32, outer_len)[:, None]
    inner_ids = lax.iota(jnp.int32, inner_len)[None, :]
    cosine, sine_part = twiddle(outer_ids * inner_ids, length)
    sine_part = -sine_part
    real_part, imag_part = (
        real_part * cosine - imag_part * sine_part,
        real_part * sine_part + imag_part * cosine,
    )
    table_real, table_imag = dft_table(inner_len)
    real_part, imag_part = complex_einsum(
        "cbk,ka->cab", real_part, imag_part, table_real, -table_imag
    )
    real_part = real_part.reshape(channel_count, length)
    imag_part = imag_part.reshape(channel_count, length)
    sample_pos = lax.iota(jnp.int32, length)
    cosine, sine_part = twiddle(sample_pos * phase_bin % total_len, total_len)
    sine_part = -sine_part
    return (real_part * cosine - imag_part * sine_part, real_part * sine_part + imag_part * cosine)


def mix_bins(spread, band, response, offsets):
    fine_len, channel_all, inner_len = (spread.shape[1], spread.shape[2], spread.shape[3])
    band_width = band.shape[1]
    half_width = band_width // 2
    shift_cols = offsets.reshape(1, fine_len, 1, inner_len)
    centered = (shift_cols + half_width) % channel_all - half_width
    moved = jnp.zeros_like(spread)
    for shift_amount in range(-half_width, half_width + 1):
        rolled = jnp.roll(spread, -shift_amount, axis=2)
        moved = jnp.where(centered == shift_amount, rolled, moved)
    moved_real = moved[0]
    moved_imag = moved[1]
    wide_real = jnp.concatenate([moved_real, moved_real[:, : band_width - 1]], axis=1)
    wide_imag = jnp.concatenate([moved_imag, moved_imag[:, : band_width - 1]], axis=1)
    responses = response.reshape(2, band_width, fine_len, 1, inner_len)
    acc_real = jnp.zeros_like(moved_real)
    acc_imag = jnp.zeros_like(moved_imag)
    for lag_index in range(band_width):
        value_real = wide_real[:, lag_index : lag_index + channel_all]
        value_imag = wide_imag[:, lag_index : lag_index + channel_all]
        gain_real = band[0, lag_index][None, :, None]
        gain_imag = band[1, lag_index][None, :, None]
        coef_real = gain_real * responses[0, lag_index] - gain_imag * responses[1, lag_index]
        coef_imag = gain_real * responses[1, lag_index] + gain_imag * responses[0, lag_index]
        acc_real = acc_real + coef_real * value_real - coef_imag * value_imag
        acc_imag = acc_imag + coef_real * value_imag + coef_imag * value_real
    return (acc_real, acc_imag)


def per_device(signal, band, response, offsets):
    blocks = lax.axis_size("tm")
    levels = blocks.bit_length() - 1
    device_pos = lax.axis_index("tm")
    phase_bin = reverse_bits(device_pos, levels)
    channel_count, length = signal.shape
    total_len = length * blocks
    inner_len = math.gcd(128, length // lax.axis_size("chan"))
    real_part = signal
    imag_part = jnp.zeros_like(signal)
    for bit_index in range(levels - 1, -1, -1):
        half_span = 1 << bit_index
        partner = from_partner(jnp.stack([real_part, imag_part]), "tm", bit_index)
        upper_half = device_pos // half_span % 2 == 1
        cosine, sine_part = twiddle(device_pos % half_span, 2 * half_span)
        diff_real = partner[0] - real_part
        diff_imag = partner[1] - imag_part
        new_real = jnp.where(
            upper_half, diff_real * cosine - diff_imag * sine_part, real_part + partner[0]
        )
        new_imag = jnp.where(
            upper_half, diff_real * sine_part + diff_imag * cosine, imag_part + partner[1]
        )
        real_part, imag_part = (new_real, new_imag)
    spec_real, spec_imag = forward_local(real_part, imag_part, phase_bin, total_len, inner_len)
    spread = lax.all_to_all(
        jnp.stack([spec_real, spec_imag]), "chan", split_axis=1, concat_axis=2, tiled=True
    )
    mixed_real, mixed_imag = mix_bins(spread, band, response, offsets)
    returned = lax.all_to_all(
        jnp.stack([mixed_real, mixed_imag]), "chan", split_axis=2, concat_axis=1, tiled=True
    )
    real_part, imag_part = inverse_local(returned[0], returned[1], phase_bin, total_len)
    for bit_index in range(levels):
        half_span = 1 << bit_index
        partner = from_partner(jnp.stack([real_part, imag_part]), "tm", bit_index)
        upper_half = device_pos // half_span % 2 == 1
        cosine, sine_part = twiddle(device_pos % half_span, 2 * half_span)
        sine_part = -sine_part
        base_real = jnp.where(upper_half, partner[0], real_part)
        base_imag = jnp.where(upper_half, partner[1], imag_part)
        scaled_real = jnp.where(upper_half, real_part, partner[0])
        scaled_imag = jnp.where(upper_half, imag_part, partner[1])
        prod_real = scaled_real * cosine - scaled_imag * sine_part
        prod_imag = scaled_real * sine_part + scaled_imag * cosine
        real_part = jnp.where(upper_half, base_real - prod_real, base_real + prod_real)
        imag_part = jnp.where(upper_half, base_imag - prod_imag, base_imag + prod_imag)
    smoothed = real_part / total_len
    return smoothed


TM, CHAN, ROWS, LANES, OUTER, BANDW, HALF = 4, 8, 8, 128, 64, 16, 8
DEVICES = TM * CHAN
TOTAL = OUTER * LANES


def split_hi_lo(value):
    hi = value.astype(jnp.bfloat16)
    return hi, (value - hi.astype(jnp.float32)).astype(jnp.bfloat16)


def product(value, table_hi, table_lo):
    hi, lo = split_hi_lo(value)
    rows = value.shape[0]
    both = jnp.dot(jnp.concatenate([hi, lo], axis=0), table_hi[...], preferred_element_type=jnp.float32)
    return both[:rows] + (both[rows:] + jnp.dot(hi, table_lo[...], preferred_element_type=jnp.float32))


def outer_table():
    n1 = np.arange(OUTER)
    table = np.zeros((OUTER, OUTER))
    for pair in range(DEVICES):
        angle = 2 * np.pi * (n1 * pair % OUTER) / OUTER
        table[2 * pair] = np.cos(angle)
        table[2 * pair + 1] = -np.sin(angle) if pair else (-1.0) ** n1
    return table


def rev(t):
    return (t % 2) * 2 + t // 2


def outer_product(table, value):
    hi, lo = split_hi_lo(value)
    return jnp.dot(table.astype(jnp.bfloat16), jnp.concatenate([hi, lo, hi], axis=0), preferred_element_type=jnp.float32)


def fused(signal, response_in, offsets_in, band_in, base_in, turn_in, table_in, out,
          response, offsets, band_rows, base, turn, table, resp, tall, band, xs, xin, ybuf, sbuf, rbuf, rt, xp, mv, mm, wh, wl, vh, vl,
          dbuf, yback, zbuf, rsend, rrecv, send, recv, own, arrive):
    t, g = lax.axis_index("tm"), lax.axis_index("chan")
    d = CHAN // 2 * g + rev(t)
    e = TM * g + t

    def remote(src, dst, k, target):
        return pltpu.make_async_remote_copy(
            src_ref=src, dst_ref=dst, send_sem=send.at[k], recv_sem=recv.at[k],
            device_id=target, device_id_type=pl.DeviceIdType.MESH)

    def local(src, dst, sem):
        return pltpu.make_async_copy(src, dst, sem)

    barrier = pltpu.get_barrier_semaphore()
    for hop in range(1, TM):
        pl.semaphore_signal(barrier, inc=1, device_id=((t + hop) % TM, g), device_id_type=pl.DeviceIdType.MESH)
    for hop in range(1, CHAN):
        pl.semaphore_signal(barrier, inc=1, device_id=(t, (g + hop) % CHAN), device_id_type=pl.DeviceIdType.MESH)
    copies = [local(src, dst, own.at[i]) for i, (src, dst) in enumerate((
        (response_in, response), (offsets_in, offsets), (band_in, band_rows), (base_in, base),
        (turn_in.at[d], turn), (table_in, table)))]
    for copy in copies:
        copy.start()
    pl.semaphore_wait(barrier, TM + CHAN - 2)

    for hop in (2, 1, 3):
        to = (t + hop) % TM
        remote(signal.at[pl.ds(ROWS * to, ROWS)], xin.at[t], 0, (to, g)).start()
    local(signal.at[pl.ds(ROWS * t, ROWS)], xin.at[t], recv.at[0]).start()

    copies[0].wait()
    copies[1].wait()
    centered = ((offsets[...] + HALF) % 256 - HALF).astype(jnp.float32)
    filler = jnp.zeros((LANES - 2 * BANDW - 8, 256), jnp.float32)
    tall[...] = jnp.concatenate([response[...], jnp.broadcast_to(centered, (8, 256)), filler], axis=0).T
    for s in range(16):
        resp[s] = tall[pl.ds(s, 16, stride=16), :]

    def send_resp(part, s, block, target):
        return pltpu.make_async_remote_copy(
            src_ref=resp.at[s], dst_ref=rbuf.at[part, pl.ds(16 * block, 16)], send_sem=rsend.at[part],
            recv_sem=rrecv.at[part], device_id=target, device_id_type=pl.DeviceIdType.MESH)

    t_b = jnp.where(t < 2, t, 5 - t)
    s_own = jnp.where(t == 0, (8 - g) % 8, 7 - g) + 8
    local(resp.at[g], rbuf.at[0, pl.ds(16 * g, 16)], rrecv.at[0]).start()
    for hop in range(1, CHAN):
        to = (g + hop) % CHAN
        send_resp(0, to, g, (t, to)).start()

    def send_b():
        for hop in range(1, CHAN):
            to = (g + hop) % CHAN
            send_resp(1, jnp.where(t == 0, (8 - to) % 8, 7 - to) + 8, g, (t_b, to)).start()

    @pl.when(t < 2)
    def _():
        send_b()
        local(resp.at[s_own], rbuf.at[1, pl.ds(16 * g, 16)], rrecv.at[1]).start()

    copies[2].wait()
    band[...] = jnp.concatenate([band_rows[...], jnp.zeros((LANES - 2 * BANDW, 256), jnp.float32)], axis=0).T

    for copy in copies[3:]:
        copy.wait()
    first = d == 0
    for part in range(2):
        tc, ts = turn[2 * part : 2 * part + 1, :], turn[2 * part + 1 : 2 * part + 2, :]
        bc, bs = base[0], base[1]
        tr = tc * bc - ts * bs
        ti = tc * bs + ts * bc
        zero = jnp.zeros_like(tr)
        if part == 0:
            blocks = ((tr, ti), (jnp.where(first, zero, -ti), jnp.where(first, zero, tr)))
        else:
            blocks = ((jnp.where(first, zero, tr), jnp.where(first, zero, ti)),
                      (jnp.where(first, tr, ti), jnp.where(first, ti, -tr)))
        for row in range(2):
            for col in range(2):
                inner = slice(LANES * row, LANES * (row + 1))
                outer = slice(LANES * (2 * part + col), LANES * (2 * part + col + 1))
                vh[outer, inner], vl[outer, inner] = split_hi_lo(blocks[row][col])
                wh[inner, outer], wl[inner, outer] = split_hi_lo(blocks[row][col].T)

    local(xin, xin, recv.at[0]).wait()

    @pl.when(t >= 2)
    def _():
        send_b()
        pltpu.make_async_remote_copy(
            src_ref=resp.at[s_own], dst_ref=rbuf.at[1, pl.ds(16 * g, 16)], send_sem=rsend.at[2],
            recv_sem=rrecv.at[1], device_id=(5 - t, g), device_id_type=pl.DeviceIdType.MESH).start()

    for b in range(TM):
        for i in range(16):
            xs[pl.ds(ROWS * (16 * b + i), ROWS), :] = xin[b, :, LANES * i : LANES * (i + 1)]
    ycols = ybuf.reshape(DEVICES * 2 * ROWS, LANES)
    taken = jnp.concatenate([xs[pl.ds(c, OUTER, stride=ROWS), :] for c in range(ROWS)], axis=1)
    result = outer_product(table[0], taken)
    for c in range(ROWS):
        ycols[pl.ds(c, OUTER, stride=ROWS), :] = result[:, LANES * c : LANES * (c + 1)]

    line = g // 2

    def send_pair(hop, carry):
        to = 8 * ((line + 4 - hop // 8) % 4) + (d + hop) % 8
        pltpu.make_async_remote_copy(
            src_ref=ybuf.at[to], dst_ref=sbuf.at[e], send_sem=send.at[1], recv_sem=arrive.at[line],
            device_id=(rev(to % 4), to // 4), device_id_type=pl.DeviceIdType.MESH).start()
        return carry

    local(ybuf.at[d], sbuf.at[e], arrive.at[line]).start()
    lax.fori_loop(1, DEVICES, send_pair, 0)

    for part in range(2):
        local(rbuf.at[part], rbuf.at[part], rrecv.at[part]).wait()
        rt[part] = rbuf[part].T

    def ingest(i):
        q = (line + i) % 4
        eight = sbuf.at[pl.ds(8 * q, 8)]
        local(eight, eight, arrive.at[q]).wait()
        rows = jnp.concatenate([eight[:, 0].reshape(64, LANES), eight[:, 1].reshape(64, LANES)], axis=1)
        spec = product(rows, wh, wl)
        for part in range(2):
            for ri in range(2):
                at = LANES * (2 * part + ri)
                xp[part, ri, pl.ds(pl.multiple_of(64 * i, 64), 64), :] = spec[:, at : at + LANES]

    def shift(i, carry):
        at = 8 * i
        for part in range(2):
            off = jnp.broadcast_to(rt[part, 32:33, :], (8, LANES))
            got = [jnp.zeros((8, LANES), jnp.float32)] * 2
            for o in range(-HALF, HALF + 1):
                hit = off == float(o)
                for ri in range(2):
                    got[ri] = jnp.where(hit, xp[part, ri, pl.ds(at + o, 8), :], got[ri])
            for ri in range(2):
                mv[part, ri, pl.ds(pl.multiple_of(at, 8), 8), :] = got[ri]
        return carry

    ingest(0)
    for part in range(2):
        for ri in range(2):
            xp[part, ri, 256:288] = xp[part, ri, 0:32]
    lax.fori_loop(1, 3, shift, 0, unroll=2)

    def chunk(step, carry):
        @pl.when(step < 3)
        def _():
            ingest(step + 1)

        lax.fori_loop(0, 8, lambda i, inner: shift(8 * step + 3 + i, inner), 0, unroll=4)

        def mix(i, inner):
            at = 64 * step + 8 + 8 * i
            gains = band[pl.ds(pl.multiple_of((64 * line + at) % 256, 8), 8), :]
            acc = [jnp.zeros((8, LANES), jnp.float32)] * 4
            for j in range(BANDW):
                br = jnp.broadcast_to(gains[:, j : j + 1], (8, LANES))
                bi = jnp.broadcast_to(gains[:, BANDW + j : BANDW + j + 1], (8, LANES))
                for part in range(2):
                    rr, ri = rt[part, j : j + 1, :], rt[part, BANDW + j : BANDW + j + 1, :]
                    cr = br * rr - bi * ri
                    ci = br * ri + bi * rr
                    xr = mv[part, 0, pl.ds(at + j, 8), :]
                    xi = mv[part, 1, pl.ds(at + j, 8), :]
                    acc[2 * part] = acc[2 * part] + (cr * xr - ci * xi)
                    acc[2 * part + 1] = acc[2 * part + 1] + (cr * xi + ci * xr)
            for q in range(4):
                mm[pl.ds(pl.multiple_of(8 * i, 8), 8), LANES * q : LANES * (q + 1)] = acc[q]
            return inner

        lax.fori_loop(0, 8, mix, 0, unroll=4)
        back = product(mm[...], vh, vl)
        for ri in range(2):
            dbuf[pl.ds(8 * step, 8), ri] = back[:, LANES * ri : LANES * (ri + 1)].reshape(8, 8, LANES)

        def send_back(u, inner):
            source = dbuf.at[8 * step + u]
            to = (8 * line + 8 * step + 1 + u) % DEVICES

            @pl.when(to != e)
            def _():
                remote(source, yback.at[d], 2, (to % TM, to // TM)).start()

            @pl.when(to == e)
            def _():
                local(source, yback.at[d], recv.at[2]).start()

            return inner

        lax.fori_loop(0, 8, send_back, 0)
        return carry

    lax.fori_loop(0, 4, chunk, 0)

    local(yback, yback, recv.at[2]).wait()
    bcols = yback.reshape(DEVICES * 2 * ROWS, LANES)
    taken = jnp.concatenate([bcols[pl.ds(c, OUTER, stride=ROWS), :] for c in range(ROWS)], axis=1)
    result = outer_product(table[1], taken)
    for c in range(ROWS):
        xs[pl.ds(c, OUTER, stride=ROWS), :] = result[:, LANES * c : LANES * (c + 1)]
    for b in range(TM):
        for i in range(16):
            zbuf[b, :, LANES * i : LANES * (i + 1)] = xs[pl.ds(ROWS * (16 * b + i), ROWS), :]
    for hop in (2, 1, 3):
        to = (t + hop) % TM
        remote(zbuf.at[to], out.at[pl.ds(ROWS * t, ROWS)], 3, (to, g)).start()
    local(zbuf.at[t], out.at[pl.ds(ROWS * t, ROWS)], recv.at[3]).start()
    local(out, out, recv.at[3]).wait()

    for k in (0, 3):
        local(signal.at[pl.ds(0, 24)], signal.at[pl.ds(0, 24)], send.at[k]).wait()
    for k in (1, 2):
        local(ybuf.at[pl.ds(0, 31)], ybuf.at[pl.ds(0, 31)], send.at[k]).wait()
    for part in range(2):
        local(resp.at[pl.ds(0, 7)], resp.at[pl.ds(0, 7)], rsend.at[part]).wait()

    @pl.when(t >= 2)
    def _():
        local(resp.at[0], resp.at[0], rsend.at[2]).wait()


def per_device_fused(signal, band, response, offsets):
    n2 = np.arange(LANES)
    angle = -2 * np.pi * (n2[:, None] * n2[None, :] % LANES) / LANES
    base = jnp.asarray(np.stack([np.cos(angle), np.sin(angle)]).astype(np.float32))
    pairs = np.arange(DEVICES)[:, None]
    other = np.where(pairs == 0, DEVICES, OUTER - pairs)
    turns = [-2 * np.pi * (n2[None, :] * k1 % TOTAL) / TOTAL for k1 in (pairs, other)]
    rows = [np.cos(turns[0]), np.sin(turns[0]), np.cos(turns[1]), np.sin(turns[1])]
    turn = jnp.asarray(np.stack(rows * 2, axis=1).astype(np.float32))
    forward = outer_table()
    tables = []
    for matrix in (forward, forward.T / TOTAL):
        matrix = matrix.astype(np.float32)
        hi = matrix.astype(jnp.bfloat16)
        lo = (matrix - hi.astype(np.float32)).astype(jnp.bfloat16)
        tables.append(np.concatenate([hi, hi, lo], axis=1).astype(np.float32))
    table = jnp.asarray(np.stack(tables))

    f32 = jnp.float32
    hbm = pl.BlockSpec(memory_space=pl.ANY)
    out = pl.pallas_call(
        fused,
        out_shape=jax.ShapeDtypeStruct((32, 16 * LANES), f32),
        in_specs=[hbm] * 7,
        out_specs=hbm,
        scratch_shapes=[
            pltpu.VMEM((2 * BANDW, 256), f32),
            pltpu.VMEM((1, 256), jnp.int32),
            pltpu.VMEM((2 * BANDW, 256), f32),
            pltpu.VMEM((2, LANES, LANES), f32),
            pltpu.VMEM((8, LANES), f32),
            pltpu.VMEM((2, OUTER, 3 * OUTER), f32),
            pltpu.VMEM((16, 16, LANES), f32),
            pltpu.VMEM((2 * LANES, LANES), f32),
            pltpu.VMEM((2 * LANES, LANES), f32),
            pltpu.VMEM((OUTER * ROWS, LANES), f32),
            pltpu.VMEM((TM, ROWS, 16 * LANES), f32),
            pltpu.VMEM((DEVICES, 2, ROWS, LANES), f32),
            pltpu.VMEM((DEVICES, 2, ROWS, LANES), f32),
            pltpu.VMEM((2, LANES, LANES), f32),
            pltpu.VMEM((2, LANES, LANES), f32),
            pltpu.VMEM((2, 2, 288, LANES), f32),
            pltpu.VMEM((2, 2, 280, LANES), f32),
            pltpu.VMEM((64, 4 * LANES), f32),
            pltpu.VMEM((2 * LANES, 4 * LANES), jnp.bfloat16),
            pltpu.VMEM((2 * LANES, 4 * LANES), jnp.bfloat16),
            pltpu.VMEM((4 * LANES, 2 * LANES), jnp.bfloat16),
            pltpu.VMEM((4 * LANES, 2 * LANES), jnp.bfloat16),
            pltpu.VMEM((DEVICES, 2, ROWS, LANES), f32),
            pltpu.VMEM((DEVICES, 2, ROWS, LANES), f32),
            pltpu.VMEM((TM, ROWS, 16 * LANES), f32),
            pltpu.SemaphoreType.DMA((3,)),
            pltpu.SemaphoreType.DMA((2,)),
            pltpu.SemaphoreType.DMA((4,)),
            pltpu.SemaphoreType.DMA((4,)),
            pltpu.SemaphoreType.DMA((6,)),
            pltpu.SemaphoreType.DMA((4,)),
        ],
        compiler_params=pltpu.CompilerParams(collective_id=0, has_side_effects=True, vmem_limit_bytes=40 << 20),
    )(*(pltpu.with_memory_space_constraint(x, pltpu.HBM) for x in (
        signal, response.reshape(2 * BANDW, 256), offsets, band.reshape(2 * BANDW, 256), base, turn, table)))
    return out


def solution(mesh):
    sizes = dict(mesh.shape)
    tuned = sizes["tm"] == TM and sizes["chan"] == CHAN
    in_specs = (P("chan", "tm"), P(), P(None, "tm", None, "chan"), P("tm", "chan"))
    out_specs = P("chan", "tm")
    return jax.shard_map(
        per_device_fused if tuned else per_device, mesh=mesh, in_specs=in_specs, out_specs=out_specs, check_vma=False
    )
```

```python
import math

import jax
import jax.numpy as jnp
import numpy as np
from jax import lax
from jax.experimental import pallas as pl
from jax.experimental.pallas import tpu as pltpu
from jax.sharding import PartitionSpec as P

PRECISE = lax.Precision.HIGHEST


def from_partner(block, axis, stride):
    count = lax.axis_size(axis)
    route = []
    for low in range(count):
        high = low | 1 << stride
        if high != low and high < count:
            route += [(low, high), (high, low)]
    return lax.ppermute(block, axis, route)


def twiddle(numer, length):
    angle = -2.0 * math.pi / length * numer.astype(jnp.float32)
    return (jnp.cos(angle), jnp.sin(angle))


def dft_table(length):
    steps = lax.iota(jnp.int32, length)
    return twiddle(steps[:, None] * steps[None, :] % length, length)


def reverse_bits(value, bit_count):
    result = value * 0
    for bit_index in range(bit_count):
        result = result + value // (1 << bit_index) % 2 * (1 << bit_count - 1 - bit_index)
    return result


def complex_einsum(form, left_real, left_imag, right_real, right_imag):
    out_real = jnp.einsum(form, left_real, right_real, precision=PRECISE) - jnp.einsum(
        form, left_imag, right_imag, precision=PRECISE
    )
    out_imag = jnp.einsum(form, left_real, right_imag, precision=PRECISE) + jnp.einsum(
        form, left_imag, right_real, precision=PRECISE
    )
    return (out_real, out_imag)


def forward_local(real_part, imag_part, phase_bin, total_len, inner_len):
    channel_count, length = real_part.shape
    outer_len = length // inner_len
    sample_pos = lax.iota(jnp.int32, length)
    cosine, sine_part = twiddle(sample_pos * phase_bin % total_len, total_len)
    real_part, imag_part = (
        real_part * cosine - imag_part * sine_part,
        real_part * sine_part + imag_part * cosine,
    )
    real_part = real_part.reshape(channel_count, inner_len, outer_len)
    imag_part = imag_part.reshape(channel_count, inner_len, outer_len)
    table_real, table_imag = dft_table(inner_len)
    real_part, imag_part = complex_einsum(
        "cab,ak->cbk", real_part, imag_part, table_real, table_imag
    )
    outer_ids = lax.iota(jnp.int32, outer_len)[:, None]
    inner_ids = lax.iota(jnp.int32, inner_len)[None, :]
    cosine, sine_part = twiddle(outer_ids * inner_ids, length)
    real_part, imag_part = (
        real_part * cosine - imag_part * sine_part,
        real_part * sine_part + imag_part * cosine,
    )
    table_real, table_imag = dft_table(outer_len)
    return complex_einsum("cbk,bm->mck", real_part, imag_part, table_real, table_imag)


def inverse_local(spec_real, spec_imag, phase_bin, total_len):
    outer_len, channel_count, inner_len = spec_real.shape
    length = outer_len * inner_len
    table_real, table_imag = dft_table(outer_len)
    real_part, imag_part = complex_einsum(
        "mck,mb->cbk", spec_real, spec_imag, table_real, -table_imag
    )
    outer_ids = lax.iota(jnp.int32, outer_len)[:, None]
    inner_ids = lax.iota(jnp.int32, inner_len)[None, :]
    cosine, sine_part = twiddle(outer_ids * inner_ids, length)
    sine_part = -sine_part
    real_part, imag_part = (
        real_part * cosine - imag_part * sine_part,
        real_part * sine_part + imag_part * cosine,
    )
    table_real, table_imag = dft_table(inner_len)
    real_part, imag_part = complex_einsum(
        "cbk,ka->cab", real_part, imag_part, table_real, -table_imag
    )
    real_part = real_part.reshape(channel_count, length)
    imag_part = imag_part.reshape(channel_count, length)
    sample_pos = lax.iota(jnp.int32, length)
    cosine, sine_part = twiddle(sample_pos * phase_bin % total_len, total_len)
    sine_part = -sine_part
    return (real_part * cosine - imag_part * sine_part, real_part * sine_part + imag_part * cosine)


def mix_bins(spread, band, response, offsets):
    fine_len, channel_all, inner_len = (spread.shape[1], spread.shape[2], spread.shape[3])
    band_width = band.shape[1]
    half_width = band_width // 2
    shift_cols = offsets.reshape(1, fine_len, 1, inner_len)
    centered = (shift_cols + half_width) % channel_all - half_width
    moved = jnp.zeros_like(spread)
    for shift_amount in range(-half_width, half_width + 1):
        rolled = jnp.roll(spread, -shift_amount, axis=2)
        moved = jnp.where(centered == shift_amount, rolled, moved)
    moved_real = moved[0]
    moved_imag = moved[1]
    wide_real = jnp.concatenate([moved_real, moved_real[:, : band_width - 1]], axis=1)
    wide_imag = jnp.concatenate([moved_imag, moved_imag[:, : band_width - 1]], axis=1)
    responses = response.reshape(2, band_width, fine_len, 1, inner_len)
    acc_real = jnp.zeros_like(moved_real)
    acc_imag = jnp.zeros_like(moved_imag)
    for lag_index in range(band_width):
        value_real = wide_real[:, lag_index : lag_index + channel_all]
        value_imag = wide_imag[:, lag_index : lag_index + channel_all]
        gain_real = band[0, lag_index][None, :, None]
        gain_imag = band[1, lag_index][None, :, None]
        coef_real = gain_real * responses[0, lag_index] - gain_imag * responses[1, lag_index]
        coef_imag = gain_real * responses[1, lag_index] + gain_imag * responses[0, lag_index]
        acc_real = acc_real + coef_real * value_real - coef_imag * value_imag
        acc_imag = acc_imag + coef_real * value_imag + coef_imag * value_real
    return (acc_real, acc_imag)


def per_device(signal, band, response, offsets):
    blocks = lax.axis_size("tm")
    levels = blocks.bit_length() - 1
    device_pos = lax.axis_index("tm")
    phase_bin = reverse_bits(device_pos, levels)
    channel_count, length = signal.shape
    total_len = length * blocks
    inner_len = math.gcd(128, length // lax.axis_size("chan"))
    real_part = signal
    imag_part = jnp.zeros_like(signal)
    for bit_index in range(levels - 1, -1, -1):
        half_span = 1 << bit_index
        partner = from_partner(jnp.stack([real_part, imag_part]), "tm", bit_index)
        upper_half = device_pos // half_span % 2 == 1
        cosine, sine_part = twiddle(device_pos % half_span, 2 * half_span)
        diff_real = partner[0] - real_part
        diff_imag = partner[1] - imag_part
        new_real = jnp.where(
            upper_half, diff_real * cosine - diff_imag * sine_part, real_part + partner[0]
        )
        new_imag = jnp.where(
            upper_half, diff_real * sine_part + diff_imag * cosine, imag_part + partner[1]
        )
        real_part, imag_part = (new_real, new_imag)
    spec_real, spec_imag = forward_local(real_part, imag_part, phase_bin, total_len, inner_len)
    spread = lax.all_to_all(
        jnp.stack([spec_real, spec_imag]), "chan", split_axis=1, concat_axis=2, tiled=True
    )
    mixed_real, mixed_imag = mix_bins(spread, band, response, offsets)
    returned = lax.all_to_all(
        jnp.stack([mixed_real, mixed_imag]), "chan", split_axis=2, concat_axis=1, tiled=True
    )
    real_part, imag_part = inverse_local(returned[0], returned[1], phase_bin, total_len)
    for bit_index in range(levels):
        half_span = 1 << bit_index
        partner = from_partner(jnp.stack([real_part, imag_part]), "tm", bit_index)
        upper_half = device_pos // half_span % 2 == 1
        cosine, sine_part = twiddle(device_pos % half_span, 2 * half_span)
        sine_part = -sine_part
        base_real = jnp.where(upper_half, partner[0], real_part)
        base_imag = jnp.where(upper_half, partner[1], imag_part)
        scaled_real = jnp.where(upper_half, real_part, partner[0])
        scaled_imag = jnp.where(upper_half, imag_part, partner[1])
        prod_real = scaled_real * cosine - scaled_imag * sine_part
        prod_imag = scaled_real * sine_part + scaled_imag * cosine
        real_part = jnp.where(upper_half, base_real - prod_real, base_real + prod_real)
        imag_part = jnp.where(upper_half, base_imag - prod_imag, base_imag + prod_imag)
    smoothed = real_part / total_len
    return smoothed


TM, CHAN, ROWS, LANES, OUTER, BANDW, HALF = 4, 8, 8, 128, 64, 16, 8
DEVICES = TM * CHAN
TOTAL = OUTER * LANES


def split_hi_lo(value):
    hi = value.astype(jnp.bfloat16)
    return hi, (value - hi.astype(jnp.float32)).astype(jnp.bfloat16)


def product(value, table_hi, table_lo):
    hi, lo = split_hi_lo(value)
    rows = value.shape[0]
    both = jnp.dot(jnp.concatenate([hi, lo], axis=0), table_hi[...], preferred_element_type=jnp.float32)
    return both[:rows] + (both[rows:] + jnp.dot(hi, table_lo[...], preferred_element_type=jnp.float32))


def outer_table():
    n1 = np.arange(OUTER)
    table = np.zeros((OUTER, OUTER))
    for pair in range(DEVICES):
        angle = 2 * np.pi * (n1 * pair % OUTER) / OUTER
        table[2 * pair] = np.cos(angle)
        table[2 * pair + 1] = -np.sin(angle) if pair else (-1.0) ** n1
    return table


def rev(t):
    return (t % 2) * 2 + t // 2


def outer_product(table, value):
    hi, lo = split_hi_lo(value)
    return jnp.dot(table.astype(jnp.bfloat16), jnp.concatenate([hi, lo, hi], axis=0), preferred_element_type=jnp.float32)


def fused(signal, response_in, offsets_in, band_in, base_in, turn_in, table_in, out,
          response, offsets, band_rows, base, turn, table, resp, tall, band, xs, xin, ybuf, sbuf, rbuf, rt, xp, mv, mm, wh, wl, vh, vl,
          dbuf, yback, zbuf, wide, resp_wide, rsend, rrecv, send, recv, own, arrive):
    t, g = lax.axis_index("tm"), lax.axis_index("chan")
    d = CHAN // 2 * g + rev(t)
    e = TM * g + t

    def remote(src, dst, k, target):
        return pltpu.make_async_remote_copy(
            src_ref=src, dst_ref=dst, send_sem=send.at[k], recv_sem=recv.at[k],
            device_id=target, device_id_type=pl.DeviceIdType.MESH)

    def local(src, dst, sem):
        return pltpu.make_async_copy(src, dst, sem)

    barrier = pltpu.get_barrier_semaphore()
    for hop in range(1, TM):
        pl.semaphore_signal(barrier, inc=1, device_id=((t + hop) % TM, g), device_id_type=pl.DeviceIdType.MESH)
    for hop in range(1, CHAN):
        pl.semaphore_signal(barrier, inc=1, device_id=(t, (g + hop) % CHAN), device_id_type=pl.DeviceIdType.MESH)
    copies = [local(src, dst, own.at[i]) for i, (src, dst) in enumerate((
        (response_in, response), (offsets_in, offsets), (band_in, band_rows), (base_in, base),
        (turn_in.at[d], turn), (table_in, table)))]
    for copy in copies:
        copy.start()
    pl.semaphore_wait(barrier, TM + CHAN - 2)

    for hop in (2, 1, 3):
        to = (t + hop) % TM
        remote(signal.at[pl.ds(ROWS * to, ROWS)], xin.at[t], 0, (to, g)).start()
    local(signal.at[pl.ds(ROWS * t, ROWS)], xin.at[t], recv.at[0]).start()

    copies[0].wait()
    copies[1].wait()
    centered = ((offsets[...] + HALF) % 256 - HALF).astype(jnp.float32)
    filler = jnp.zeros((LANES - 2 * BANDW - 8, 256), jnp.float32)
    tall[...] = jnp.concatenate([response[...], jnp.broadcast_to(centered, (8, 256)), filler], axis=0).T
    for s in range(16):
        resp[s] = tall[pl.ds(s, 16, stride=16), :]

    def send_resp(part, s, block, target):
        return pltpu.make_async_remote_copy(
            src_ref=resp.at[s], dst_ref=rbuf.at[part, pl.ds(16 * block, 16)], send_sem=rsend.at[part],
            recv_sem=rrecv.at[part], device_id=target, device_id_type=pl.DeviceIdType.MESH)

    t_b = jnp.where(t < 2, t, 5 - t)
    s_own = jnp.where(t == 0, (8 - g) % 8, 7 - g) + 8
    local(resp.at[g], rbuf.at[0, pl.ds(16 * g, 16)], rrecv.at[0]).start()
    for hop in range(1, CHAN):
        to = (g + hop) % CHAN
        send_resp(0, to, g, (t, to)).start()

    def send_b():
        for hop in range(1, CHAN):
            to = (g + hop) % CHAN
            send_resp(1, jnp.where(t == 0, (8 - to) % 8, 7 - to) + 8, g, (t_b, to)).start()

    @pl.when(t < 2)
    def _():
        send_b()
        local(resp.at[s_own], rbuf.at[1, pl.ds(16 * g, 16)], rrecv.at[1]).start()

    copies[2].wait()
    band[...] = jnp.concatenate([band_rows[...], jnp.zeros((LANES - 2 * BANDW, 256), jnp.float32)], axis=0).T

    for copy in copies[3:]:
        copy.wait()
    first = d == 0
    for part in range(2):
        tc, ts = turn[2 * part : 2 * part + 1, :], turn[2 * part + 1 : 2 * part + 2, :]
        bc, bs = base[0], base[1]
        tr = tc * bc - ts * bs
        ti = tc * bs + ts * bc
        zero = jnp.zeros_like(tr)
        if part == 0:
            blocks = ((tr, ti), (jnp.where(first, zero, -ti), jnp.where(first, zero, tr)))
        else:
            blocks = ((jnp.where(first, zero, tr), jnp.where(first, zero, ti)),
                      (jnp.where(first, tr, ti), jnp.where(first, ti, -tr)))
        for row in range(2):
            for col in range(2):
                inner = slice(LANES * row, LANES * (row + 1))
                outer = slice(LANES * (2 * part + col), LANES * (2 * part + col + 1))
                vh[outer, inner], vl[outer, inner] = split_hi_lo(blocks[row][col])
                wh[inner, outer], wl[inner, outer] = split_hi_lo(blocks[row][col].T)

    def spread(i, carry):
        rows = pl.ds(pl.multiple_of(8 * i, 8), 8)
        gains = band[rows, :]
        for j in range(2 * BANDW):
            wide[j, rows, :] = jnp.broadcast_to(gains[:, j : j + 1], (8, LANES))
        return carry

    lax.fori_loop(0, 32, spread, 0)

    local(xin, xin, recv.at[0]).wait()

    @pl.when(t >= 2)
    def _():
        send_b()
        pltpu.make_async_remote_copy(
            src_ref=resp.at[s_own], dst_ref=rbuf.at[1, pl.ds(16 * g, 16)], send_sem=rsend.at[2],
            recv_sem=rrecv.at[1], device_id=(5 - t, g), device_id_type=pl.DeviceIdType.MESH).start()

    for b in range(TM):
        for i in range(16):
            xs[pl.ds(ROWS * (16 * b + i), ROWS), :] = xin[b, :, LANES * i : LANES * (i + 1)]
    ycols = ybuf.reshape(DEVICES * 2 * ROWS, LANES)
    taken = jnp.concatenate([xs[pl.ds(c, OUTER, stride=ROWS), :] for c in range(ROWS)], axis=1)
    result = outer_product(table[0], taken)
    for c in range(ROWS):
        ycols[pl.ds(c, OUTER, stride=ROWS), :] = result[:, LANES * c : LANES * (c + 1)]

    line = g // 2

    def send_pair(hop, carry):
        to = 8 * ((line + 4 - hop // 8) % 4) + (d + hop) % 8
        pltpu.make_async_remote_copy(
            src_ref=ybuf.at[to], dst_ref=sbuf.at[e], send_sem=send.at[1], recv_sem=arrive.at[line],
            device_id=(rev(to % 4), to // 4), device_id_type=pl.DeviceIdType.MESH).start()
        return carry

    local(ybuf.at[d], sbuf.at[e], arrive.at[line]).start()
    lax.fori_loop(1, DEVICES, send_pair, 0)

    for part in range(2):
        local(rbuf.at[part], rbuf.at[part], rrecv.at[part]).wait()
        rt[part] = rbuf[part].T
        for j in range(2 * BANDW + 1):
            resp_wide[part, j] = jnp.broadcast_to(rt[part, j : j + 1, :], (8, LANES))

    def ingest(i):
        q = (line + i) % 4
        eight = sbuf.at[pl.ds(8 * q, 8)]
        local(eight, eight, arrive.at[q]).wait()
        rows = jnp.concatenate([eight[:, 0].reshape(64, LANES), eight[:, 1].reshape(64, LANES)], axis=1)
        spec = product(rows, wh, wl)
        for part in range(2):
            for ri in range(2):
                at = LANES * (2 * part + ri)
                xp[part, ri, pl.ds(pl.multiple_of(64 * i, 64), 64), :] = spec[:, at : at + LANES]

    def shift(i, carry):
        at = 8 * i
        for part in range(2):
            off = resp_wide[part, 2 * BANDW]
            got = [jnp.zeros((8, LANES), jnp.float32)] * 2
            for o in range(-HALF, HALF + 1):
                hit = off == float(o)
                for ri in range(2):
                    got[ri] = jnp.where(hit, xp[part, ri, pl.ds(at + o, 8), :], got[ri])
            for ri in range(2):
                mv[part, ri, pl.ds(pl.multiple_of(at, 8), 8), :] = got[ri]
        return carry

    ingest(0)
    for part in range(2):
        for ri in range(2):
            xp[part, ri, 256:288] = xp[part, ri, 0:32]
    lax.fori_loop(1, 3, shift, 0, unroll=2)

    def chunk(step, carry):
        @pl.when(step < 3)
        def _():
            ingest(step + 1)

        lax.fori_loop(0, 8, lambda i, inner: shift(8 * step + 3 + i, inner), 0, unroll=8)

        def mix(i, inner):
            at = 64 * step + 8 + 8 * i
            gains = pl.ds(pl.multiple_of((64 * line + at) % 256, 8), 8)
            acc = [jnp.zeros((8, LANES), jnp.float32)] * 4
            for j in range(BANDW):
                br, bi = wide[j, gains, :], wide[BANDW + j, gains, :]
                for part in range(2):
                    rr, ri = resp_wide[part, j], resp_wide[part, BANDW + j]
                    cr = br * rr - bi * ri
                    ci = br * ri + bi * rr
                    xr = mv[part, 0, pl.ds(at + j, 8), :]
                    xi = mv[part, 1, pl.ds(at + j, 8), :]
                    acc[2 * part] = acc[2 * part] + (cr * xr - ci * xi)
                    acc[2 * part + 1] = acc[2 * part + 1] + (cr * xi + ci * xr)
            for q in range(4):
                mm[pl.ds(pl.multiple_of(8 * i, 8), 8), LANES * q : LANES * (q + 1)] = acc[q]
            return inner

        lax.fori_loop(0, 8, mix, 0, unroll=8)
        back = product(mm[...], vh, vl)
        for ri in range(2):
            dbuf[pl.ds(8 * step, 8), ri] = back[:, LANES * ri : LANES * (ri + 1)].reshape(8, 8, LANES)

        def send_back(u, inner):
            source = dbuf.at[8 * step + u]
            to = (8 * line + 8 * step + 1 + u) % DEVICES

            @pl.when(to != e)
            def _():
                remote(source, yback.at[d], 2, (to % TM, to // TM)).start()

            @pl.when(to == e)
            def _():
                local(source, yback.at[d], recv.at[2]).start()

            return inner

        lax.fori_loop(0, 8, send_back, 0)
        return carry

    lax.fori_loop(0, 4, chunk, 0)

    local(yback, yback, recv.at[2]).wait()
    bcols = yback.reshape(DEVICES * 2 * ROWS, LANES)
    taken = jnp.concatenate([bcols[pl.ds(c, OUTER, stride=ROWS), :] for c in range(ROWS)], axis=1)
    result = outer_product(table[1], taken)
    for c in range(ROWS):
        xs[pl.ds(c, OUTER, stride=ROWS), :] = result[:, LANES * c : LANES * (c + 1)]
    for b in range(TM):
        for i in range(16):
            zbuf[b, :, LANES * i : LANES * (i + 1)] = xs[pl.ds(ROWS * (16 * b + i), ROWS), :]
    for hop in (2, 1, 3):
        to = (t + hop) % TM
        remote(zbuf.at[to], out.at[pl.ds(ROWS * t, ROWS)], 3, (to, g)).start()
    local(zbuf.at[t], out.at[pl.ds(ROWS * t, ROWS)], recv.at[3]).start()
    local(out, out, recv.at[3]).wait()

    for k in (0, 3):
        local(signal.at[pl.ds(0, 24)], signal.at[pl.ds(0, 24)], send.at[k]).wait()
    for k in (1, 2):
        local(ybuf.at[pl.ds(0, 31)], ybuf.at[pl.ds(0, 31)], send.at[k]).wait()
    for part in range(2):
        local(resp.at[pl.ds(0, 7)], resp.at[pl.ds(0, 7)], rsend.at[part]).wait()

    @pl.when(t >= 2)
    def _():
        local(resp.at[0], resp.at[0], rsend.at[2]).wait()


def per_device_fused(signal, band, response, offsets):
    n2 = np.arange(LANES)
    angle = -2 * np.pi * (n2[:, None] * n2[None, :] % LANES) / LANES
    base = jnp.asarray(np.stack([np.cos(angle), np.sin(angle)]).astype(np.float32))
    pairs = np.arange(DEVICES)[:, None]
    other = np.where(pairs == 0, DEVICES, OUTER - pairs)
    turns = [-2 * np.pi * (n2[None, :] * k1 % TOTAL) / TOTAL for k1 in (pairs, other)]
    rows = [np.cos(turns[0]), np.sin(turns[0]), np.cos(turns[1]), np.sin(turns[1])]
    turn = jnp.asarray(np.stack(rows * 2, axis=1).astype(np.float32))
    forward = outer_table()
    tables = []
    for matrix in (forward, forward.T / TOTAL):
        matrix = matrix.astype(np.float32)
        hi = matrix.astype(jnp.bfloat16)
        lo = (matrix - hi.astype(np.float32)).astype(jnp.bfloat16)
        tables.append(np.concatenate([hi, hi, lo], axis=1).astype(np.float32))
    table = jnp.asarray(np.stack(tables))

    f32 = jnp.float32
    hbm = pl.BlockSpec(memory_space=pl.ANY)
    out = pl.pallas_call(
        fused,
        out_shape=jax.ShapeDtypeStruct((32, 16 * LANES), f32),
        in_specs=[hbm] * 7,
        out_specs=hbm,
        scratch_shapes=[
            pltpu.VMEM((2 * BANDW, 256), f32),
            pltpu.VMEM((1, 256), jnp.int32),
            pltpu.VMEM((2 * BANDW, 256), f32),
            pltpu.VMEM((2, LANES, LANES), f32),
            pltpu.VMEM((8, LANES), f32),
            pltpu.VMEM((2, OUTER, 3 * OUTER), f32),
            pltpu.VMEM((16, 16, LANES), f32),
            pltpu.VMEM((2 * LANES, LANES), f32),
            pltpu.VMEM((2 * LANES, LANES), f32),
            pltpu.VMEM((OUTER * ROWS, LANES), f32),
            pltpu.VMEM((TM, ROWS, 16 * LANES), f32),
            pltpu.VMEM((DEVICES, 2, ROWS, LANES), f32),
            pltpu.VMEM((DEVICES, 2, ROWS, LANES), f32),
            pltpu.VMEM((2, LANES, LANES), f32),
            pltpu.VMEM((2, LANES, LANES), f32),
            pltpu.VMEM((2, 2, 288, LANES), f32),
            pltpu.VMEM((2, 2, 280, LANES), f32),
            pltpu.VMEM((64, 4 * LANES), f32),
            pltpu.VMEM((2 * LANES, 4 * LANES), jnp.bfloat16),
            pltpu.VMEM((2 * LANES, 4 * LANES), jnp.bfloat16),
            pltpu.VMEM((4 * LANES, 2 * LANES), jnp.bfloat16),
            pltpu.VMEM((4 * LANES, 2 * LANES), jnp.bfloat16),
            pltpu.VMEM((DEVICES, 2, ROWS, LANES), f32),
            pltpu.VMEM((DEVICES, 2, ROWS, LANES), f32),
            pltpu.VMEM((TM, ROWS, 16 * LANES), f32),
            pltpu.VMEM((2 * BANDW, 256, LANES), f32),
            pltpu.VMEM((2, 2 * BANDW + 1, 8, LANES), f32),
            pltpu.SemaphoreType.DMA((3,)),
            pltpu.SemaphoreType.DMA((2,)),
            pltpu.SemaphoreType.DMA((4,)),
            pltpu.SemaphoreType.DMA((4,)),
            pltpu.SemaphoreType.DMA((6,)),
            pltpu.SemaphoreType.DMA((4,)),
        ],
        compiler_params=pltpu.CompilerParams(collective_id=0, has_side_effects=True, vmem_limit_bytes=40 << 20),
    )(*(pltpu.with_memory_space_constraint(x, pltpu.HBM) for x in (
        signal, response.reshape(2 * BANDW, 256), offsets, band.reshape(2 * BANDW, 256), base, turn, table)))
    return out


def solution(mesh):
    sizes = dict(mesh.shape)
    tuned = sizes["tm"] == TM and sizes["chan"] == CHAN
    in_specs = (P("chan", "tm"), P(), P(None, "tm", None, "chan"), P("tm", "chan"))
    out_specs = P("chan", "tm")
    return jax.shard_map(
        per_device_fused if tuned else per_device, mesh=mesh, in_specs=in_specs, out_specs=out_specs, check_vma=False
    )
```

```python
import math

import jax
import jax.numpy as jnp
import numpy as np
from jax import lax
from jax.experimental import pallas as pl
from jax.experimental.pallas import tpu as pltpu
from jax.sharding import PartitionSpec as P

PRECISE = lax.Precision.HIGHEST


def from_partner(block, axis, stride):
    count = lax.axis_size(axis)
    route = []
    for low in range(count):
        high = low | 1 << stride
        if high != low and high < count:
            route += [(low, high), (high, low)]
    return lax.ppermute(block, axis, route)


def twiddle(numer, length):
    angle = -2.0 * math.pi / length * numer.astype(jnp.float32)
    return (jnp.cos(angle), jnp.sin(angle))


def dft_table(length):
    steps = lax.iota(jnp.int32, length)
    return twiddle(steps[:, None] * steps[None, :] % length, length)


def reverse_bits(value, bit_count):
    result = value * 0
    for bit_index in range(bit_count):
        result = result + value // (1 << bit_index) % 2 * (1 << bit_count - 1 - bit_index)
    return result


def complex_einsum(form, left_real, left_imag, right_real, right_imag):
    out_real = jnp.einsum(form, left_real, right_real, precision=PRECISE) - jnp.einsum(
        form, left_imag, right_imag, precision=PRECISE
    )
    out_imag = jnp.einsum(form, left_real, right_imag, precision=PRECISE) + jnp.einsum(
        form, left_imag, right_real, precision=PRECISE
    )
    return (out_real, out_imag)


def forward_local(real_part, imag_part, phase_bin, total_len, inner_len):
    channel_count, length = real_part.shape
    outer_len = length // inner_len
    sample_pos = lax.iota(jnp.int32, length)
    cosine, sine_part = twiddle(sample_pos * phase_bin % total_len, total_len)
    real_part, imag_part = (
        real_part * cosine - imag_part * sine_part,
        real_part * sine_part + imag_part * cosine,
    )
    real_part = real_part.reshape(channel_count, inner_len, outer_len)
    imag_part = imag_part.reshape(channel_count, inner_len, outer_len)
    table_real, table_imag = dft_table(inner_len)
    real_part, imag_part = complex_einsum(
        "cab,ak->cbk", real_part, imag_part, table_real, table_imag
    )
    outer_ids = lax.iota(jnp.int32, outer_len)[:, None]
    inner_ids = lax.iota(jnp.int32, inner_len)[None, :]
    cosine, sine_part = twiddle(outer_ids * inner_ids, length)
    real_part, imag_part = (
        real_part * cosine - imag_part * sine_part,
        real_part * sine_part + imag_part * cosine,
    )
    table_real, table_imag = dft_table(outer_len)
    return complex_einsum("cbk,bm->mck", real_part, imag_part, table_real, table_imag)


def inverse_local(spec_real, spec_imag, phase_bin, total_len):
    outer_len, channel_count, inner_len = spec_real.shape
    length = outer_len * inner_len
    table_real, table_imag = dft_table(outer_len)
    real_part, imag_part = complex_einsum(
        "mck,mb->cbk", spec_real, spec_imag, table_real, -table_imag
    )
    outer_ids = lax.iota(jnp.int32, outer_len)[:, None]
    inner_ids = lax.iota(jnp.int32, inner_len)[None, :]
    cosine, sine_part = twiddle(outer_ids * inner_ids, length)
    sine_part = -sine_part
    real_part, imag_part = (
        real_part * cosine - imag_part * sine_part,
        real_part * sine_part + imag_part * cosine,
    )
    table_real, table_imag = dft_table(inner_len)
    real_part, imag_part = complex_einsum(
        "cbk,ka->cab", real_part, imag_part, table_real, -table_imag
    )
    real_part = real_part.reshape(channel_count, length)
    imag_part = imag_part.reshape(channel_count, length)
    sample_pos = lax.iota(jnp.int32, length)
    cosine, sine_part = twiddle(sample_pos * phase_bin % total_len, total_len)
    sine_part = -sine_part
    return (real_part * cosine - imag_part * sine_part, real_part * sine_part + imag_part * cosine)


def mix_bins(spread, band, response, offsets):
    fine_len, channel_all, inner_len = (spread.shape[1], spread.shape[2], spread.shape[3])
    band_width = band.shape[1]
    half_width = band_width // 2
    shift_cols = offsets.reshape(1, fine_len, 1, inner_len)
    centered = (shift_cols + half_width) % channel_all - half_width
    moved = jnp.zeros_like(spread)
    for shift_amount in range(-half_width, half_width + 1):
        rolled = jnp.roll(spread, -shift_amount, axis=2)
        moved = jnp.where(centered == shift_amount, rolled, moved)
    moved_real = moved[0]
    moved_imag = moved[1]
    wide_real = jnp.concatenate([moved_real, moved_real[:, : band_width - 1]], axis=1)
    wide_imag = jnp.concatenate([moved_imag, moved_imag[:, : band_width - 1]], axis=1)
    responses = response.reshape(2, band_width, fine_len, 1, inner_len)
    acc_real = jnp.zeros_like(moved_real)
    acc_imag = jnp.zeros_like(moved_imag)
    for lag_index in range(band_width):
        value_real = wide_real[:, lag_index : lag_index + channel_all]
        value_imag = wide_imag[:, lag_index : lag_index + channel_all]
        gain_real = band[0, lag_index][None, :, None]
        gain_imag = band[1, lag_index][None, :, None]
        coef_real = gain_real * responses[0, lag_index] - gain_imag * responses[1, lag_index]
        coef_imag = gain_real * responses[1, lag_index] + gain_imag * responses[0, lag_index]
        acc_real = acc_real + coef_real * value_real - coef_imag * value_imag
        acc_imag = acc_imag + coef_real * value_imag + coef_imag * value_real
    return (acc_real, acc_imag)


def per_device(signal, band, response, offsets):
    blocks = lax.axis_size("tm")
    levels = blocks.bit_length() - 1
    device_pos = lax.axis_index("tm")
    phase_bin = reverse_bits(device_pos, levels)
    channel_count, length = signal.shape
    total_len = length * blocks
    inner_len = math.gcd(128, length // lax.axis_size("chan"))
    real_part = signal
    imag_part = jnp.zeros_like(signal)
    for bit_index in range(levels - 1, -1, -1):
        half_span = 1 << bit_index
        partner = from_partner(jnp.stack([real_part, imag_part]), "tm", bit_index)
        upper_half = device_pos // half_span % 2 == 1
        cosine, sine_part = twiddle(device_pos % half_span, 2 * half_span)
        diff_real = partner[0] - real_part
        diff_imag = partner[1] - imag_part
        new_real = jnp.where(
            upper_half, diff_real * cosine - diff_imag * sine_part, real_part + partner[0]
        )
        new_imag = jnp.where(
            upper_half, diff_real * sine_part + diff_imag * cosine, imag_part + partner[1]
        )
        real_part, imag_part = (new_real, new_imag)
    spec_real, spec_imag = forward_local(real_part, imag_part, phase_bin, total_len, inner_len)
    spread = lax.all_to_all(
        jnp.stack([spec_real, spec_imag]), "chan", split_axis=1, concat_axis=2, tiled=True
    )
    mixed_real, mixed_imag = mix_bins(spread, band, response, offsets)
    returned = lax.all_to_all(
        jnp.stack([mixed_real, mixed_imag]), "chan", split_axis=2, concat_axis=1, tiled=True
    )
    real_part, imag_part = inverse_local(returned[0], returned[1], phase_bin, total_len)
    for bit_index in range(levels):
        half_span = 1 << bit_index
        partner = from_partner(jnp.stack([real_part, imag_part]), "tm", bit_index)
        upper_half = device_pos // half_span % 2 == 1
        cosine, sine_part = twiddle(device_pos % half_span, 2 * half_span)
        sine_part = -sine_part
        base_real = jnp.where(upper_half, partner[0], real_part)
        base_imag = jnp.where(upper_half, partner[1], imag_part)
        scaled_real = jnp.where(upper_half, real_part, partner[0])
        scaled_imag = jnp.where(upper_half, imag_part, partner[1])
        prod_real = scaled_real * cosine - scaled_imag * sine_part
        prod_imag = scaled_real * sine_part + scaled_imag * cosine
        real_part = jnp.where(upper_half, base_real - prod_real, base_real + prod_real)
        imag_part = jnp.where(upper_half, base_imag - prod_imag, base_imag + prod_imag)
    smoothed = real_part / total_len
    return smoothed


TM, CHAN, ROWS, LANES, OUTER, BANDW, HALF = 4, 8, 8, 128, 64, 16, 8
DEVICES = TM * CHAN
TOTAL = OUTER * LANES


def split_hi_lo(value):
    hi = value.astype(jnp.bfloat16)
    return hi, (value - hi.astype(jnp.float32)).astype(jnp.bfloat16)


def product(value, table_hi, table_lo):
    hi, lo = split_hi_lo(value)
    rows = value.shape[0]
    both = jnp.dot(jnp.concatenate([hi, lo], axis=0), table_hi[...], preferred_element_type=jnp.float32)
    return both[:rows] + (both[rows:] + jnp.dot(hi, table_lo[...], preferred_element_type=jnp.float32))


def outer_table():
    n1 = np.arange(OUTER)
    table = np.zeros((OUTER, OUTER))
    for pair in range(DEVICES):
        angle = 2 * np.pi * (n1 * pair % OUTER) / OUTER
        table[2 * pair] = np.cos(angle)
        table[2 * pair + 1] = -np.sin(angle) if pair else (-1.0) ** n1
    return table


def rev(t):
    return (t % 2) * 2 + t // 2


def outer_product(table, value):
    hi, lo = split_hi_lo(value)
    return jnp.dot(table.astype(jnp.bfloat16), jnp.concatenate([hi, lo, hi], axis=0), preferred_element_type=jnp.float32)


def fused(signal, response_in, offsets_in, band_in, base_in, turn_in, table_in, out,
          response, offsets, band_rows, base, turn, table, resp, tall, band, xs, xin, ybuf, sbuf, rbuf, rt, xp, mv, mm, wh, wl, vh, vl,
          dbuf, yback, zbuf, wide, resp_wide, rsend, rrecv, send, recv, own, arrive):
    t, g = lax.axis_index("tm"), lax.axis_index("chan")
    d = CHAN // 2 * g + rev(t)
    e = TM * g + t

    def remote(src, dst, k, target, arrival):
        return pltpu.make_async_remote_copy(
            src_ref=src, dst_ref=dst, send_sem=send.at[k], recv_sem=recv.at[arrival],
            device_id=target, device_id_type=pl.DeviceIdType.MESH)

    def local(src, dst, sem):
        return pltpu.make_async_copy(src, dst, sem)

    barrier = pltpu.get_barrier_semaphore()
    for hop in range(1, TM):
        pl.semaphore_signal(barrier, inc=1, device_id=((t + hop) % TM, g), device_id_type=pl.DeviceIdType.MESH)
    for hop in range(1, CHAN):
        pl.semaphore_signal(barrier, inc=1, device_id=(t, (g + hop) % CHAN), device_id_type=pl.DeviceIdType.MESH)
    copies = [local(src, dst, own.at[i]) for i, (src, dst) in enumerate((
        (response_in, response), (offsets_in, offsets), (band_in, band_rows), (base_in, base),
        (turn_in.at[d], turn), (table_in, table)))]
    for copy in copies:
        copy.start()
    pl.semaphore_wait(barrier, TM + CHAN - 2)

    for h in range(2):
        for hop in (2, 1, 3):
            to = (t + hop) % TM
            remote(signal.at[pl.ds(ROWS * to + 4 * h, 4)], xin.at[t, pl.ds(4 * h, 4)], 0, (to, g), h).start()
        local(signal.at[pl.ds(ROWS * t + 4 * h, 4)], xin.at[t, pl.ds(4 * h, 4)], recv.at[h]).start()

    copies[0].wait()
    copies[1].wait()
    centered = ((offsets[...] + HALF) % 256 - HALF).astype(jnp.float32)
    filler = jnp.zeros((LANES - 2 * BANDW - 8, 256), jnp.float32)
    tall[...] = jnp.concatenate([response[...], jnp.broadcast_to(centered, (8, 256)), filler], axis=0).T
    for s in range(16):
        resp[s] = tall[pl.ds(s, 16, stride=16), :]

    def send_resp(part, s, block, target):
        return pltpu.make_async_remote_copy(
            src_ref=resp.at[s], dst_ref=rbuf.at[part, pl.ds(16 * block, 16)], send_sem=rsend.at[part],
            recv_sem=rrecv.at[part], device_id=target, device_id_type=pl.DeviceIdType.MESH)

    t_b = jnp.where(t < 2, t, 5 - t)
    s_own = jnp.where(t == 0, (8 - g) % 8, 7 - g) + 8
    local(resp.at[g], rbuf.at[0, pl.ds(16 * g, 16)], rrecv.at[0]).start()
    for hop in range(1, CHAN):
        to = (g + hop) % CHAN
        send_resp(0, to, g, (t, to)).start()

    def send_b():
        for hop in range(1, CHAN):
            to = (g + hop) % CHAN
            send_resp(1, jnp.where(t == 0, (8 - to) % 8, 7 - to) + 8, g, (t_b, to)).start()

    @pl.when(t < 2)
    def _():
        send_b()
        local(resp.at[s_own], rbuf.at[1, pl.ds(16 * g, 16)], rrecv.at[1]).start()

    copies[2].wait()
    band[...] = jnp.concatenate([band_rows[...], jnp.zeros((LANES - 2 * BANDW, 256), jnp.float32)], axis=0).T

    for copy in copies[3:]:
        copy.wait()
    first = d == 0
    for part in range(2):
        tc, ts = turn[2 * part : 2 * part + 1, :], turn[2 * part + 1 : 2 * part + 2, :]
        bc, bs = base[0], base[1]
        tr = tc * bc - ts * bs
        ti = tc * bs + ts * bc
        zero = jnp.zeros_like(tr)
        if part == 0:
            blocks = ((tr, ti), (jnp.where(first, zero, -ti), jnp.where(first, zero, tr)))
        else:
            blocks = ((jnp.where(first, zero, tr), jnp.where(first, zero, ti)),
                      (jnp.where(first, tr, ti), jnp.where(first, ti, -tr)))
        for row in range(2):
            for col in range(2):
                inner = slice(LANES * row, LANES * (row + 1))
                outer = slice(LANES * (2 * part + col), LANES * (2 * part + col + 1))
                vh[outer, inner], vl[outer, inner] = split_hi_lo(blocks[row][col])
                wh[inner, outer], wl[inner, outer] = split_hi_lo(blocks[row][col].T)

    line = g // 2
    ycols = ybuf.reshape(DEVICES * 2 * ROWS, LANES)
    for h in range(2):
        half = pl.ds(4 * h, 4)
        local(xin.at[:, half], xin.at[:, half], recv.at[h]).wait()
        for b in range(TM):
            for i in range(16):
                at = ROWS * (16 * b + i) + 4 * h
                xs[pl.ds(at, 4), :] = xin[b, 4 * h : 4 * h + 4, LANES * i : LANES * (i + 1)]
        taken = jnp.concatenate([xs[pl.ds(4 * h + c, OUTER, stride=ROWS), :] for c in range(4)], axis=1)
        result = outer_product(table[0], taken)
        for c in range(4):
            ycols[pl.ds(4 * h + c, OUTER, stride=ROWS), :] = result[:, LANES * c : LANES * (c + 1)]

        def send_pair(hop, carry):
            to = 8 * ((line + 4 - hop // 8) % 4) + (d + hop) % 8
            pltpu.make_async_remote_copy(
                src_ref=ybuf.at[to, :, half], dst_ref=sbuf.at[e, :, half], send_sem=send.at[1],
                recv_sem=arrive.at[line], device_id=(rev(to % 4), to // 4),
                device_id_type=pl.DeviceIdType.MESH).start()
            return carry

        local(ybuf.at[d, :, half], sbuf.at[e, :, half], arrive.at[line]).start()
        lax.fori_loop(1, DEVICES, send_pair, 0)

    @pl.when(t >= 2)
    def _():
        send_b()
        pltpu.make_async_remote_copy(
            src_ref=resp.at[s_own], dst_ref=rbuf.at[1, pl.ds(16 * g, 16)], send_sem=rsend.at[2],
            recv_sem=rrecv.at[1], device_id=(5 - t, g), device_id_type=pl.DeviceIdType.MESH).start()

    def spread(i, carry):
        rows = pl.ds(pl.multiple_of(8 * i, 8), 8)
        gains = band[rows, :]
        for j in range(2 * BANDW):
            wide[j, rows, :] = jnp.broadcast_to(gains[:, j : j + 1], (8, LANES))
        return carry

    lax.fori_loop(0, 32, spread, 0)

    for part in range(2):
        local(rbuf.at[part], rbuf.at[part], rrecv.at[part]).wait()
        rt[part] = rbuf[part].T
        for j in range(2 * BANDW + 1):
            resp_wide[part, j] = jnp.broadcast_to(rt[part, j : j + 1, :], (8, LANES))

    def ingest(i):
        q = (line + i) % 4
        eight = sbuf.at[pl.ds(8 * q, 8)]
        local(eight, eight, arrive.at[q]).wait()
        rows = jnp.concatenate([eight[:, 0].reshape(64, LANES), eight[:, 1].reshape(64, LANES)], axis=1)
        spec = product(rows, wh, wl)
        for part in range(2):
            for ri in range(2):
                at = LANES * (2 * part + ri)
                xp[part, ri, pl.ds(pl.multiple_of(64 * i, 64), 64), :] = spec[:, at : at + LANES]

    def shift(i, carry):
        at = 8 * i
        for part in range(2):
            off = resp_wide[part, 2 * BANDW]
            got = [jnp.zeros((8, LANES), jnp.float32)] * 2
            for o in range(-HALF, HALF + 1):
                hit = off == float(o)
                for ri in range(2):
                    got[ri] = jnp.where(hit, xp[part, ri, pl.ds(at + o, 8), :], got[ri])
            for ri in range(2):
                mv[part, ri, pl.ds(pl.multiple_of(at, 8), 8), :] = got[ri]
        return carry

    ingest(0)
    for part in range(2):
        for ri in range(2):
            xp[part, ri, 256:288] = xp[part, ri, 0:32]
    lax.fori_loop(1, 3, shift, 0, unroll=2)

    def chunk(step, carry):
        @pl.when(step < 3)
        def _():
            ingest(step + 1)

        lax.fori_loop(0, 8, lambda i, inner: shift(8 * step + 3 + i, inner), 0, unroll=8)

        def mix(i, inner):
            at = 64 * step + 8 + 8 * i
            gains = pl.ds(pl.multiple_of((64 * line + at) % 256, 8), 8)
            acc = [jnp.zeros((8, LANES), jnp.float32)] * 4
            for j in range(BANDW):
                br, bi = wide[j, gains, :], wide[BANDW + j, gains, :]
                for part in range(2):
                    rr, ri = resp_wide[part, j], resp_wide[part, BANDW + j]
                    cr = br * rr - bi * ri
                    ci = br * ri + bi * rr
                    xr = mv[part, 0, pl.ds(at + j, 8), :]
                    xi = mv[part, 1, pl.ds(at + j, 8), :]
                    acc[2 * part] = acc[2 * part] + (cr * xr - ci * xi)
                    acc[2 * part + 1] = acc[2 * part + 1] + (cr * xi + ci * xr)
            for q in range(4):
                mm[pl.ds(pl.multiple_of(8 * i, 8), 8), LANES * q : LANES * (q + 1)] = acc[q]
            return inner

        lax.fori_loop(0, 8, mix, 0, unroll=8)
        back = product(mm[...], vh, vl)
        for ri in range(2):
            dbuf[pl.ds(8 * step, 8), ri] = back[:, LANES * ri : LANES * (ri + 1)].reshape(8, 8, LANES)

        send_back(step, 0)

        @pl.when(step > 0)
        def _():
            send_back(step - 1, 1)

        return carry

    def send_back(step, h):
        half = pl.ds(4 * h, 4)

        def one(u, inner):
            source, target = dbuf.at[8 * step + u, :, half], yback.at[d, :, half]
            to = (8 * line + 8 * step + 1 + u) % DEVICES

            @pl.when(to != e)
            def _():
                remote(source, target, 2, (to % TM, to // TM), 2 + h).start()

            @pl.when(to == e)
            def _():
                local(source, target, recv.at[2 + h]).start()

            return inner

        lax.fori_loop(0, 8, one, 0)

    lax.fori_loop(0, 4, chunk, 0)
    send_back(3, 1)

    bcols = yback.reshape(DEVICES * 2 * ROWS, LANES)
    for h in range(2):
        half = pl.ds(4 * h, 4)
        local(yback.at[:, :, half], yback.at[:, :, half], recv.at[2 + h]).wait()
        taken = jnp.concatenate([bcols[pl.ds(4 * h + c, OUTER, stride=ROWS), :] for c in range(4)], axis=1)
        result = outer_product(table[1], taken)
        for c in range(4):
            xs[pl.ds(4 * h + c, OUTER, stride=ROWS), :] = result[:, LANES * c : LANES * (c + 1)]
        for b in range(TM):
            for i in range(16):
                at = ROWS * (16 * b + i) + 4 * h
                zbuf[b, 4 * h : 4 * h + 4, LANES * i : LANES * (i + 1)] = xs[pl.ds(at, 4), :]
        for hop in (2, 1, 3):
            to = (t + hop) % TM
            remote(zbuf.at[to, half], out.at[pl.ds(ROWS * t + 4 * h, 4)], 3, (to, g), 4).start()
        local(zbuf.at[t, half], out.at[pl.ds(ROWS * t + 4 * h, 4)], recv.at[4]).start()
    local(out, out, recv.at[4]).wait()

    for k in (0, 3):
        local(signal.at[pl.ds(0, 24)], signal.at[pl.ds(0, 24)], send.at[k]).wait()
    for k in (1, 2):
        local(ybuf.at[pl.ds(0, 31)], ybuf.at[pl.ds(0, 31)], send.at[k]).wait()
    for part in range(2):
        local(resp.at[pl.ds(0, 7)], resp.at[pl.ds(0, 7)], rsend.at[part]).wait()

    @pl.when(t >= 2)
    def _():
        local(resp.at[0], resp.at[0], rsend.at[2]).wait()


def per_device_fused(signal, band, response, offsets):
    n2 = np.arange(LANES)
    angle = -2 * np.pi * (n2[:, None] * n2[None, :] % LANES) / LANES
    base = jnp.asarray(np.stack([np.cos(angle), np.sin(angle)]).astype(np.float32))
    pairs = np.arange(DEVICES)[:, None]
    other = np.where(pairs == 0, DEVICES, OUTER - pairs)
    turns = [-2 * np.pi * (n2[None, :] * k1 % TOTAL) / TOTAL for k1 in (pairs, other)]
    rows = [np.cos(turns[0]), np.sin(turns[0]), np.cos(turns[1]), np.sin(turns[1])]
    turn = jnp.asarray(np.stack(rows * 2, axis=1).astype(np.float32))
    forward = outer_table()
    tables = []
    for matrix in (forward, forward.T / TOTAL):
        matrix = matrix.astype(np.float32)
        hi = matrix.astype(jnp.bfloat16)
        lo = (matrix - hi.astype(np.float32)).astype(jnp.bfloat16)
        tables.append(np.concatenate([hi, hi, lo], axis=1).astype(np.float32))
    table = jnp.asarray(np.stack(tables))

    f32 = jnp.float32
    hbm = pl.BlockSpec(memory_space=pl.ANY)
    out = pl.pallas_call(
        fused,
        out_shape=jax.ShapeDtypeStruct((32, 16 * LANES), f32),
        in_specs=[hbm] * 7,
        out_specs=hbm,
        scratch_shapes=[
            pltpu.VMEM((2 * BANDW, 256), f32),
            pltpu.VMEM((1, 256), jnp.int32),
            pltpu.VMEM((2 * BANDW, 256), f32),
            pltpu.VMEM((2, LANES, LANES), f32),
            pltpu.VMEM((8, LANES), f32),
            pltpu.VMEM((2, OUTER, 3 * OUTER), f32),
            pltpu.VMEM((16, 16, LANES), f32),
            pltpu.VMEM((2 * LANES, LANES), f32),
            pltpu.VMEM((2 * LANES, LANES), f32),
            pltpu.VMEM((OUTER * ROWS, LANES), f32),
            pltpu.VMEM((TM, ROWS, 16 * LANES), f32),
            pltpu.VMEM((DEVICES, 2, ROWS, LANES), f32),
            pltpu.VMEM((DEVICES, 2, ROWS, LANES), f32),
            pltpu.VMEM((2, LANES, LANES), f32),
            pltpu.VMEM((2, LANES, LANES), f32),
            pltpu.VMEM((2, 2, 288, LANES), f32),
            pltpu.VMEM((2, 2, 280, LANES), f32),
            pltpu.VMEM((64, 4 * LANES), f32),
            pltpu.VMEM((2 * LANES, 4 * LANES), jnp.bfloat16),
            pltpu.VMEM((2 * LANES, 4 * LANES), jnp.bfloat16),
            pltpu.VMEM((4 * LANES, 2 * LANES), jnp.bfloat16),
            pltpu.VMEM((4 * LANES, 2 * LANES), jnp.bfloat16),
            pltpu.VMEM((DEVICES, 2, ROWS, LANES), f32),
            pltpu.VMEM((DEVICES, 2, ROWS, LANES), f32),
            pltpu.VMEM((TM, ROWS, 16 * LANES), f32),
            pltpu.VMEM((2 * BANDW, 256, LANES), f32),
            pltpu.VMEM((2, 2 * BANDW + 1, 8, LANES), f32),
            pltpu.SemaphoreType.DMA((3,)),
            pltpu.SemaphoreType.DMA((2,)),
            pltpu.SemaphoreType.DMA((4,)),
            pltpu.SemaphoreType.DMA((5,)),
            pltpu.SemaphoreType.DMA((6,)),
            pltpu.SemaphoreType.DMA((4,)),
        ],
        compiler_params=pltpu.CompilerParams(collective_id=0, has_side_effects=True, vmem_limit_bytes=40 << 20),
    )(*(pltpu.with_memory_space_constraint(x, pltpu.HBM) for x in (
        signal, response.reshape(2 * BANDW, 256), offsets, band.reshape(2 * BANDW, 256), base, turn, table)))
    return out


def solution(mesh):
    sizes = dict(mesh.shape)
    tuned = sizes["tm"] == TM and sizes["chan"] == CHAN
    in_specs = (P("chan", "tm"), P(), P(None, "tm", None, "chan"), P("tm", "chan"))
    out_specs = P("chan", "tm")
    return jax.shard_map(
        per_device_fused if tuned else per_device, mesh=mesh, in_specs=in_specs, out_specs=out_specs, check_vma=False
    )
```

```python
import math

import jax
import jax.numpy as jnp
import numpy as np
from jax import lax
from jax.experimental import pallas as pl
from jax.experimental.pallas import tpu as pltpu
from jax.sharding import PartitionSpec as P

PRECISE = lax.Precision.HIGHEST


def from_partner(block, axis, stride):
    count = lax.axis_size(axis)
    route = []
    for low in range(count):
        high = low | 1 << stride
        if high != low and high < count:
            route += [(low, high), (high, low)]
    return lax.ppermute(block, axis, route)


def twiddle(numer, length):
    angle = -2.0 * math.pi / length * numer.astype(jnp.float32)
    return (jnp.cos(angle), jnp.sin(angle))


def dft_table(length):
    steps = lax.iota(jnp.int32, length)
    return twiddle(steps[:, None] * steps[None, :] % length, length)


def reverse_bits(value, bit_count):
    result = value * 0
    for bit_index in range(bit_count):
        result = result + value // (1 << bit_index) % 2 * (1 << bit_count - 1 - bit_index)
    return result


def complex_einsum(form, left_real, left_imag, right_real, right_imag):
    out_real = jnp.einsum(form, left_real, right_real, precision=PRECISE) - jnp.einsum(
        form, left_imag, right_imag, precision=PRECISE
    )
    out_imag = jnp.einsum(form, left_real, right_imag, precision=PRECISE) + jnp.einsum(
        form, left_imag, right_real, precision=PRECISE
    )
    return (out_real, out_imag)


def forward_local(real_part, imag_part, phase_bin, total_len, inner_len):
    channel_count, length = real_part.shape
    outer_len = length // inner_len
    sample_pos = lax.iota(jnp.int32, length)
    cosine, sine_part = twiddle(sample_pos * phase_bin % total_len, total_len)
    real_part, imag_part = (
        real_part * cosine - imag_part * sine_part,
        real_part * sine_part + imag_part * cosine,
    )
    real_part = real_part.reshape(channel_count, inner_len, outer_len)
    imag_part = imag_part.reshape(channel_count, inner_len, outer_len)
    table_real, table_imag = dft_table(inner_len)
    real_part, imag_part = complex_einsum(
        "cab,ak->cbk", real_part, imag_part, table_real, table_imag
    )
    outer_ids = lax.iota(jnp.int32, outer_len)[:, None]
    inner_ids = lax.iota(jnp.int32, inner_len)[None, :]
    cosine, sine_part = twiddle(outer_ids * inner_ids, length)
    real_part, imag_part = (
        real_part * cosine - imag_part * sine_part,
        real_part * sine_part + imag_part * cosine,
    )
    table_real, table_imag = dft_table(outer_len)
    return complex_einsum("cbk,bm->mck", real_part, imag_part, table_real, table_imag)


def inverse_local(spec_real, spec_imag, phase_bin, total_len):
    outer_len, channel_count, inner_len = spec_real.shape
    length = outer_len * inner_len
    table_real, table_imag = dft_table(outer_len)
    real_part, imag_part = complex_einsum(
        "mck,mb->cbk", spec_real, spec_imag, table_real, -table_imag
    )
    outer_ids = lax.iota(jnp.int32, outer_len)[:, None]
    inner_ids = lax.iota(jnp.int32, inner_len)[None, :]
    cosine, sine_part = twiddle(outer_ids * inner_ids, length)
    sine_part = -sine_part
    real_part, imag_part = (
        real_part * cosine - imag_part * sine_part,
        real_part * sine_part + imag_part * cosine,
    )
    table_real, table_imag = dft_table(inner_len)
    real_part, imag_part = complex_einsum(
        "cbk,ka->cab", real_part, imag_part, table_real, -table_imag
    )
    real_part = real_part.reshape(channel_count, length)
    imag_part = imag_part.reshape(channel_count, length)
    sample_pos = lax.iota(jnp.int32, length)
    cosine, sine_part = twiddle(sample_pos * phase_bin % total_len, total_len)
    sine_part = -sine_part
    return (real_part * cosine - imag_part * sine_part, real_part * sine_part + imag_part * cosine)


def mix_bins(spread, band, response, offsets):
    fine_len, channel_all, inner_len = (spread.shape[1], spread.shape[2], spread.shape[3])
    band_width = band.shape[1]
    half_width = band_width // 2
    shift_cols = offsets.reshape(1, fine_len, 1, inner_len)
    centered = (shift_cols + half_width) % channel_all - half_width
    moved = jnp.zeros_like(spread)
    for shift_amount in range(-half_width, half_width + 1):
        rolled = jnp.roll(spread, -shift_amount, axis=2)
        moved = jnp.where(centered == shift_amount, rolled, moved)
    moved_real = moved[0]
    moved_imag = moved[1]
    wide_real = jnp.concatenate([moved_real, moved_real[:, : band_width - 1]], axis=1)
    wide_imag = jnp.concatenate([moved_imag, moved_imag[:, : band_width - 1]], axis=1)
    responses = response.reshape(2, band_width, fine_len, 1, inner_len)
    acc_real = jnp.zeros_like(moved_real)
    acc_imag = jnp.zeros_like(moved_imag)
    for lag_index in range(band_width):
        value_real = wide_real[:, lag_index : lag_index + channel_all]
        value_imag = wide_imag[:, lag_index : lag_index + channel_all]
        gain_real = band[0, lag_index][None, :, None]
        gain_imag = band[1, lag_index][None, :, None]
        coef_real = gain_real * responses[0, lag_index] - gain_imag * responses[1, lag_index]
        coef_imag = gain_real * responses[1, lag_index] + gain_imag * responses[0, lag_index]
        acc_real = acc_real + coef_real * value_real - coef_imag * value_imag
        acc_imag = acc_imag + coef_real * value_imag + coef_imag * value_real
    return (acc_real, acc_imag)


def per_device(signal, band, response, offsets):
    blocks = lax.axis_size("tm")
    levels = blocks.bit_length() - 1
    device_pos = lax.axis_index("tm")
    phase_bin = reverse_bits(device_pos, levels)
    channel_count, length = signal.shape
    total_len = length * blocks
    inner_len = math.gcd(128, length // lax.axis_size("chan"))
    real_part = signal
    imag_part = jnp.zeros_like(signal)
    for bit_index in range(levels - 1, -1, -1):
        half_span = 1 << bit_index
        partner = from_partner(jnp.stack([real_part, imag_part]), "tm", bit_index)
        upper_half = device_pos // half_span % 2 == 1
        cosine, sine_part = twiddle(device_pos % half_span, 2 * half_span)
        diff_real = partner[0] - real_part
        diff_imag = partner[1] - imag_part
        new_real = jnp.where(
            upper_half, diff_real * cosine - diff_imag * sine_part, real_part + partner[0]
        )
        new_imag = jnp.where(
            upper_half, diff_real * sine_part + diff_imag * cosine, imag_part + partner[1]
        )
        real_part, imag_part = (new_real, new_imag)
    spec_real, spec_imag = forward_local(real_part, imag_part, phase_bin, total_len, inner_len)
    spread = lax.all_to_all(
        jnp.stack([spec_real, spec_imag]), "chan", split_axis=1, concat_axis=2, tiled=True
    )
    mixed_real, mixed_imag = mix_bins(spread, band, response, offsets)
    returned = lax.all_to_all(
        jnp.stack([mixed_real, mixed_imag]), "chan", split_axis=2, concat_axis=1, tiled=True
    )
    real_part, imag_part = inverse_local(returned[0], returned[1], phase_bin, total_len)
    for bit_index in range(levels):
        half_span = 1 << bit_index
        partner = from_partner(jnp.stack([real_part, imag_part]), "tm", bit_index)
        upper_half = device_pos // half_span % 2 == 1
        cosine, sine_part = twiddle(device_pos % half_span, 2 * half_span)
        sine_part = -sine_part
        base_real = jnp.where(upper_half, partner[0], real_part)
        base_imag = jnp.where(upper_half, partner[1], imag_part)
        scaled_real = jnp.where(upper_half, real_part, partner[0])
        scaled_imag = jnp.where(upper_half, imag_part, partner[1])
        prod_real = scaled_real * cosine - scaled_imag * sine_part
        prod_imag = scaled_real * sine_part + scaled_imag * cosine
        real_part = jnp.where(upper_half, base_real - prod_real, base_real + prod_real)
        imag_part = jnp.where(upper_half, base_imag - prod_imag, base_imag + prod_imag)
    smoothed = real_part / total_len
    return smoothed


TM, CHAN, ROWS, LANES, OUTER, BANDW, HALF = 4, 8, 8, 128, 64, 16, 8
DEVICES = TM * CHAN
TOTAL = OUTER * LANES


def split_hi_lo(value):
    hi = value.astype(jnp.bfloat16)
    return hi, (value - hi.astype(jnp.float32)).astype(jnp.bfloat16)


def product(value, table_hi, table_lo):
    hi, lo = split_hi_lo(value)
    rows = value.shape[0]
    both = jnp.dot(jnp.concatenate([hi, lo], axis=0), table_hi[...], preferred_element_type=jnp.float32)
    return both[:rows] + (both[rows:] + jnp.dot(hi, table_lo[...], preferred_element_type=jnp.float32))


def outer_table():
    n1 = np.arange(OUTER)
    table = np.zeros((OUTER, OUTER))
    for pair in range(DEVICES):
        angle = 2 * np.pi * (n1 * pair % OUTER) / OUTER
        table[2 * pair] = np.cos(angle)
        table[2 * pair + 1] = -np.sin(angle) if pair else (-1.0) ** n1
    return table


def rev(t):
    return (t % 2) * 2 + t // 2


def outer_product(table, value):
    hi, lo = split_hi_lo(value)
    return jnp.dot(table.astype(jnp.bfloat16), jnp.concatenate([hi, lo, hi], axis=0), preferred_element_type=jnp.float32)


def fused(signal, response_in, offsets_in, band_in, base_in, turn_in, table_in, out,
          response, offsets, band_rows, base, turn, table, resp, tall, band, xs, xin, ybuf, sbuf, rbuf, rt, xp, mv, mm, wh, wl, vh, vl,
          dbuf, yback, zbuf, wide, resp_wide, rsend, rrecv, send, recv, own, arrive):
    t, g = lax.axis_index("tm"), lax.axis_index("chan")
    d = CHAN // 2 * g + rev(t)
    e = TM * g + t
    line = g // 2
    lines = [(line + i) % 4 for i in range(4)]
    cores = [g - 2 * line, 1 - (g - 2 * line)]
    times = [(t + i) % TM for i in range(TM)]
    revs = [rev(i) for i in times]

    def remote(src, dst, k, target):
        return pltpu.make_async_remote_copy(
            src_ref=src, dst_ref=dst, send_sem=send.at[k], recv_sem=recv.at[k],
            device_id=target, device_id_type=pl.DeviceIdType.MESH)

    def local(src, dst, sem):
        return pltpu.make_async_copy(src, dst, sem)

    barrier = pltpu.get_barrier_semaphore()
    for hop in range(1, TM):
        pl.semaphore_signal(barrier, inc=1, device_id=((t + hop) % TM, g), device_id_type=pl.DeviceIdType.MESH)
    for hop in range(1, CHAN):
        pl.semaphore_signal(barrier, inc=1, device_id=(t, (g + hop) % CHAN), device_id_type=pl.DeviceIdType.MESH)
    copies = [local(src, dst, own.at[i]) for i, (src, dst) in enumerate((
        (response_in, response), (offsets_in, offsets), (band_in, band_rows), (base_in, base),
        (turn_in.at[d], turn), (table_in, table)))]
    for copy in copies:
        copy.start()
    pl.semaphore_wait(barrier, TM + CHAN - 2)

    for hop in (2, 1, 3):
        to = (t + hop) % TM
        remote(signal.at[pl.ds(ROWS * to, ROWS)], xin.at[t], 0, (to, g)).start()
    local(signal.at[pl.ds(ROWS * t, ROWS)], xin.at[t], recv.at[0]).start()

    copies[0].wait()
    copies[1].wait()
    centered = ((offsets[...] + HALF) % 256 - HALF).astype(jnp.float32)
    filler = jnp.zeros((LANES - 2 * BANDW - 8, 256), jnp.float32)
    tall[...] = jnp.concatenate([response[...], jnp.broadcast_to(centered, (8, 256)), filler], axis=0).T
    for s in range(16):
        resp[s] = tall[pl.ds(s, 16, stride=16), :]

    def send_resp(part, s, block, target):
        return pltpu.make_async_remote_copy(
            src_ref=resp.at[s], dst_ref=rbuf.at[part, pl.ds(16 * block, 16)], send_sem=rsend.at[part],
            recv_sem=rrecv.at[part], device_id=target, device_id_type=pl.DeviceIdType.MESH)

    t_b = jnp.where(t < 2, t, 5 - t)
    s_own = jnp.where(t == 0, (8 - g) % 8, 7 - g) + 8
    local(resp.at[g], rbuf.at[0, pl.ds(16 * g, 16)], rrecv.at[0]).start()
    for hop in range(1, CHAN):
        to = (g + hop) % CHAN
        send_resp(0, to, g, (t, to)).start()

    def send_b():
        for hop in range(1, CHAN):
            to = (g + hop) % CHAN
            send_resp(1, jnp.where(t == 0, (8 - to) % 8, 7 - to) + 8, g, (t_b, to)).start()

    @pl.when(t < 2)
    def _():
        send_b()
        local(resp.at[s_own], rbuf.at[1, pl.ds(16 * g, 16)], rrecv.at[1]).start()

    copies[2].wait()
    band[...] = jnp.concatenate([band_rows[...], jnp.zeros((LANES - 2 * BANDW, 256), jnp.float32)], axis=0).T

    for copy in copies[3:]:
        copy.wait()
    first = d == 0
    for part in range(2):
        tc, ts = turn[2 * part : 2 * part + 1, :], turn[2 * part + 1 : 2 * part + 2, :]
        bc, bs = base[0], base[1]
        tr = tc * bc - ts * bs
        ti = tc * bs + ts * bc
        zero = jnp.zeros_like(tr)
        if part == 0:
            blocks = ((tr, ti), (jnp.where(first, zero, -ti), jnp.where(first, zero, tr)))
        else:
            blocks = ((jnp.where(first, zero, tr), jnp.where(first, zero, ti)),
                      (jnp.where(first, tr, ti), jnp.where(first, ti, -tr)))
        for row in range(2):
            for col in range(2):
                inner = slice(LANES * row, LANES * (row + 1))
                outer = slice(LANES * (2 * part + col), LANES * (2 * part + col + 1))
                vh[outer, inner], vl[outer, inner] = split_hi_lo(blocks[row][col])
                wh[inner, outer], wl[inner, outer] = split_hi_lo(blocks[row][col].T)

    def spread(i, carry):
        rows = pl.ds(pl.multiple_of(8 * i, 8), 8)
        gains = band[rows, :]
        for j in range(2 * BANDW):
            wide[j, rows, :] = jnp.broadcast_to(gains[:, j : j + 1], (8, LANES))
        return carry

    lax.fori_loop(0, 32, spread, 0)

    local(xin, xin, recv.at[0]).wait()

    @pl.when(t >= 2)
    def _():
        send_b()
        pltpu.make_async_remote_copy(
            src_ref=resp.at[s_own], dst_ref=rbuf.at[1, pl.ds(16 * g, 16)], send_sem=rsend.at[2],
            recv_sem=rrecv.at[1], device_id=(5 - t, g), device_id_type=pl.DeviceIdType.MESH).start()

    for b in range(TM):
        for i in range(16):
            xs[pl.ds(ROWS * (16 * b + i), ROWS), :] = xin[b, :, LANES * i : LANES * (i + 1)]
    ycols = ybuf.reshape(DEVICES * 2 * ROWS, LANES)
    taken = jnp.concatenate([xs[pl.ds(c, OUTER, stride=ROWS), :] for c in range(ROWS)], axis=1)
    result = outer_product(table[0], taken)
    for c in range(ROWS):
        ycols[pl.ds(c, OUTER, stride=ROWS), :] = result[:, LANES * c : LANES * (c + 1)]

    local(ybuf.at[d], sbuf.at[e], arrive.at[line]).start()
    for back in range(4):
        for core in cores:
            to_g = 2 * lines[-back % 4] + core
            for hop in (2, 1, 3, 0):
                if back == 0 and core is cores[0] and hop == 0:
                    continue
                pltpu.make_async_remote_copy(
                    src_ref=ybuf.at[4 * to_g + revs[hop]], dst_ref=sbuf.at[e], send_sem=send.at[1],
                    recv_sem=arrive.at[line], device_id=(times[hop], to_g),
                    device_id_type=pl.DeviceIdType.MESH).start()

    for part in range(2):
        local(rbuf.at[part], rbuf.at[part], rrecv.at[part]).wait()
        rt[part] = rbuf[part].T
        for j in range(2 * BANDW + 1):
            resp_wide[part, j] = jnp.broadcast_to(rt[part, j : j + 1, :], (8, LANES))

    def ingest(i):
        q = (line + i) % 4
        eight = sbuf.at[pl.ds(8 * q, 8)]
        local(eight, eight, arrive.at[q]).wait()
        rows = jnp.concatenate([eight[:, 0].reshape(64, LANES), eight[:, 1].reshape(64, LANES)], axis=1)
        spec = product(rows, wh, wl)
        for part in range(2):
            for ri in range(2):
                at = LANES * (2 * part + ri)
                xp[part, ri, pl.ds(pl.multiple_of(64 * i, 64), 64), :] = spec[:, at : at + LANES]

    def shift(i, carry):
        at = 8 * i
        for part in range(2):
            off = resp_wide[part, 2 * BANDW]
            got = [jnp.zeros((8, LANES), jnp.float32)] * 2
            for o in range(-HALF, HALF + 1):
                hit = off == float(o)
                for ri in range(2):
                    got[ri] = jnp.where(hit, xp[part, ri, pl.ds(at + o, 8), :], got[ri])
            for ri in range(2):
                mv[part, ri, pl.ds(pl.multiple_of(at, 8), 8), :] = got[ri]
        return carry

    ingest(0)
    for part in range(2):
        for ri in range(2):
            xp[part, ri, 256:288] = xp[part, ri, 0:32]
    lax.fori_loop(1, 3, shift, 0, unroll=2)

    def chunk(step, carry):
        @pl.when(step < 3)
        def _():
            ingest(step + 1)

        lax.fori_loop(0, 8, lambda i, inner: shift(8 * step + 3 + i, inner), 0, unroll=4)

        def mix(i, inner):
            at = 64 * step + 8 + 8 * i
            gains = pl.ds(pl.multiple_of((64 * line + at) % 256, 8), 8)
            acc = [jnp.zeros((8, LANES), jnp.float32)] * 4
            for j in range(BANDW):
                br, bi = wide[j, gains, :], wide[BANDW + j, gains, :]
                for part in range(2):
                    rr, ri = resp_wide[part, j], resp_wide[part, BANDW + j]
                    cr = br * rr - bi * ri
                    ci = br * ri + bi * rr
                    xr = mv[part, 0, pl.ds(at + j, 8), :]
                    xi = mv[part, 1, pl.ds(at + j, 8), :]
                    acc[2 * part] = acc[2 * part] + (cr * xr - ci * xi)
                    acc[2 * part + 1] = acc[2 * part + 1] + (cr * xi + ci * xr)
            for q in range(4):
                mm[pl.ds(pl.multiple_of(8 * i, 8), 8), LANES * q : LANES * (q + 1)] = acc[q]
            return inner

        lax.fori_loop(0, 8, mix, 0, unroll=4)
        back = product(mm[...], vh, vl)
        for ri in range(2):
            dbuf[pl.ds(8 * step, 8), ri] = back[:, LANES * ri : LANES * (ri + 1)].reshape(8, 8, LANES)

        here, after = 2 * ((line + step) % 4), 2 * ((line + step + 1) % 4)
        for u in range(8):
            source = dbuf.at[8 * step + u]
            to_t, to_g = (1 + u) % 4, (here, here + 1, after)[(1 + u) // 4]
            own_block = (to_t == t) & (to_g == g)

            @pl.when(jnp.logical_not(own_block))
            def _():
                remote(source, yback.at[d], 2, (to_t, to_g)).start()

            @pl.when(own_block)
            def _():
                local(source, yback.at[d], recv.at[2]).start()

        return carry

    lax.fori_loop(0, 4, chunk, 0)

    local(yback, yback, recv.at[2]).wait()
    bcols = yback.reshape(DEVICES * 2 * ROWS, LANES)
    taken = jnp.concatenate([bcols[pl.ds(c, OUTER, stride=ROWS), :] for c in range(ROWS)], axis=1)
    result = outer_product(table[1], taken)
    for c in range(ROWS):
        xs[pl.ds(c, OUTER, stride=ROWS), :] = result[:, LANES * c : LANES * (c + 1)]
    for b in range(TM):
        for i in range(16):
            zbuf[b, :, LANES * i : LANES * (i + 1)] = xs[pl.ds(ROWS * (16 * b + i), ROWS), :]
    for hop in (2, 1, 3):
        to = (t + hop) % TM
        remote(zbuf.at[to], out.at[pl.ds(ROWS * t, ROWS)], 3, (to, g)).start()
    local(zbuf.at[t], out.at[pl.ds(ROWS * t, ROWS)], recv.at[3]).start()
    local(out, out, recv.at[3]).wait()

    for k in (0, 3):
        local(signal.at[pl.ds(0, 24)], signal.at[pl.ds(0, 24)], send.at[k]).wait()
    for k in (1, 2):
        local(ybuf.at[pl.ds(0, 31)], ybuf.at[pl.ds(0, 31)], send.at[k]).wait()
    for part in range(2):
        local(resp.at[pl.ds(0, 7)], resp.at[pl.ds(0, 7)], rsend.at[part]).wait()

    @pl.when(t >= 2)
    def _():
        local(resp.at[0], resp.at[0], rsend.at[2]).wait()


def per_device_fused(signal, band, response, offsets):
    n2 = np.arange(LANES)
    angle = -2 * np.pi * (n2[:, None] * n2[None, :] % LANES) / LANES
    base = jnp.asarray(np.stack([np.cos(angle), np.sin(angle)]).astype(np.float32))
    pairs = np.arange(DEVICES)[:, None]
    other = np.where(pairs == 0, DEVICES, OUTER - pairs)
    turns = [-2 * np.pi * (n2[None, :] * k1 % TOTAL) / TOTAL for k1 in (pairs, other)]
    rows = [np.cos(turns[0]), np.sin(turns[0]), np.cos(turns[1]), np.sin(turns[1])]
    turn = jnp.asarray(np.stack(rows * 2, axis=1).astype(np.float32))
    forward = outer_table()
    tables = []
    for matrix in (forward, forward.T / TOTAL):
        matrix = matrix.astype(np.float32)
        hi = matrix.astype(jnp.bfloat16)
        lo = (matrix - hi.astype(np.float32)).astype(jnp.bfloat16)
        tables.append(np.concatenate([hi, hi, lo], axis=1).astype(np.float32))
    table = jnp.asarray(np.stack(tables))

    f32 = jnp.float32
    hbm = pl.BlockSpec(memory_space=pl.ANY)
    out = pl.pallas_call(
        fused,
        out_shape=jax.ShapeDtypeStruct((32, 16 * LANES), f32),
        in_specs=[hbm] * 7,
        out_specs=hbm,
        scratch_shapes=[
            pltpu.VMEM((2 * BANDW, 256), f32),
            pltpu.VMEM((1, 256), jnp.int32),
            pltpu.VMEM((2 * BANDW, 256), f32),
            pltpu.VMEM((2, LANES, LANES), f32),
            pltpu.VMEM((8, LANES), f32),
            pltpu.VMEM((2, OUTER, 3 * OUTER), f32),
            pltpu.VMEM((16, 16, LANES), f32),
            pltpu.VMEM((2 * LANES, LANES), f32),
            pltpu.VMEM((2 * LANES, LANES), f32),
            pltpu.VMEM((OUTER * ROWS, LANES), f32),
            pltpu.VMEM((TM, ROWS, 16 * LANES), f32),
            pltpu.VMEM((DEVICES, 2, ROWS, LANES), f32),
            pltpu.VMEM((DEVICES, 2, ROWS, LANES), f32),
            pltpu.VMEM((2, LANES, LANES), f32),
            pltpu.VMEM((2, LANES, LANES), f32),
            pltpu.VMEM((2, 2, 288, LANES), f32),
            pltpu.VMEM((2, 2, 280, LANES), f32),
            pltpu.VMEM((64, 4 * LANES), f32),
            pltpu.VMEM((2 * LANES, 4 * LANES), jnp.bfloat16),
            pltpu.VMEM((2 * LANES, 4 * LANES), jnp.bfloat16),
            pltpu.VMEM((4 * LANES, 2 * LANES), jnp.bfloat16),
            pltpu.VMEM((4 * LANES, 2 * LANES), jnp.bfloat16),
            pltpu.VMEM((DEVICES, 2, ROWS, LANES), f32),
            pltpu.VMEM((DEVICES, 2, ROWS, LANES), f32),
            pltpu.VMEM((TM, ROWS, 16 * LANES), f32),
            pltpu.VMEM((2 * BANDW, 256, LANES), f32),
            pltpu.VMEM((2, 2 * BANDW + 1, 8, LANES), f32),
            pltpu.SemaphoreType.DMA((3,)),
            pltpu.SemaphoreType.DMA((2,)),
            pltpu.SemaphoreType.DMA((4,)),
            pltpu.SemaphoreType.DMA((4,)),
            pltpu.SemaphoreType.DMA((6,)),
            pltpu.SemaphoreType.DMA((4,)),
        ],
        compiler_params=pltpu.CompilerParams(collective_id=0, has_side_effects=True, vmem_limit_bytes=40 << 20),
    )(*(pltpu.with_memory_space_constraint(x, pltpu.HBM) for x in (
        signal, response.reshape(2 * BANDW, 256), offsets, band.reshape(2 * BANDW, 256), base, turn, table)))
    return out


def solution(mesh):
    sizes = dict(mesh.shape)
    tuned = sizes["tm"] == TM and sizes["chan"] == CHAN
    in_specs = (P("chan", "tm"), P(), P(None, "tm", None, "chan"), P("tm", "chan"))
    out_specs = P("chan", "tm")
    return jax.shard_map(
        per_device_fused if tuned else per_device, mesh=mesh, in_specs=in_specs, out_specs=out_specs, check_vma=False
    )
```

```python
import math

import jax
import jax.numpy as jnp
import numpy as np
from jax import lax
from jax.experimental import pallas as pl
from jax.experimental.pallas import tpu as pltpu
from jax.sharding import PartitionSpec as P

PRECISE = lax.Precision.HIGHEST


def from_partner(block, axis, stride):
    count = lax.axis_size(axis)
    route = []
    for low in range(count):
        high = low | 1 << stride
        if high != low and high < count:
            route += [(low, high), (high, low)]
    return lax.ppermute(block, axis, route)


def twiddle(numer, length):
    angle = -2.0 * math.pi / length * numer.astype(jnp.float32)
    return (jnp.cos(angle), jnp.sin(angle))


def dft_table(length):
    steps = lax.iota(jnp.int32, length)
    return twiddle(steps[:, None] * steps[None, :] % length, length)


def reverse_bits(value, bit_count):
    result = value * 0
    for bit_index in range(bit_count):
        result = result + value // (1 << bit_index) % 2 * (1 << bit_count - 1 - bit_index)
    return result


def complex_einsum(form, left_real, left_imag, right_real, right_imag):
    out_real = jnp.einsum(form, left_real, right_real, precision=PRECISE) - jnp.einsum(
        form, left_imag, right_imag, precision=PRECISE
    )
    out_imag = jnp.einsum(form, left_real, right_imag, precision=PRECISE) + jnp.einsum(
        form, left_imag, right_real, precision=PRECISE
    )
    return (out_real, out_imag)


def forward_local(real_part, imag_part, phase_bin, total_len, inner_len):
    channel_count, length = real_part.shape
    outer_len = length // inner_len
    sample_pos = lax.iota(jnp.int32, length)
    cosine, sine_part = twiddle(sample_pos * phase_bin % total_len, total_len)
    real_part, imag_part = (
        real_part * cosine - imag_part * sine_part,
        real_part * sine_part + imag_part * cosine,
    )
    real_part = real_part.reshape(channel_count, inner_len, outer_len)
    imag_part = imag_part.reshape(channel_count, inner_len, outer_len)
    table_real, table_imag = dft_table(inner_len)
    real_part, imag_part = complex_einsum(
        "cab,ak->cbk", real_part, imag_part, table_real, table_imag
    )
    outer_ids = lax.iota(jnp.int32, outer_len)[:, None]
    inner_ids = lax.iota(jnp.int32, inner_len)[None, :]
    cosine, sine_part = twiddle(outer_ids * inner_ids, length)
    real_part, imag_part = (
        real_part * cosine - imag_part * sine_part,
        real_part * sine_part + imag_part * cosine,
    )
    table_real, table_imag = dft_table(outer_len)
    return complex_einsum("cbk,bm->mck", real_part, imag_part, table_real, table_imag)


def inverse_local(spec_real, spec_imag, phase_bin, total_len):
    outer_len, channel_count, inner_len = spec_real.shape
    length = outer_len * inner_len
    table_real, table_imag = dft_table(outer_len)
    real_part, imag_part = complex_einsum(
        "mck,mb->cbk", spec_real, spec_imag, table_real, -table_imag
    )
    outer_ids = lax.iota(jnp.int32, outer_len)[:, None]
    inner_ids = lax.iota(jnp.int32, inner_len)[None, :]
    cosine, sine_part = twiddle(outer_ids * inner_ids, length)
    sine_part = -sine_part
    real_part, imag_part = (
        real_part * cosine - imag_part * sine_part,
        real_part * sine_part + imag_part * cosine,
    )
    table_real, table_imag = dft_table(inner_len)
    real_part, imag_part = complex_einsum(
        "cbk,ka->cab", real_part, imag_part, table_real, -table_imag
    )
    real_part = real_part.reshape(channel_count, length)
    imag_part = imag_part.reshape(channel_count, length)
    sample_pos = lax.iota(jnp.int32, length)
    cosine, sine_part = twiddle(sample_pos * phase_bin % total_len, total_len)
    sine_part = -sine_part
    return (real_part * cosine - imag_part * sine_part, real_part * sine_part + imag_part * cosine)


def mix_bins(spread, band, response, offsets):
    fine_len, channel_all, inner_len = (spread.shape[1], spread.shape[2], spread.shape[3])
    band_width = band.shape[1]
    half_width = band_width // 2
    shift_cols = offsets.reshape(1, fine_len, 1, inner_len)
    centered = (shift_cols + half_width) % channel_all - half_width
    moved = jnp.zeros_like(spread)
    for shift_amount in range(-half_width, half_width + 1):
        rolled = jnp.roll(spread, -shift_amount, axis=2)
        moved = jnp.where(centered == shift_amount, rolled, moved)
    moved_real = moved[0]
    moved_imag = moved[1]
    wide_real = jnp.concatenate([moved_real, moved_real[:, : band_width - 1]], axis=1)
    wide_imag = jnp.concatenate([moved_imag, moved_imag[:, : band_width - 1]], axis=1)
    responses = response.reshape(2, band_width, fine_len, 1, inner_len)
    acc_real = jnp.zeros_like(moved_real)
    acc_imag = jnp.zeros_like(moved_imag)
    for lag_index in range(band_width):
        value_real = wide_real[:, lag_index : lag_index + channel_all]
        value_imag = wide_imag[:, lag_index : lag_index + channel_all]
        gain_real = band[0, lag_index][None, :, None]
        gain_imag = band[1, lag_index][None, :, None]
        coef_real = gain_real * responses[0, lag_index] - gain_imag * responses[1, lag_index]
        coef_imag = gain_real * responses[1, lag_index] + gain_imag * responses[0, lag_index]
        acc_real = acc_real + coef_real * value_real - coef_imag * value_imag
        acc_imag = acc_imag + coef_real * value_imag + coef_imag * value_real
    return (acc_real, acc_imag)


def per_device(signal, band, response, offsets):
    blocks = lax.axis_size("tm")
    levels = blocks.bit_length() - 1
    device_pos = lax.axis_index("tm")
    phase_bin = reverse_bits(device_pos, levels)
    channel_count, length = signal.shape
    total_len = length * blocks
    inner_len = math.gcd(128, length // lax.axis_size("chan"))
    real_part = signal
    imag_part = jnp.zeros_like(signal)
    for bit_index in range(levels - 1, -1, -1):
        half_span = 1 << bit_index
        partner = from_partner(jnp.stack([real_part, imag_part]), "tm", bit_index)
        upper_half = device_pos // half_span % 2 == 1
        cosine, sine_part = twiddle(device_pos % half_span, 2 * half_span)
        diff_real = partner[0] - real_part
        diff_imag = partner[1] - imag_part
        new_real = jnp.where(
            upper_half, diff_real * cosine - diff_imag * sine_part, real_part + partner[0]
        )
        new_imag = jnp.where(
            upper_half, diff_real * sine_part + diff_imag * cosine, imag_part + partner[1]
        )
        real_part, imag_part = (new_real, new_imag)
    spec_real, spec_imag = forward_local(real_part, imag_part, phase_bin, total_len, inner_len)
    spread = lax.all_to_all(
        jnp.stack([spec_real, spec_imag]), "chan", split_axis=1, concat_axis=2, tiled=True
    )
    mixed_real, mixed_imag = mix_bins(spread, band, response, offsets)
    returned = lax.all_to_all(
        jnp.stack([mixed_real, mixed_imag]), "chan", split_axis=2, concat_axis=1, tiled=True
    )
    real_part, imag_part = inverse_local(returned[0], returned[1], phase_bin, total_len)
    for bit_index in range(levels):
        half_span = 1 << bit_index
        partner = from_partner(jnp.stack([real_part, imag_part]), "tm", bit_index)
        upper_half = device_pos // half_span % 2 == 1
        cosine, sine_part = twiddle(device_pos % half_span, 2 * half_span)
        sine_part = -sine_part
        base_real = jnp.where(upper_half, partner[0], real_part)
        base_imag = jnp.where(upper_half, partner[1], imag_part)
        scaled_real = jnp.where(upper_half, real_part, partner[0])
        scaled_imag = jnp.where(upper_half, imag_part, partner[1])
        prod_real = scaled_real * cosine - scaled_imag * sine_part
        prod_imag = scaled_real * sine_part + scaled_imag * cosine
        real_part = jnp.where(upper_half, base_real - prod_real, base_real + prod_real)
        imag_part = jnp.where(upper_half, base_imag - prod_imag, base_imag + prod_imag)
    smoothed = real_part / total_len
    return smoothed


TM, CHAN, ROWS, LANES, OUTER, BANDW, HALF = 4, 8, 8, 128, 64, 16, 8
DEVICES = TM * CHAN
TOTAL = OUTER * LANES


def split_hi_lo(value):
    hi = value.astype(jnp.bfloat16)
    return hi, (value - hi.astype(jnp.float32)).astype(jnp.bfloat16)


def product(value, table_hi, table_lo):
    hi, lo = split_hi_lo(value)
    rows = value.shape[0]
    both = jnp.dot(jnp.concatenate([hi, lo], axis=0), table_hi[...], preferred_element_type=jnp.float32)
    return both[:rows] + (both[rows:] + jnp.dot(hi, table_lo[...], preferred_element_type=jnp.float32))


def outer_table():
    n1 = np.arange(OUTER)
    table = np.zeros((OUTER, OUTER))
    for pair in range(DEVICES):
        angle = 2 * np.pi * (n1 * pair % OUTER) / OUTER
        table[2 * pair] = np.cos(angle)
        table[2 * pair + 1] = -np.sin(angle) if pair else (-1.0) ** n1
    return table


def rev(t):
    return (t % 2) * 2 + t // 2


def outer_product(table, value):
    hi, lo = split_hi_lo(value)
    return jnp.dot(table.astype(jnp.bfloat16), jnp.concatenate([hi, lo, hi], axis=0), preferred_element_type=jnp.float32)


def fused(signal, response_in, offsets_in, band_in, base_in, turn_in, table_in, out,
          response, offsets, band_rows, base, turn, table, resp, tall, band, xs, xin, ybuf, sbuf, rbuf, rt, xp, mv, mm, wh, wl, vh, vl,
          dbuf, yback, zbuf, wide, resp_wide, rsend, rrecv, send, recv, own, arrive):
    t, g = lax.axis_index("tm"), lax.axis_index("chan")
    d = CHAN // 2 * g + rev(t)
    e = TM * g + t
    line = g // 2
    lines = [(line + i) % 4 for i in range(4)]
    cores = [g - 2 * line, 1 - (g - 2 * line)]
    times = [(t + i) % TM for i in range(TM)]
    revs = [rev(i) for i in times]

    def remote(src, dst, k, target):
        return pltpu.make_async_remote_copy(
            src_ref=src, dst_ref=dst, send_sem=send.at[k], recv_sem=recv.at[k],
            device_id=target, device_id_type=pl.DeviceIdType.MESH)

    def local(src, dst, sem):
        return pltpu.make_async_copy(src, dst, sem)

    barrier = pltpu.get_barrier_semaphore()
    for hop in range(1, TM):
        pl.semaphore_signal(barrier, inc=1, device_id=((t + hop) % TM, g), device_id_type=pl.DeviceIdType.MESH)
    for hop in range(1, CHAN):
        pl.semaphore_signal(barrier, inc=1, device_id=(t, (g + hop) % CHAN), device_id_type=pl.DeviceIdType.MESH)
    copies = [local(src, dst, own.at[i]) for i, (src, dst) in enumerate((
        (response_in, response), (offsets_in, offsets), (band_in, band_rows), (base_in, base),
        (turn_in.at[d], turn), (table_in, table)))]
    for copy in copies:
        copy.start()
    pl.semaphore_wait(barrier, TM + CHAN - 2)

    for part in (slice(0, 1024), slice(1024, 2048)):
        for hop in (2, 1, 3):
            to = times[hop]
            remote(signal.at[pl.ds(ROWS * to, ROWS), part], xin.at[t, :, part], 0, (to, g)).start()
    local(signal.at[pl.ds(ROWS * t, ROWS)], xin.at[t], recv.at[0]).start()

    copies[0].wait()
    copies[1].wait()
    centered = ((offsets[...] + HALF) % 256 - HALF).astype(jnp.float32)
    filler = jnp.zeros((LANES - 2 * BANDW - 8, 256), jnp.float32)
    tall[...] = jnp.concatenate([response[...], jnp.broadcast_to(centered, (8, 256)), filler], axis=0).T
    for s in range(16):
        resp[s] = tall[pl.ds(s, 16, stride=16), :]

    def send_resp(part, s, block, target):
        return pltpu.make_async_remote_copy(
            src_ref=resp.at[s], dst_ref=rbuf.at[part, pl.ds(16 * block, 16)], send_sem=rsend.at[part],
            recv_sem=rrecv.at[part], device_id=target, device_id_type=pl.DeviceIdType.MESH)

    t_b = jnp.where(t < 2, t, 5 - t)
    s_own = jnp.where(t == 0, (8 - g) % 8, 7 - g) + 8
    local(resp.at[g], rbuf.at[0, pl.ds(16 * g, 16)], rrecv.at[0]).start()
    for hop in range(1, CHAN):
        to = (g + hop) % CHAN
        send_resp(0, to, g, (t, to)).start()

    def send_b():
        for hop in range(1, CHAN):
            to = (g + hop) % CHAN
            send_resp(1, jnp.where(t == 0, (8 - to) % 8, 7 - to) + 8, g, (t_b, to)).start()

    @pl.when(t < 2)
    def _():
        send_b()
        local(resp.at[s_own], rbuf.at[1, pl.ds(16 * g, 16)], rrecv.at[1]).start()

    copies[2].wait()
    band[...] = jnp.concatenate([band_rows[...], jnp.zeros((LANES - 2 * BANDW, 256), jnp.float32)], axis=0).T

    for copy in copies[3:]:
        copy.wait()
    first = d == 0
    for part in range(2):
        tc, ts = turn[2 * part : 2 * part + 1, :], turn[2 * part + 1 : 2 * part + 2, :]
        bc, bs = base[0], base[1]
        tr = tc * bc - ts * bs
        ti = tc * bs + ts * bc
        zero = jnp.zeros_like(tr)
        if part == 0:
            blocks = ((tr, ti), (jnp.where(first, zero, -ti), jnp.where(first, zero, tr)))
        else:
            blocks = ((jnp.where(first, zero, tr), jnp.where(first, zero, ti)),
                      (jnp.where(first, tr, ti), jnp.where(first, ti, -tr)))
        for row in range(2):
            for col in range(2):
                inner = slice(LANES * row, LANES * (row + 1))
                outer = slice(LANES * (2 * part + col), LANES * (2 * part + col + 1))
                vh[outer, inner], vl[outer, inner] = split_hi_lo(blocks[row][col])
                wh[inner, outer], wl[inner, outer] = split_hi_lo(blocks[row][col].T)

    local(xin, xin, recv.at[0]).wait()

    for b in range(TM):
        for i in range(16):
            xs[pl.ds(ROWS * (16 * b + i), ROWS), :] = xin[b, :, LANES * i : LANES * (i + 1)]
    ycols = ybuf.reshape(DEVICES * 2 * ROWS, LANES)
    taken = jnp.concatenate([xs[pl.ds(c, OUTER, stride=ROWS), :] for c in range(ROWS)], axis=1)
    result = outer_product(table[0], taken)
    for c in range(ROWS):
        ycols[pl.ds(c, OUTER, stride=ROWS), :] = result[:, LANES * c : LANES * (c + 1)]

    local(ybuf.at[d], sbuf.at[e], arrive.at[line]).start()
    for back in range(4):
        for core in cores:
            to_g = 2 * lines[-back % 4] + core
            for hop in (2, 1, 3, 0):
                if back == 0 and core is cores[0] and hop == 0:
                    continue
                pltpu.make_async_remote_copy(
                    src_ref=ybuf.at[4 * to_g + revs[hop]], dst_ref=sbuf.at[e], send_sem=send.at[1],
                    recv_sem=arrive.at[line], device_id=(times[hop], to_g),
                    device_id_type=pl.DeviceIdType.MESH).start()

    @pl.when(t >= 2)
    def _():
        send_b()
        pltpu.make_async_remote_copy(
            src_ref=resp.at[s_own], dst_ref=rbuf.at[1, pl.ds(16 * g, 16)], send_sem=rsend.at[2],
            recv_sem=rrecv.at[1], device_id=(5 - t, g), device_id_type=pl.DeviceIdType.MESH).start()

    def spread(i, carry):
        rows = pl.ds(pl.multiple_of(8 * i, 8), 8)
        gains = band[rows, :]
        for j in range(2 * BANDW):
            wide[j, rows, :] = jnp.broadcast_to(gains[:, j : j + 1], (8, LANES))
        return carry

    lax.fori_loop(0, 32, spread, 0)

    for part in range(2):
        local(rbuf.at[part], rbuf.at[part], rrecv.at[part]).wait()
        rt[part] = rbuf[part].T
        for j in range(2 * BANDW + 1):
            resp_wide[part, j] = jnp.broadcast_to(rt[part, j : j + 1, :], (8, LANES))

    def ingest(i):
        q = (line + i) % 4
        eight = sbuf.at[pl.ds(8 * q, 8)]
        local(eight, eight, arrive.at[q]).wait()
        rows = jnp.concatenate([eight[:, 0].reshape(64, LANES), eight[:, 1].reshape(64, LANES)], axis=1)
        spec = product(rows, wh, wl)
        for part in range(2):
            for ri in range(2):
                at = LANES * (2 * part + ri)
                xp[part, ri, pl.ds(pl.multiple_of(64 * i, 64), 64), :] = spec[:, at : at + LANES]

    def shift(i, carry):
        at = 8 * i
        for part in range(2):
            off = resp_wide[part, 2 * BANDW]
            got = [jnp.zeros((8, LANES), jnp.float32)] * 2
            for o in range(-HALF, HALF + 1):
                hit = off == float(o)
                for ri in range(2):
                    got[ri] = jnp.where(hit, xp[part, ri, pl.ds(at + o, 8), :], got[ri])
            for ri in range(2):
                mv[part, ri, pl.ds(pl.multiple_of(at, 8), 8), :] = got[ri]
        return carry

    ingest(0)
    for part in range(2):
        for ri in range(2):
            xp[part, ri, 256:288] = xp[part, ri, 0:32]
    lax.fori_loop(1, 3, shift, 0, unroll=2)

    def chunk(step, carry):
        @pl.when(step < 3)
        def _():
            ingest(step + 1)

        lax.fori_loop(0, 8, lambda i, inner: shift(8 * step + 3 + i, inner), 0, unroll=4)

        def mix(i, inner):
            at = 64 * step + 8 + 8 * i
            gains = pl.ds(pl.multiple_of((64 * line + at) % 256, 8), 8)
            acc = [jnp.zeros((8, LANES), jnp.float32)] * 4
            for j in range(BANDW):
                br, bi = wide[j, gains, :], wide[BANDW + j, gains, :]
                for part in range(2):
                    rr, ri = resp_wide[part, j], resp_wide[part, BANDW + j]
                    cr = br * rr - bi * ri
                    ci = br * ri + bi * rr
                    xr = mv[part, 0, pl.ds(at + j, 8), :]
                    xi = mv[part, 1, pl.ds(at + j, 8), :]
                    acc[2 * part] = acc[2 * part] + (cr * xr - ci * xi)
                    acc[2 * part + 1] = acc[2 * part + 1] + (cr * xi + ci * xr)
            for q in range(4):
                mm[pl.ds(pl.multiple_of(8 * i, 8), 8), LANES * q : LANES * (q + 1)] = acc[q]
            return inner

        lax.fori_loop(0, 8, mix, 0, unroll=4)
        back = product(mm[...], vh, vl)
        for ri in range(2):
            dbuf[pl.ds(8 * step, 8), ri] = back[:, LANES * ri : LANES * (ri + 1)].reshape(8, 8, LANES)

        here, after = 2 * ((line + step) % 4), 2 * ((line + step + 1) % 4)
        for u in range(8):
            source = dbuf.at[8 * step + u]
            to_t, to_g = (1 + u) % 4, (here, here + 1, after)[(1 + u) // 4]
            own_block = (to_t == t) & (to_g == g)

            @pl.when(jnp.logical_not(own_block))
            def _():
                remote(source, yback.at[d], 2, (to_t, to_g)).start()

            @pl.when(own_block)
            def _():
                local(source, yback.at[d], recv.at[2]).start()

        return carry

    lax.fori_loop(0, 4, chunk, 0)

    local(yback, yback, recv.at[2]).wait()
    bcols = yback.reshape(DEVICES * 2 * ROWS, LANES)
    taken = jnp.concatenate([bcols[pl.ds(c, OUTER, stride=ROWS), :] for c in range(ROWS)], axis=1)
    result = outer_product(table[1], taken)
    for c in range(ROWS):
        xs[pl.ds(c, OUTER, stride=ROWS), :] = result[:, LANES * c : LANES * (c + 1)]
    for b in range(TM):
        for i in range(16):
            zbuf[b, :, LANES * i : LANES * (i + 1)] = xs[pl.ds(ROWS * (16 * b + i), ROWS), :]
    for part in (slice(0, 1024), slice(1024, 2048)):
        for hop in (2, 1, 3):
            to = times[hop]
            remote(zbuf.at[to, :, part], out.at[pl.ds(ROWS * t, ROWS), part], 3, (to, g)).start()
    local(zbuf.at[t], out.at[pl.ds(ROWS * t, ROWS)], recv.at[3]).start()
    local(out, out, recv.at[3]).wait()

    for k in (0, 3):
        local(signal.at[pl.ds(0, 24)], signal.at[pl.ds(0, 24)], send.at[k]).wait()
    for k in (1, 2):
        local(ybuf.at[pl.ds(0, 31)], ybuf.at[pl.ds(0, 31)], send.at[k]).wait()
    for part in range(2):
        local(resp.at[pl.ds(0, 7)], resp.at[pl.ds(0, 7)], rsend.at[part]).wait()

    @pl.when(t >= 2)
    def _():
        local(resp.at[0], resp.at[0], rsend.at[2]).wait()


def per_device_fused(signal, band, response, offsets):
    n2 = np.arange(LANES)
    angle = -2 * np.pi * (n2[:, None] * n2[None, :] % LANES) / LANES
    base = jnp.asarray(np.stack([np.cos(angle), np.sin(angle)]).astype(np.float32))
    pairs = np.arange(DEVICES)[:, None]
    other = np.where(pairs == 0, DEVICES, OUTER - pairs)
    turns = [-2 * np.pi * (n2[None, :] * k1 % TOTAL) / TOTAL for k1 in (pairs, other)]
    rows = [np.cos(turns[0]), np.sin(turns[0]), np.cos(turns[1]), np.sin(turns[1])]
    turn = jnp.asarray(np.stack(rows * 2, axis=1).astype(np.float32))
    forward = outer_table()
    tables = []
    for matrix in (forward, forward.T / TOTAL):
        matrix = matrix.astype(np.float32)
        hi = matrix.astype(jnp.bfloat16)
        lo = (matrix - hi.astype(np.float32)).astype(jnp.bfloat16)
        tables.append(np.concatenate([hi, hi, lo], axis=1).astype(np.float32))
    table = jnp.asarray(np.stack(tables))

    f32 = jnp.float32
    hbm = pl.BlockSpec(memory_space=pl.ANY)
    out = pl.pallas_call(
        fused,
        out_shape=jax.ShapeDtypeStruct((32, 16 * LANES), f32),
        in_specs=[hbm] * 7,
        out_specs=hbm,
        scratch_shapes=[
            pltpu.VMEM((2 * BANDW, 256), f32),
            pltpu.VMEM((1, 256), jnp.int32),
            pltpu.VMEM((2 * BANDW, 256), f32),
            pltpu.VMEM((2, LANES, LANES), f32),
            pltpu.VMEM((8, LANES), f32),
            pltpu.VMEM((2, OUTER, 3 * OUTER), f32),
            pltpu.VMEM((16, 16, LANES), f32),
            pltpu.VMEM((2 * LANES, LANES), f32),
            pltpu.VMEM((2 * LANES, LANES), f32),
            pltpu.VMEM((OUTER * ROWS, LANES), f32),
            pltpu.VMEM((TM, ROWS, 16 * LANES), f32),
            pltpu.VMEM((DEVICES, 2, ROWS, LANES), f32),
            pltpu.VMEM((DEVICES, 2, ROWS, LANES), f32),
            pltpu.VMEM((2, LANES, LANES), f32),
            pltpu.VMEM((2, LANES, LANES), f32),
            pltpu.VMEM((2, 2, 288, LANES), f32),
            pltpu.VMEM((2, 2, 280, LANES), f32),
            pltpu.VMEM((64, 4 * LANES), f32),
            pltpu.VMEM((2 * LANES, 4 * LANES), jnp.bfloat16),
            pltpu.VMEM((2 * LANES, 4 * LANES), jnp.bfloat16),
            pltpu.VMEM((4 * LANES, 2 * LANES), jnp.bfloat16),
            pltpu.VMEM((4 * LANES, 2 * LANES), jnp.bfloat16),
            pltpu.VMEM((DEVICES, 2, ROWS, LANES), f32),
            pltpu.VMEM((DEVICES, 2, ROWS, LANES), f32),
            pltpu.VMEM((TM, ROWS, 16 * LANES), f32),
            pltpu.VMEM((2 * BANDW, 256, LANES), f32),
            pltpu.VMEM((2, 2 * BANDW + 1, 8, LANES), f32),
            pltpu.SemaphoreType.DMA((3,)),
            pltpu.SemaphoreType.DMA((2,)),
            pltpu.SemaphoreType.DMA((4,)),
            pltpu.SemaphoreType.DMA((4,)),
            pltpu.SemaphoreType.DMA((6,)),
            pltpu.SemaphoreType.DMA((4,)),
        ],
        compiler_params=pltpu.CompilerParams(collective_id=0, has_side_effects=True, vmem_limit_bytes=40 << 20),
    )(*(pltpu.with_memory_space_constraint(x, pltpu.HBM) for x in (
        signal, response.reshape(2 * BANDW, 256), offsets, band.reshape(2 * BANDW, 256), base, turn, table)))
    return out


def solution(mesh):
    sizes = dict(mesh.shape)
    tuned = sizes["tm"] == TM and sizes["chan"] == CHAN
    in_specs = (P("chan", "tm"), P(), P(None, "tm", None, "chan"), P("tm", "chan"))
    out_specs = P("chan", "tm")
    return jax.shard_map(
        per_device_fused if tuned else per_device, mesh=mesh, in_specs=in_specs, out_specs=out_specs, check_vma=False
    )
```

```python
import math

import jax
import jax.numpy as jnp
import numpy as np
from jax import lax
from jax.experimental import pallas as pl
from jax.experimental.pallas import tpu as pltpu
from jax.sharding import PartitionSpec as P

PRECISE = lax.Precision.HIGHEST


def from_partner(block, axis, stride):
    count = lax.axis_size(axis)
    route = []
    for low in range(count):
        high = low | 1 << stride
        if high != low and high < count:
            route += [(low, high), (high, low)]
    return lax.ppermute(block, axis, route)


def twiddle(numer, length):
    angle = -2.0 * math.pi / length * numer.astype(jnp.float32)
    return (jnp.cos(angle), jnp.sin(angle))


def dft_table(length):
    steps = lax.iota(jnp.int32, length)
    return twiddle(steps[:, None] * steps[None, :] % length, length)


def reverse_bits(value, bit_count):
    result = value * 0
    for bit_index in range(bit_count):
        result = result + value // (1 << bit_index) % 2 * (1 << bit_count - 1 - bit_index)
    return result


def complex_einsum(form, left_real, left_imag, right_real, right_imag):
    out_real = jnp.einsum(form, left_real, right_real, precision=PRECISE) - jnp.einsum(
        form, left_imag, right_imag, precision=PRECISE
    )
    out_imag = jnp.einsum(form, left_real, right_imag, precision=PRECISE) + jnp.einsum(
        form, left_imag, right_real, precision=PRECISE
    )
    return (out_real, out_imag)


def forward_local(real_part, imag_part, phase_bin, total_len, inner_len):
    channel_count, length = real_part.shape
    outer_len = length // inner_len
    sample_pos = lax.iota(jnp.int32, length)
    cosine, sine_part = twiddle(sample_pos * phase_bin % total_len, total_len)
    real_part, imag_part = (
        real_part * cosine - imag_part * sine_part,
        real_part * sine_part + imag_part * cosine,
    )
    real_part = real_part.reshape(channel_count, inner_len, outer_len)
    imag_part = imag_part.reshape(channel_count, inner_len, outer_len)
    table_real, table_imag = dft_table(inner_len)
    real_part, imag_part = complex_einsum(
        "cab,ak->cbk", real_part, imag_part, table_real, table_imag
    )
    outer_ids = lax.iota(jnp.int32, outer_len)[:, None]
    inner_ids = lax.iota(jnp.int32, inner_len)[None, :]
    cosine, sine_part = twiddle(outer_ids * inner_ids, length)
    real_part, imag_part = (
        real_part * cosine - imag_part * sine_part,
        real_part * sine_part + imag_part * cosine,
    )
    table_real, table_imag = dft_table(outer_len)
    return complex_einsum("cbk,bm->mck", real_part, imag_part, table_real, table_imag)


def inverse_local(spec_real, spec_imag, phase_bin, total_len):
    outer_len, channel_count, inner_len = spec_real.shape
    length = outer_len * inner_len
    table_real, table_imag = dft_table(outer_len)
    real_part, imag_part = complex_einsum(
        "mck,mb->cbk", spec_real, spec_imag, table_real, -table_imag
    )
    outer_ids = lax.iota(jnp.int32, outer_len)[:, None]
    inner_ids = lax.iota(jnp.int32, inner_len)[None, :]
    cosine, sine_part = twiddle(outer_ids * inner_ids, length)
    sine_part = -sine_part
    real_part, imag_part = (
        real_part * cosine - imag_part * sine_part,
        real_part * sine_part + imag_part * cosine,
    )
    table_real, table_imag = dft_table(inner_len)
    real_part, imag_part = complex_einsum(
        "cbk,ka->cab", real_part, imag_part, table_real, -table_imag
    )
    real_part = real_part.reshape(channel_count, length)
    imag_part = imag_part.reshape(channel_count, length)
    sample_pos = lax.iota(jnp.int32, length)
    cosine, sine_part = twiddle(sample_pos * phase_bin % total_len, total_len)
    sine_part = -sine_part
    return (real_part * cosine - imag_part * sine_part, real_part * sine_part + imag_part * cosine)


def mix_bins(spread, band, response, offsets):
    fine_len, channel_all, inner_len = (spread.shape[1], spread.shape[2], spread.shape[3])
    band_width = band.shape[1]
    half_width = band_width // 2
    shift_cols = offsets.reshape(1, fine_len, 1, inner_len)
    centered = (shift_cols + half_width) % channel_all - half_width
    moved = jnp.zeros_like(spread)
    for shift_amount in range(-half_width, half_width + 1):
        rolled = jnp.roll(spread, -shift_amount, axis=2)
        moved = jnp.where(centered == shift_amount, rolled, moved)
    moved_real = moved[0]
    moved_imag = moved[1]
    wide_real = jnp.concatenate([moved_real, moved_real[:, : band_width - 1]], axis=1)
    wide_imag = jnp.concatenate([moved_imag, moved_imag[:, : band_width - 1]], axis=1)
    responses = response.reshape(2, band_width, fine_len, 1, inner_len)
    acc_real = jnp.zeros_like(moved_real)
    acc_imag = jnp.zeros_like(moved_imag)
    for lag_index in range(band_width):
        value_real = wide_real[:, lag_index : lag_index + channel_all]
        value_imag = wide_imag[:, lag_index : lag_index + channel_all]
        gain_real = band[0, lag_index][None, :, None]
        gain_imag = band[1, lag_index][None, :, None]
        coef_real = gain_real * responses[0, lag_index] - gain_imag * responses[1, lag_index]
        coef_imag = gain_real * responses[1, lag_index] + gain_imag * responses[0, lag_index]
        acc_real = acc_real + coef_real * value_real - coef_imag * value_imag
        acc_imag = acc_imag + coef_real * value_imag + coef_imag * value_real
    return (acc_real, acc_imag)


def per_device(signal, band, response, offsets):
    blocks = lax.axis_size("tm")
    levels = blocks.bit_length() - 1
    device_pos = lax.axis_index("tm")
    phase_bin = reverse_bits(device_pos, levels)
    channel_count, length = signal.shape
    total_len = length * blocks
    inner_len = math.gcd(128, length // lax.axis_size("chan"))
    real_part = signal
    imag_part = jnp.zeros_like(signal)
    for bit_index in range(levels - 1, -1, -1):
        half_span = 1 << bit_index
        partner = from_partner(jnp.stack([real_part, imag_part]), "tm", bit_index)
        upper_half = device_pos // half_span % 2 == 1
        cosine, sine_part = twiddle(device_pos % half_span, 2 * half_span)
        diff_real = partner[0] - real_part
        diff_imag = partner[1] - imag_part
        new_real = jnp.where(
            upper_half, diff_real * cosine - diff_imag * sine_part, real_part + partner[0]
        )
        new_imag = jnp.where(
            upper_half, diff_real * sine_part + diff_imag * cosine, imag_part + partner[1]
        )
        real_part, imag_part = (new_real, new_imag)
    spec_real, spec_imag = forward_local(real_part, imag_part, phase_bin, total_len, inner_len)
    spread = lax.all_to_all(
        jnp.stack([spec_real, spec_imag]), "chan", split_axis=1, concat_axis=2, tiled=True
    )
    mixed_real, mixed_imag = mix_bins(spread, band, response, offsets)
    returned = lax.all_to_all(
        jnp.stack([mixed_real, mixed_imag]), "chan", split_axis=2, concat_axis=1, tiled=True
    )
    real_part, imag_part = inverse_local(returned[0], returned[1], phase_bin, total_len)
    for bit_index in range(levels):
        half_span = 1 << bit_index
        partner = from_partner(jnp.stack([real_part, imag_part]), "tm", bit_index)
        upper_half = device_pos // half_span % 2 == 1
        cosine, sine_part = twiddle(device_pos % half_span, 2 * half_span)
        sine_part = -sine_part
        base_real = jnp.where(upper_half, partner[0], real_part)
        base_imag = jnp.where(upper_half, partner[1], imag_part)
        scaled_real = jnp.where(upper_half, real_part, partner[0])
        scaled_imag = jnp.where(upper_half, imag_part, partner[1])
        prod_real = scaled_real * cosine - scaled_imag * sine_part
        prod_imag = scaled_real * sine_part + scaled_imag * cosine
        real_part = jnp.where(upper_half, base_real - prod_real, base_real + prod_real)
        imag_part = jnp.where(upper_half, base_imag - prod_imag, base_imag + prod_imag)
    smoothed = real_part / total_len
    return smoothed


TM, CHAN, ROWS, LANES, OUTER, BANDW, HALF = 4, 8, 8, 128, 64, 16, 8
DEVICES = TM * CHAN
TOTAL = OUTER * LANES


def split_hi_lo(value):
    hi = value.astype(jnp.bfloat16)
    return hi, (value - hi.astype(jnp.float32)).astype(jnp.bfloat16)


def product(value, table_hi, table_lo):
    hi, lo = split_hi_lo(value)
    rows = value.shape[0]
    both = jnp.dot(jnp.concatenate([hi, lo], axis=0), table_hi[...], preferred_element_type=jnp.float32)
    return both[:rows] + (both[rows:] + jnp.dot(hi, table_lo[...], preferred_element_type=jnp.float32))


def outer_table():
    n1 = np.arange(OUTER)
    table = np.zeros((OUTER, OUTER))
    for pair in range(DEVICES):
        angle = 2 * np.pi * (n1 * pair % OUTER) / OUTER
        table[2 * pair] = np.cos(angle)
        table[2 * pair + 1] = -np.sin(angle) if pair else (-1.0) ** n1
    return table


def rev(t):
    return (t % 2) * 2 + t // 2


def outer_product(table, value):
    hi, lo = split_hi_lo(value)
    return jnp.dot(table.astype(jnp.bfloat16), jnp.concatenate([hi, lo, hi], axis=0), preferred_element_type=jnp.float32)


def fused(signal, response_in, offsets_in, band_in, base_in, turn_in, table_in, out,
          response, offsets, band_rows, base, turn, table, resp, tall, band, xs, xin, ybuf, sbuf, rbuf, rt, xp, mv, mm, wh, wl, vh, vl,
          dbuf, yback, zbuf, wide, resp_wide, rsend, rrecv, send, recv, own, arrive):
    t, g = lax.axis_index("tm"), lax.axis_index("chan")
    d = CHAN // 2 * g + rev(t)
    e = TM * g + t
    line = g // 2
    lines = [(line + i) % 4 for i in range(4)]
    cores = [g - 2 * line, 1 - (g - 2 * line)]
    times = [(t + i) % TM for i in range(TM)]
    revs = [rev(i) for i in times]

    def remote(src, dst, k, target):
        return pltpu.make_async_remote_copy(
            src_ref=src, dst_ref=dst, send_sem=send.at[k], recv_sem=recv.at[k],
            device_id=target, device_id_type=pl.DeviceIdType.MESH)

    def local(src, dst, sem):
        return pltpu.make_async_copy(src, dst, sem)

    barrier = pltpu.get_barrier_semaphore()
    for hop in range(1, TM):
        pl.semaphore_signal(barrier, inc=1, device_id=((t + hop) % TM, g), device_id_type=pl.DeviceIdType.MESH)
    for hop in range(1, CHAN):
        pl.semaphore_signal(barrier, inc=1, device_id=(t, (g + hop) % CHAN), device_id_type=pl.DeviceIdType.MESH)

    @pl.when(t >= 2)
    def _():
        for hop in range(1, CHAN):
            pl.semaphore_signal(
                barrier, inc=1, device_id=(5 - t, (g + hop) % CHAN), device_id_type=pl.DeviceIdType.MESH)

    copies = [local(src, dst, own.at[i]) for i, (src, dst) in enumerate((
        (response_in, response), (offsets_in, offsets), (band_in, band_rows), (base_in, base),
        (turn_in.at[d], turn), (table_in, table)))]
    for copy in copies:
        copy.start()
    @pl.when(t < 2)
    def _():
        pl.semaphore_wait(barrier, TM + CHAN - 2)

    @pl.when(t >= 2)
    def _():
        pl.semaphore_wait(barrier, TM + 2 * CHAN - 3)

    for hop in (2, 1, 3):
        to = (t + hop) % TM
        remote(signal.at[pl.ds(ROWS * to, ROWS)], xin.at[t], 0, (to, g)).start()
    local(signal.at[pl.ds(ROWS * t, ROWS)], xin.at[t], recv.at[0]).start()

    copies[0].wait()
    copies[1].wait()
    centered = ((offsets[...] + HALF) % 256 - HALF).astype(jnp.float32)
    filler = jnp.zeros((LANES - 2 * BANDW - 8, 256), jnp.float32)
    tall[...] = jnp.concatenate([response[...], jnp.broadcast_to(centered, (8, 256)), filler], axis=0).T
    for s in range(16):
        resp[s] = tall[pl.ds(s, 16, stride=16), :]

    def send_resp(part, s, block, target):
        return pltpu.make_async_remote_copy(
            src_ref=resp.at[s], dst_ref=rbuf.at[part, pl.ds(16 * block, 16)], send_sem=rsend.at[part],
            recv_sem=rrecv.at[part], device_id=target, device_id_type=pl.DeviceIdType.MESH)

    t_b = jnp.where(t < 2, t, 5 - t)
    s_own = jnp.where(t == 0, (8 - g) % 8, 7 - g) + 8
    local(resp.at[g], rbuf.at[0, pl.ds(16 * g, 16)], rrecv.at[0]).start()
    for hop in range(1, CHAN):
        to = (g + hop) % CHAN
        send_resp(0, to, g, (t, to)).start()

    def send_b():
        for hop in range(1, CHAN):
            to = (g + hop) % CHAN
            send_resp(1, jnp.where(t == 0, (8 - to) % 8, 7 - to) + 8, g, (t_b, to)).start()

    @pl.when(t < 2)
    def _():
        send_b()
        local(resp.at[s_own], rbuf.at[1, pl.ds(16 * g, 16)], rrecv.at[1]).start()

    @pl.when(t >= 2)
    def _():
        send_b()
        pltpu.make_async_remote_copy(
            src_ref=resp.at[s_own], dst_ref=rbuf.at[1, pl.ds(16 * g, 16)], send_sem=rsend.at[2],
            recv_sem=rrecv.at[1], device_id=(5 - t, g), device_id_type=pl.DeviceIdType.MESH).start()

    copies[2].wait()
    band[...] = jnp.concatenate([band_rows[...], jnp.zeros((LANES - 2 * BANDW, 256), jnp.float32)], axis=0).T

    for copy in copies[3:]:
        copy.wait()
    first = d == 0
    for part in range(2):
        tc, ts = turn[2 * part : 2 * part + 1, :], turn[2 * part + 1 : 2 * part + 2, :]
        bc, bs = base[0], base[1]
        tr = tc * bc - ts * bs
        ti = tc * bs + ts * bc
        zero = jnp.zeros_like(tr)
        if part == 0:
            blocks = ((tr, ti), (jnp.where(first, zero, -ti), jnp.where(first, zero, tr)))
        else:
            blocks = ((jnp.where(first, zero, tr), jnp.where(first, zero, ti)),
                      (jnp.where(first, tr, ti), jnp.where(first, ti, -tr)))
        for row in range(2):
            for col in range(2):
                inner = slice(LANES * row, LANES * (row + 1))
                outer = slice(LANES * (2 * part + col), LANES * (2 * part + col + 1))
                vh[outer, inner], vl[outer, inner] = split_hi_lo(blocks[row][col])
                wh[inner, outer], wl[inner, outer] = split_hi_lo(blocks[row][col].T)

    def spread(i, carry):
        rows = pl.ds(pl.multiple_of(8 * i, 8), 8)
        gains = band[rows, :]
        for j in range(2 * BANDW):
            wide[j, rows, :] = jnp.broadcast_to(gains[:, j : j + 1], (8, LANES))
        return carry

    lax.fori_loop(0, 32, spread, 0)

    local(xin, xin, recv.at[0]).wait()

    for b in range(TM):
        for i in range(16):
            xs[pl.ds(ROWS * (16 * b + i), ROWS), :] = xin[b, :, LANES * i : LANES * (i + 1)]
    ycols = ybuf.reshape(DEVICES * 2 * ROWS, LANES)
    taken = jnp.concatenate([xs[pl.ds(c, OUTER, stride=ROWS), :] for c in range(ROWS)], axis=1)
    result = outer_product(table[0], taken)
    for c in range(ROWS):
        ycols[pl.ds(c, OUTER, stride=ROWS), :] = result[:, LANES * c : LANES * (c + 1)]

    local(ybuf.at[d], sbuf.at[e], arrive.at[line]).start()
    for back in range(4):
        for core in cores:
            to_g = 2 * lines[-back % 4] + core
            for hop in (2, 1, 3, 0):
                if back == 0 and core is cores[0] and hop == 0:
                    continue
                pltpu.make_async_remote_copy(
                    src_ref=ybuf.at[4 * to_g + revs[hop]], dst_ref=sbuf.at[e], send_sem=send.at[1],
                    recv_sem=arrive.at[line], device_id=(times[hop], to_g),
                    device_id_type=pl.DeviceIdType.MESH).start()

    for part in range(2):
        local(rbuf.at[part], rbuf.at[part], rrecv.at[part]).wait()
        rt[part] = rbuf[part].T
        for j in range(2 * BANDW + 1):
            resp_wide[part, j] = jnp.broadcast_to(rt[part, j : j + 1, :], (8, LANES))

    def ingest(i):
        q = (line + i) % 4
        eight = sbuf.at[pl.ds(8 * q, 8)]
        local(eight, eight, arrive.at[q]).wait()
        rows = jnp.concatenate([eight[:, 0].reshape(64, LANES), eight[:, 1].reshape(64, LANES)], axis=1)
        spec = product(rows, wh, wl)
        for part in range(2):
            for ri in range(2):
                at = LANES * (2 * part + ri)
                xp[part, ri, pl.ds(pl.multiple_of(64 * i, 64), 64), :] = spec[:, at : at + LANES]

    def shift(i, carry):
        at = 8 * i
        for part in range(2):
            off = resp_wide[part, 2 * BANDW]
            got = [jnp.zeros((8, LANES), jnp.float32)] * 2
            for o in range(-HALF, HALF + 1):
                hit = off == float(o)
                for ri in range(2):
                    got[ri] = jnp.where(hit, xp[part, ri, pl.ds(at + o, 8), :], got[ri])
            for ri in range(2):
                mv[part, ri, pl.ds(pl.multiple_of(at, 8), 8), :] = got[ri]
        return carry

    ingest(0)
    for part in range(2):
        for ri in range(2):
            xp[part, ri, 256:288] = xp[part, ri, 0:32]
    lax.fori_loop(1, 3, shift, 0, unroll=2)

    def chunk(step, carry):
        @pl.when(step < 3)
        def _():
            ingest(step + 1)

        lax.fori_loop(0, 8, lambda i, inner: shift(8 * step + 3 + i, inner), 0, unroll=4)

        def mix(i, inner):
            at = 64 * step + 8 + 8 * i
            gains = pl.ds(pl.multiple_of((64 * line + at) % 256, 8), 8)
            acc = [jnp.zeros((8, LANES), jnp.float32)] * 4
            for j in range(BANDW):
                br, bi = wide[j, gains, :], wide[BANDW + j, gains, :]
                for part in range(2):
                    rr, ri = resp_wide[part, j], resp_wide[part, BANDW + j]
                    cr = br * rr - bi * ri
                    ci = br * ri + bi * rr
                    xr = mv[part, 0, pl.ds(at + j, 8), :]
                    xi = mv[part, 1, pl.ds(at + j, 8), :]
                    acc[2 * part] = acc[2 * part] + (cr * xr - ci * xi)
                    acc[2 * part + 1] = acc[2 * part + 1] + (cr * xi + ci * xr)
            for q in range(4):
                mm[pl.ds(pl.multiple_of(8 * i, 8), 8), LANES * q : LANES * (q + 1)] = acc[q]
            return inner

        lax.fori_loop(0, 8, mix, 0, unroll=4)
        back = product(mm[...], vh, vl)
        for ri in range(2):
            dbuf[pl.ds(8 * step, 8), ri] = back[:, LANES * ri : LANES * (ri + 1)].reshape(8, 8, LANES)

        here, after = 2 * ((line + step) % 4), 2 * ((line + step + 1) % 4)
        for u in range(8):
            source = dbuf.at[8 * step + u]
            to_t, to_g = (1 + u) % 4, (here, here + 1, after)[(1 + u) // 4]
            own_block = (to_t == t) & (to_g == g)

            @pl.when(jnp.logical_not(own_block))
            def _():
                remote(source, yback.at[d], 2, (to_t, to_g)).start()

            @pl.when(own_block)
            def _():
                local(source, yback.at[d], recv.at[2]).start()

        return carry

    lax.fori_loop(0, 4, chunk, 0)

    local(yback, yback, recv.at[2]).wait()
    bcols = yback.reshape(DEVICES * 2 * ROWS, LANES)
    taken = jnp.concatenate([bcols[pl.ds(c, OUTER, stride=ROWS), :] for c in range(ROWS)], axis=1)
    result = outer_product(table[1], taken)
    for c in range(ROWS):
        xs[pl.ds(c, OUTER, stride=ROWS), :] = result[:, LANES * c : LANES * (c + 1)]
    for b in range(TM):
        for i in range(16):
            zbuf[b, :, LANES * i : LANES * (i + 1)] = xs[pl.ds(ROWS * (16 * b + i), ROWS), :]
    for hop in (2, 1, 3):
        to = (t + hop) % TM
        remote(zbuf.at[to], out.at[pl.ds(ROWS * t, ROWS)], 3, (to, g)).start()
    local(zbuf.at[t], out.at[pl.ds(ROWS * t, ROWS)], recv.at[3]).start()
    local(out, out, recv.at[3]).wait()

    for k in (0, 3):
        local(signal.at[pl.ds(0, 24)], signal.at[pl.ds(0, 24)], send.at[k]).wait()
    for k in (1, 2):
        local(ybuf.at[pl.ds(0, 31)], ybuf.at[pl.ds(0, 31)], send.at[k]).wait()
    for part in range(2):
        local(resp.at[pl.ds(0, 7)], resp.at[pl.ds(0, 7)], rsend.at[part]).wait()

    @pl.when(t >= 2)
    def _():
        local(resp.at[0], resp.at[0], rsend.at[2]).wait()


def per_device_fused(signal, band, response, offsets):
    n2 = np.arange(LANES)
    angle = -2 * np.pi * (n2[:, None] * n2[None, :] % LANES) / LANES
    base = jnp.asarray(np.stack([np.cos(angle), np.sin(angle)]).astype(np.float32))
    pairs = np.arange(DEVICES)[:, None]
    other = np.where(pairs == 0, DEVICES, OUTER - pairs)
    turns = [-2 * np.pi * (n2[None, :] * k1 % TOTAL) / TOTAL for k1 in (pairs, other)]
    rows = [np.cos(turns[0]), np.sin(turns[0]), np.cos(turns[1]), np.sin(turns[1])]
    turn = jnp.asarray(np.stack(rows * 2, axis=1).astype(np.float32))
    forward = outer_table()
    tables = []
    for matrix in (forward, forward.T / TOTAL):
        matrix = matrix.astype(np.float32)
        hi = matrix.astype(jnp.bfloat16)
        lo = (matrix - hi.astype(np.float32)).astype(jnp.bfloat16)
        tables.append(np.concatenate([hi, hi, lo], axis=1).astype(np.float32))
    table = jnp.asarray(np.stack(tables))

    f32 = jnp.float32
    hbm = pl.BlockSpec(memory_space=pl.ANY)
    out = pl.pallas_call(
        fused,
        out_shape=jax.ShapeDtypeStruct((32, 16 * LANES), f32),
        in_specs=[hbm] * 7,
        out_specs=hbm,
        scratch_shapes=[
            pltpu.VMEM((2 * BANDW, 256), f32),
            pltpu.VMEM((1, 256), jnp.int32),
            pltpu.VMEM((2 * BANDW, 256), f32),
            pltpu.VMEM((2, LANES, LANES), f32),
            pltpu.VMEM((8, LANES), f32),
            pltpu.VMEM((2, OUTER, 3 * OUTER), f32),
            pltpu.VMEM((16, 16, LANES), f32),
            pltpu.VMEM((2 * LANES, LANES), f32),
            pltpu.VMEM((2 * LANES, LANES), f32),
            pltpu.VMEM((OUTER * ROWS, LANES), f32),
            pltpu.VMEM((TM, ROWS, 16 * LANES), f32),
            pltpu.VMEM((DEVICES, 2, ROWS, LANES), f32),
            pltpu.VMEM((DEVICES, 2, ROWS, LANES), f32),
            pltpu.VMEM((2, LANES, LANES), f32),
            pltpu.VMEM((2, LANES, LANES), f32),
            pltpu.VMEM((2, 2, 288, LANES), f32),
            pltpu.VMEM((2, 2, 280, LANES), f32),
            pltpu.VMEM((64, 4 * LANES), f32),
            pltpu.VMEM((2 * LANES, 4 * LANES), jnp.bfloat16),
            pltpu.VMEM((2 * LANES, 4 * LANES), jnp.bfloat16),
            pltpu.VMEM((4 * LANES, 2 * LANES), jnp.bfloat16),
            pltpu.VMEM((4 * LANES, 2 * LANES), jnp.bfloat16),
            pltpu.VMEM((DEVICES, 2, ROWS, LANES), f32),
            pltpu.VMEM((DEVICES, 2, ROWS, LANES), f32),
            pltpu.VMEM((TM, ROWS, 16 * LANES), f32),
            pltpu.VMEM((2 * BANDW, 256, LANES), f32),
            pltpu.VMEM((2, 2 * BANDW + 1, 8, LANES), f32),
            pltpu.SemaphoreType.DMA((3,)),
            pltpu.SemaphoreType.DMA((2,)),
            pltpu.SemaphoreType.DMA((4,)),
            pltpu.SemaphoreType.DMA((4,)),
            pltpu.SemaphoreType.DMA((6,)),
            pltpu.SemaphoreType.DMA((4,)),
        ],
        compiler_params=pltpu.CompilerParams(collective_id=0, has_side_effects=True, vmem_limit_bytes=40 << 20),
    )(*(pltpu.with_memory_space_constraint(x, pltpu.HBM) for x in (
        signal, response.reshape(2 * BANDW, 256), offsets, band.reshape(2 * BANDW, 256), base, turn, table)))
    return out


def solution(mesh):
    sizes = dict(mesh.shape)
    tuned = sizes["tm"] == TM and sizes["chan"] == CHAN
    in_specs = (P("chan", "tm"), P(), P(None, "tm", None, "chan"), P("tm", "chan"))
    out_specs = P("chan", "tm")
    return jax.shard_map(
        per_device_fused if tuned else per_device, mesh=mesh, in_specs=in_specs, out_specs=out_specs, check_vma=False
    )
```

```python
import math

import jax
import jax.numpy as jnp
import numpy as np
from jax import lax
from jax.experimental import pallas as pl
from jax.experimental.pallas import tpu as pltpu
from jax.sharding import PartitionSpec as P

PRECISE = lax.Precision.HIGHEST


def from_partner(block, axis, stride):
    count = lax.axis_size(axis)
    route = []
    for low in range(count):
        high = low | 1 << stride
        if high != low and high < count:
            route += [(low, high), (high, low)]
    return lax.ppermute(block, axis, route)


def twiddle(numer, length):
    angle = -2.0 * math.pi / length * numer.astype(jnp.float32)
    return (jnp.cos(angle), jnp.sin(angle))


def dft_table(length):
    steps = lax.iota(jnp.int32, length)
    return twiddle(steps[:, None] * steps[None, :] % length, length)


def reverse_bits(value, bit_count):
    result = value * 0
    for bit_index in range(bit_count):
        result = result + value // (1 << bit_index) % 2 * (1 << bit_count - 1 - bit_index)
    return result


def complex_einsum(form, left_real, left_imag, right_real, right_imag):
    out_real = jnp.einsum(form, left_real, right_real, precision=PRECISE) - jnp.einsum(
        form, left_imag, right_imag, precision=PRECISE
    )
    out_imag = jnp.einsum(form, left_real, right_imag, precision=PRECISE) + jnp.einsum(
        form, left_imag, right_real, precision=PRECISE
    )
    return (out_real, out_imag)


def forward_local(real_part, imag_part, phase_bin, total_len, inner_len):
    channel_count, length = real_part.shape
    outer_len = length // inner_len
    sample_pos = lax.iota(jnp.int32, length)
    cosine, sine_part = twiddle(sample_pos * phase_bin % total_len, total_len)
    real_part, imag_part = (
        real_part * cosine - imag_part * sine_part,
        real_part * sine_part + imag_part * cosine,
    )
    real_part = real_part.reshape(channel_count, inner_len, outer_len)
    imag_part = imag_part.reshape(channel_count, inner_len, outer_len)
    table_real, table_imag = dft_table(inner_len)
    real_part, imag_part = complex_einsum(
        "cab,ak->cbk", real_part, imag_part, table_real, table_imag
    )
    outer_ids = lax.iota(jnp.int32, outer_len)[:, None]
    inner_ids = lax.iota(jnp.int32, inner_len)[None, :]
    cosine, sine_part = twiddle(outer_ids * inner_ids, length)
    real_part, imag_part = (
        real_part * cosine - imag_part * sine_part,
        real_part * sine_part + imag_part * cosine,
    )
    table_real, table_imag = dft_table(outer_len)
    return complex_einsum("cbk,bm->mck", real_part, imag_part, table_real, table_imag)


def inverse_local(spec_real, spec_imag, phase_bin, total_len):
    outer_len, channel_count, inner_len = spec_real.shape
    length = outer_len * inner_len
    table_real, table_imag = dft_table(outer_len)
    real_part, imag_part = complex_einsum(
        "mck,mb->cbk", spec_real, spec_imag, table_real, -table_imag
    )
    outer_ids = lax.iota(jnp.int32, outer_len)[:, None]
    inner_ids = lax.iota(jnp.int32, inner_len)[None, :]
    cosine, sine_part = twiddle(outer_ids * inner_ids, length)
    sine_part = -sine_part
    real_part, imag_part = (
        real_part * cosine - imag_part * sine_part,
        real_part * sine_part + imag_part * cosine,
    )
    table_real, table_imag = dft_table(inner_len)
    real_part, imag_part = complex_einsum(
        "cbk,ka->cab", real_part, imag_part, table_real, -table_imag
    )
    real_part = real_part.reshape(channel_count, length)
    imag_part = imag_part.reshape(channel_count, length)
    sample_pos = lax.iota(jnp.int32, length)
    cosine, sine_part = twiddle(sample_pos * phase_bin % total_len, total_len)
    sine_part = -sine_part
    return (real_part * cosine - imag_part * sine_part, real_part * sine_part + imag_part * cosine)


def mix_bins(spread, band, response, offsets):
    fine_len, channel_all, inner_len = (spread.shape[1], spread.shape[2], spread.shape[3])
    band_width = band.shape[1]
    half_width = band_width // 2
    shift_cols = offsets.reshape(1, fine_len, 1, inner_len)
    centered = (shift_cols + half_width) % channel_all - half_width
    moved = jnp.zeros_like(spread)
    for shift_amount in range(-half_width, half_width + 1):
        rolled = jnp.roll(spread, -shift_amount, axis=2)
        moved = jnp.where(centered == shift_amount, rolled, moved)
    moved_real = moved[0]
    moved_imag = moved[1]
    wide_real = jnp.concatenate([moved_real, moved_real[:, : band_width - 1]], axis=1)
    wide_imag = jnp.concatenate([moved_imag, moved_imag[:, : band_width - 1]], axis=1)
    responses = response.reshape(2, band_width, fine_len, 1, inner_len)
    acc_real = jnp.zeros_like(moved_real)
    acc_imag = jnp.zeros_like(moved_imag)
    for lag_index in range(band_width):
        value_real = wide_real[:, lag_index : lag_index + channel_all]
        value_imag = wide_imag[:, lag_index : lag_index + channel_all]
        gain_real = band[0, lag_index][None, :, None]
        gain_imag = band[1, lag_index][None, :, None]
        coef_real = gain_real * responses[0, lag_index] - gain_imag * responses[1, lag_index]
        coef_imag = gain_real * responses[1, lag_index] + gain_imag * responses[0, lag_index]
        acc_real = acc_real + coef_real * value_real - coef_imag * value_imag
        acc_imag = acc_imag + coef_real * value_imag + coef_imag * value_real
    return (acc_real, acc_imag)


def per_device(signal, band, response, offsets):
    blocks = lax.axis_size("tm")
    levels = blocks.bit_length() - 1
    device_pos = lax.axis_index("tm")
    phase_bin = reverse_bits(device_pos, levels)
    channel_count, length = signal.shape
    total_len = length * blocks
    inner_len = math.gcd(128, length // lax.axis_size("chan"))
    real_part = signal
    imag_part = jnp.zeros_like(signal)
    for bit_index in range(levels - 1, -1, -1):
        half_span = 1 << bit_index
        partner = from_partner(jnp.stack([real_part, imag_part]), "tm", bit_index)
        upper_half = device_pos // half_span % 2 == 1
        cosine, sine_part = twiddle(device_pos % half_span, 2 * half_span)
        diff_real = partner[0] - real_part
        diff_imag = partner[1] - imag_part
        new_real = jnp.where(
            upper_half, diff_real * cosine - diff_imag * sine_part, real_part + partner[0]
        )
        new_imag = jnp.where(
            upper_half, diff_real * sine_part + diff_imag * cosine, imag_part + partner[1]
        )
        real_part, imag_part = (new_real, new_imag)
    spec_real, spec_imag = forward_local(real_part, imag_part, phase_bin, total_len, inner_len)
    spread = lax.all_to_all(
        jnp.stack([spec_real, spec_imag]), "chan", split_axis=1, concat_axis=2, tiled=True
    )
    mixed_real, mixed_imag = mix_bins(spread, band, response, offsets)
    returned = lax.all_to_all(
        jnp.stack([mixed_real, mixed_imag]), "chan", split_axis=2, concat_axis=1, tiled=True
    )
    real_part, imag_part = inverse_local(returned[0], returned[1], phase_bin, total_len)
    for bit_index in range(levels):
        half_span = 1 << bit_index
        partner = from_partner(jnp.stack([real_part, imag_part]), "tm", bit_index)
        upper_half = device_pos // half_span % 2 == 1
        cosine, sine_part = twiddle(device_pos % half_span, 2 * half_span)
        sine_part = -sine_part
        base_real = jnp.where(upper_half, partner[0], real_part)
        base_imag = jnp.where(upper_half, partner[1], imag_part)
        scaled_real = jnp.where(upper_half, real_part, partner[0])
        scaled_imag = jnp.where(upper_half, imag_part, partner[1])
        prod_real = scaled_real * cosine - scaled_imag * sine_part
        prod_imag = scaled_real * sine_part + scaled_imag * cosine
        real_part = jnp.where(upper_half, base_real - prod_real, base_real + prod_real)
        imag_part = jnp.where(upper_half, base_imag - prod_imag, base_imag + prod_imag)
    smoothed = real_part / total_len
    return smoothed


TM, CHAN, ROWS, LANES, OUTER, BANDW, HALF = 4, 8, 8, 128, 64, 16, 8
DEVICES = TM * CHAN
TOTAL = OUTER * LANES


def split_hi_lo(value):
    hi = value.astype(jnp.bfloat16)
    return hi, (value - hi.astype(jnp.float32)).astype(jnp.bfloat16)


def product(value, table_hi, table_lo):
    hi, lo = split_hi_lo(value)
    rows = value.shape[0]
    both = jnp.dot(jnp.concatenate([hi, lo], axis=0), table_hi[...], preferred_element_type=jnp.float32)
    return both[:rows] + (both[rows:] + jnp.dot(hi, table_lo[...], preferred_element_type=jnp.float32))


def outer_table():
    n1 = np.arange(OUTER)
    table = np.zeros((OUTER, OUTER))
    for pair in range(DEVICES):
        angle = 2 * np.pi * (n1 * pair % OUTER) / OUTER
        table[2 * pair] = np.cos(angle)
        table[2 * pair + 1] = -np.sin(angle) if pair else (-1.0) ** n1
    return table


def rev(t):
    return (t % 2) * 2 + t // 2


def outer_product(table, value):
    hi, lo = split_hi_lo(value)
    return jnp.dot(table.astype(jnp.bfloat16), jnp.concatenate([hi, lo, hi], axis=0), preferred_element_type=jnp.float32)


def fused(signal, response_in, offsets_in, band_in, base_in, turn_in, table_in, out,
          response, offsets, band_rows, base, turn, table, resp, tall, band, xs, xin, ybuf, sbuf, rbuf, rt, xp, mv, mm, wh, wl, vh, vl,
          dbuf, yback, zbuf, resp_wide, rsend, rrecv, send, recv, own, arrive):
    t, g = lax.axis_index("tm"), lax.axis_index("chan")
    d = CHAN // 2 * g + rev(t)
    e = TM * g + t
    line = g // 2
    lines = [(line + i) % 4 for i in range(4)]
    cores = [g - 2 * line, 1 - (g - 2 * line)]
    times = [(t + i) % TM for i in range(TM)]
    revs = [rev(i) for i in times]

    def remote(src, dst, k, target):
        return pltpu.make_async_remote_copy(
            src_ref=src, dst_ref=dst, send_sem=send.at[k], recv_sem=recv.at[k],
            device_id=target, device_id_type=pl.DeviceIdType.MESH)

    def local(src, dst, sem):
        return pltpu.make_async_copy(src, dst, sem)

    barrier = pltpu.get_barrier_semaphore()
    for hop in range(1, TM):
        pl.semaphore_signal(barrier, inc=1, device_id=((t + hop) % TM, g), device_id_type=pl.DeviceIdType.MESH)
    for hop in range(1, CHAN):
        pl.semaphore_signal(barrier, inc=1, device_id=(t, (g + hop) % CHAN), device_id_type=pl.DeviceIdType.MESH)
    copies = [local(src, dst, own.at[i]) for i, (src, dst) in enumerate((
        (response_in, response), (offsets_in, offsets), (band_in, band_rows), (base_in, base),
        (turn_in.at[d], turn), (table_in, table)))]
    for copy in copies:
        copy.start()
    pl.semaphore_wait(barrier, TM + CHAN - 2)

    for hop in (2, 1, 3):
        to = (t + hop) % TM
        remote(signal.at[pl.ds(ROWS * to, ROWS)], xin.at[t], 0, (to, g)).start()
    local(signal.at[pl.ds(ROWS * t, ROWS)], xin.at[t], recv.at[0]).start()

    copies[0].wait()
    copies[1].wait()
    centered = ((offsets[...] + HALF) % 256 - HALF).astype(jnp.float32)
    filler = jnp.zeros((LANES - 2 * BANDW - 8, 256), jnp.float32)
    tall[...] = jnp.concatenate([response[...], jnp.broadcast_to(centered, (8, 256)), filler], axis=0).T
    for s in range(16):
        resp[s] = tall[pl.ds(s, 16, stride=16), :]

    def send_resp(part, s, block, target):
        return pltpu.make_async_remote_copy(
            src_ref=resp.at[s], dst_ref=rbuf.at[part, pl.ds(16 * block, 16)], send_sem=rsend.at[part],
            recv_sem=rrecv.at[part], device_id=target, device_id_type=pl.DeviceIdType.MESH)

    t_b = jnp.where(t < 2, t, 5 - t)
    s_own = jnp.where(t == 0, (8 - g) % 8, 7 - g) + 8
    local(resp.at[g], rbuf.at[0, pl.ds(16 * g, 16)], rrecv.at[0]).start()
    for hop in range(1, CHAN):
        to = (g + hop) % CHAN
        send_resp(0, to, g, (t, to)).start()

    def send_b():
        for hop in range(1, CHAN):
            to = (g + hop) % CHAN
            send_resp(1, jnp.where(t == 0, (8 - to) % 8, 7 - to) + 8, g, (t_b, to)).start()

    @pl.when(t < 2)
    def _():
        send_b()
        local(resp.at[s_own], rbuf.at[1, pl.ds(16 * g, 16)], rrecv.at[1]).start()

    copies[2].wait()
    band[...] = jnp.concatenate([band_rows[...], jnp.zeros((LANES - 2 * BANDW, 256), jnp.float32)], axis=0).T

    for copy in copies[3:]:
        copy.wait()
    first = d == 0
    for part in range(2):
        tc, ts = turn[2 * part : 2 * part + 1, :], turn[2 * part + 1 : 2 * part + 2, :]
        bc, bs = base[0], base[1]
        tr = tc * bc - ts * bs
        ti = tc * bs + ts * bc
        zero = jnp.zeros_like(tr)
        if part == 0:
            blocks = ((tr, ti), (jnp.where(first, zero, -ti), jnp.where(first, zero, tr)))
        else:
            blocks = ((jnp.where(first, zero, tr), jnp.where(first, zero, ti)),
                      (jnp.where(first, tr, ti), jnp.where(first, ti, -tr)))
        for row in range(2):
            for col in range(2):
                inner = slice(LANES * row, LANES * (row + 1))
                outer = slice(LANES * (2 * part + col), LANES * (2 * part + col + 1))
                vh[outer, inner], vl[outer, inner] = split_hi_lo(blocks[row][col])
                wh[inner, outer], wl[inner, outer] = split_hi_lo(blocks[row][col].T)

    local(xin, xin, recv.at[0]).wait()

    @pl.when(t >= 2)
    def _():
        send_b()
        pltpu.make_async_remote_copy(
            src_ref=resp.at[s_own], dst_ref=rbuf.at[1, pl.ds(16 * g, 16)], send_sem=rsend.at[2],
            recv_sem=rrecv.at[1], device_id=(5 - t, g), device_id_type=pl.DeviceIdType.MESH).start()

    for b in range(TM):
        for i in range(16):
            xs[pl.ds(ROWS * (16 * b + i), ROWS), :] = xin[b, :, LANES * i : LANES * (i + 1)]
    ycols = ybuf.reshape(DEVICES * 2 * ROWS, LANES)
    taken = jnp.concatenate([xs[pl.ds(c, OUTER, stride=ROWS), :] for c in range(ROWS)], axis=1)
    result = outer_product(table[0], taken)
    for c in range(ROWS):
        ycols[pl.ds(c, OUTER, stride=ROWS), :] = result[:, LANES * c : LANES * (c + 1)]

    local(ybuf.at[d], sbuf.at[e], arrive.at[line]).start()
    for back in range(4):
        for core in cores:
            to_g = 2 * lines[-back % 4] + core
            for hop in (2, 1, 3, 0):
                if back == 0 and core is cores[0] and hop == 0:
                    continue
                pltpu.make_async_remote_copy(
                    src_ref=ybuf.at[4 * to_g + revs[hop]], dst_ref=sbuf.at[e], send_sem=send.at[1],
                    recv_sem=arrive.at[line], device_id=(times[hop], to_g),
                    device_id_type=pl.DeviceIdType.MESH).start()

    for part in range(2):
        local(rbuf.at[part], rbuf.at[part], rrecv.at[part]).wait()
        rt[part] = rbuf[part].T
        for j in range(2 * BANDW + 1):
            resp_wide[part, j] = jnp.broadcast_to(rt[part, j : j + 1, :], (8, LANES))

    def ingest(i):
        q = (line + i) % 4
        eight = sbuf.at[pl.ds(8 * q, 8)]
        local(eight, eight, arrive.at[q]).wait()
        rows = jnp.concatenate([eight[:, 0].reshape(64, LANES), eight[:, 1].reshape(64, LANES)], axis=1)
        spec = product(rows, wh, wl)
        for part in range(2):
            for ri in range(2):
                at = LANES * (2 * part + ri)
                xp[part, ri, pl.ds(pl.multiple_of(64 * i, 64), 64), :] = spec[:, at : at + LANES]

    def shift(i, carry):
        at = 8 * i
        for part in range(2):
            off = resp_wide[part, 2 * BANDW]
            got = [jnp.zeros((8, LANES), jnp.float32)] * 2
            for o in range(-HALF, HALF + 1):
                hit = off == float(o)
                for ri in range(2):
                    got[ri] = jnp.where(hit, xp[part, ri, pl.ds(at + o, 8), :], got[ri])
            for ri in range(2):
                mv[part, ri, pl.ds(pl.multiple_of(at, 8), 8), :] = got[ri]
        return carry

    ingest(0)
    for part in range(2):
        for ri in range(2):
            xp[part, ri, 256:288] = xp[part, ri, 0:32]
    lax.fori_loop(1, 3, shift, 0, unroll=2)

    def chunk(step, carry):
        @pl.when(step < 3)
        def _():
            ingest(step + 1)

        lax.fori_loop(0, 8, lambda i, inner: shift(8 * step + 3 + i, inner), 0, unroll=4)

        def mix(i, inner):
            at = 64 * step + 8 + 8 * i
            gains = band[pl.ds(pl.multiple_of((64 * line + at) % 256, 8), 8), :]
            acc = [jnp.zeros((8, LANES), jnp.float32)] * 4
            for j in range(BANDW):
                br = jnp.broadcast_to(gains[:, j : j + 1], (8, LANES))
                bi = jnp.broadcast_to(gains[:, BANDW + j : BANDW + j + 1], (8, LANES))
                for part in range(2):
                    rr, ri = resp_wide[part, j], resp_wide[part, BANDW + j]
                    cr = br * rr - bi * ri
                    ci = br * ri + bi * rr
                    xr = mv[part, 0, pl.ds(at + j, 8), :]
                    xi = mv[part, 1, pl.ds(at + j, 8), :]
                    acc[2 * part] = acc[2 * part] + (cr * xr - ci * xi)
                    acc[2 * part + 1] = acc[2 * part + 1] + (cr * xi + ci * xr)
            for q in range(4):
                mm[pl.ds(pl.multiple_of(8 * i, 8), 8), LANES * q : LANES * (q + 1)] = acc[q]
            return inner

        lax.fori_loop(0, 8, mix, 0, unroll=4)
        back = product(mm[...], vh, vl)
        for ri in range(2):
            dbuf[pl.ds(8 * step, 8), ri] = back[:, LANES * ri : LANES * (ri + 1)].reshape(8, 8, LANES)

        here, after = 2 * ((line + step) % 4), 2 * ((line + step + 1) % 4)
        for u in range(8):
            source = dbuf.at[8 * step + u]
            to_t, to_g = (1 + u) % 4, (here, here + 1, after)[(1 + u) // 4]
            own_block = (to_t == t) & (to_g == g)

            @pl.when(jnp.logical_not(own_block))
            def _():
                remote(source, yback.at[d], 2, (to_t, to_g)).start()

            @pl.when(own_block)
            def _():
                local(source, yback.at[d], recv.at[2]).start()

        return carry

    lax.fori_loop(0, 4, chunk, 0)

    local(yback, yback, recv.at[2]).wait()
    bcols = yback.reshape(DEVICES * 2 * ROWS, LANES)
    taken = jnp.concatenate([bcols[pl.ds(c, OUTER, stride=ROWS), :] for c in range(ROWS)], axis=1)
    result = outer_product(table[1], taken)
    for c in range(ROWS):
        xs[pl.ds(c, OUTER, stride=ROWS), :] = result[:, LANES * c : LANES * (c + 1)]
    for b in range(TM):
        for i in range(16):
            zbuf[b, :, LANES * i : LANES * (i + 1)] = xs[pl.ds(ROWS * (16 * b + i), ROWS), :]
    for hop in (2, 1, 3):
        to = (t + hop) % TM
        remote(zbuf.at[to], out.at[pl.ds(ROWS * t, ROWS)], 3, (to, g)).start()
    local(zbuf.at[t], out.at[pl.ds(ROWS * t, ROWS)], recv.at[3]).start()
    local(out, out, recv.at[3]).wait()

    for k in (0, 3):
        local(signal.at[pl.ds(0, 24)], signal.at[pl.ds(0, 24)], send.at[k]).wait()
    for k in (1, 2):
        local(ybuf.at[pl.ds(0, 31)], ybuf.at[pl.ds(0, 31)], send.at[k]).wait()
    for part in range(2):
        local(resp.at[pl.ds(0, 7)], resp.at[pl.ds(0, 7)], rsend.at[part]).wait()

    @pl.when(t >= 2)
    def _():
        local(resp.at[0], resp.at[0], rsend.at[2]).wait()


def per_device_fused(signal, band, response, offsets):
    n2 = np.arange(LANES)
    angle = -2 * np.pi * (n2[:, None] * n2[None, :] % LANES) / LANES
    base = jnp.asarray(np.stack([np.cos(angle), np.sin(angle)]).astype(np.float32))
    pairs = np.arange(DEVICES)[:, None]
    other = np.where(pairs == 0, DEVICES, OUTER - pairs)
    turns = [-2 * np.pi * (n2[None, :] * k1 % TOTAL) / TOTAL for k1 in (pairs, other)]
    rows = [np.cos(turns[0]), np.sin(turns[0]), np.cos(turns[1]), np.sin(turns[1])]
    turn = jnp.asarray(np.stack(rows * 2, axis=1).astype(np.float32))
    forward = outer_table()
    tables = []
    for matrix in (forward, forward.T / TOTAL):
        matrix = matrix.astype(np.float32)
        hi = matrix.astype(jnp.bfloat16)
        lo = (matrix - hi.astype(np.float32)).astype(jnp.bfloat16)
        tables.append(np.concatenate([hi, hi, lo], axis=1).astype(np.float32))
    table = jnp.asarray(np.stack(tables))

    f32 = jnp.float32
    hbm = pl.BlockSpec(memory_space=pl.ANY)
    out = pl.pallas_call(
        fused,
        out_shape=jax.ShapeDtypeStruct((32, 16 * LANES), f32),
        in_specs=[hbm] * 7,
        out_specs=hbm,
        scratch_shapes=[
            pltpu.VMEM((2 * BANDW, 256), f32),
            pltpu.VMEM((1, 256), jnp.int32),
            pltpu.VMEM((2 * BANDW, 256), f32),
            pltpu.VMEM((2, LANES, LANES), f32),
            pltpu.VMEM((8, LANES), f32),
            pltpu.VMEM((2, OUTER, 3 * OUTER), f32),
            pltpu.VMEM((16, 16, LANES), f32),
            pltpu.VMEM((2 * LANES, LANES), f32),
            pltpu.VMEM((2 * LANES, LANES), f32),
            pltpu.VMEM((OUTER * ROWS, LANES), f32),
            pltpu.VMEM((TM, ROWS, 16 * LANES), f32),
            pltpu.VMEM((DEVICES, 2, ROWS, LANES), f32),
            pltpu.VMEM((DEVICES, 2, ROWS, LANES), f32),
            pltpu.VMEM((2, LANES, LANES), f32),
            pltpu.VMEM((2, LANES, LANES), f32),
            pltpu.VMEM((2, 2, 288, LANES), f32),
            pltpu.VMEM((2, 2, 280, LANES), f32),
            pltpu.VMEM((64, 4 * LANES), f32),
            pltpu.VMEM((2 * LANES, 4 * LANES), jnp.bfloat16),
            pltpu.VMEM((2 * LANES, 4 * LANES), jnp.bfloat16),
            pltpu.VMEM((4 * LANES, 2 * LANES), jnp.bfloat16),
            pltpu.VMEM((4 * LANES, 2 * LANES), jnp.bfloat16),
            pltpu.VMEM((DEVICES, 2, ROWS, LANES), f32),
            pltpu.VMEM((DEVICES, 2, ROWS, LANES), f32),
            pltpu.VMEM((TM, ROWS, 16 * LANES), f32),
            pltpu.VMEM((2, 2 * BANDW + 1, 8, LANES), f32),
            pltpu.SemaphoreType.DMA((3,)),
            pltpu.SemaphoreType.DMA((2,)),
            pltpu.SemaphoreType.DMA((4,)),
            pltpu.SemaphoreType.DMA((4,)),
            pltpu.SemaphoreType.DMA((6,)),
            pltpu.SemaphoreType.DMA((4,)),
        ],
        compiler_params=pltpu.CompilerParams(collective_id=0, has_side_effects=True, vmem_limit_bytes=40 << 20),
    )(*(pltpu.with_memory_space_constraint(x, pltpu.HBM) for x in (
        signal, response.reshape(2 * BANDW, 256), offsets, band.reshape(2 * BANDW, 256), base, turn, table)))
    return out


def solution(mesh):
    sizes = dict(mesh.shape)
    tuned = sizes["tm"] == TM and sizes["chan"] == CHAN
    in_specs = (P("chan", "tm"), P(), P(None, "tm", None, "chan"), P("tm", "chan"))
    out_specs = P("chan", "tm")
    return jax.shard_map(
        per_device_fused if tuned else per_device, mesh=mesh, in_specs=in_specs, out_specs=out_specs, check_vma=False
    )
```
